32 devices in a mesh: elem: 8 (over z, y), orb: 4 (over x, core).
Axes of the slice: x: 2, y: 2, z: 4, core: 2. Of those that a mesh axis runs over, the one named last changes fastest.
Arguments:
- orbitals: bfloat16 [6144, 4096], P('elem', 'orb')
- hamiltonian: bfloat16 [96, 7, 64, 64], P('elem'), may hold values from -0.25 to 0.25
- neighbours: int32 [96, 7], P('elem'), may hold values from 0 to 95, as said below
Outputs:
- updated: bfloat16 [6144, 4096], P('elem', 'orb')
The draws below stay inside these ranges and needn't reach their ends.
Inputs may be any that keep to these rules, and one draw needn't show every extreme that they name: Elements form tiles of 12 consecutive indices, each tile a periodic 3 x 4 plane of elements in some order, tiles stacked periodically. An element's row lists itself, its two neighbours along each in-plane direction, then the element at the same place in the previous tile and in the next tile.
All inputs are finite; a program needn't handle non-finite values.
Results may differ from the reference program's by a relative error of at most 0.0062.
Values may be sent and summed in bfloat16 or wider, within the bound.
No kernel may reach another device: no remote copies, remote signals or barrier semaphores. Data moves between devices by JAX's collectives and lax.ppermute only.
A program may use at most 64 MiB of HBM per device.

```python
import jax
import jax.numpy as jnp
from jax import lax

B = 64
NORB = 4096
GX = 3
GY = 4
EL = 12
ELEMS = 96
ROWS = 6144


def draw_orbitals(key, part):
    key_base = jax.random.fold_in(key, 0)
    key_row = jax.random.fold_in(key, 1)
    key_col = jax.random.fold_in(key, 2)
    key_tile = jax.random.fold_in(key, 4)
    low = jnp.log(0.3)
    high = jnp.log(3.0)
    col_scale = jnp.exp(jax.random.uniform(key_col, (NORB,), jnp.float32, low, high))
    ramp = jnp.exp(jnp.log(3.0) * jnp.arange(ROWS, dtype=jnp.float32) / ROWS)
    tiles = ELEMS // EL
    tile_scale = jnp.exp(jax.random.uniform(key_tile, (tiles,), jnp.float32, 0.0, jnp.log(40.0)))
    tile_rows = jnp.repeat(tile_scale, EL * B, total_repeat_length=ROWS)
    row_scale = jnp.exp(jax.random.uniform(key_row, (ROWS,), jnp.float32, low, high)) * ramp * tile_rows
    base = jax.random.normal(key_base, (ROWS, NORB), jnp.float32)
    base = jnp.clip(base, -5.0, 5.0)
    values = base * row_scale[:, None] * col_scale[None, :]
    return values.astype(jnp.bfloat16)


def draw_neighbours(key, part):
    tiles = ELEMS // EL
    keys = jax.random.split(key, tiles)
    order = jax.vmap(lambda single: jax.random.permutation(single, EL))(keys).astype(jnp.int32)
    cells = jnp.arange(EL, dtype=jnp.int32)
    xpos = cells // GY
    ypos = cells % GY
    tile_ids = jnp.arange(tiles, dtype=jnp.int32)

    def element_at(tile, cell):
        return tile * EL + order[tile, cell]
    own_tile = tile_ids[:, None] + jnp.zeros((1, EL), jnp.int32)
    own_cell = cells[None, :] + jnp.zeros((tiles, 1), jnp.int32)
    xminus = ((xpos - 1) % GX * GY + ypos)[None, :] + jnp.zeros((tiles, 1), jnp.int32)
    xplus = ((xpos + 1) % GX * GY + ypos)[None, :] + jnp.zeros((tiles, 1), jnp.int32)
    yminus = (xpos * GY + (ypos - 1) % GY)[None, :] + jnp.zeros((tiles, 1), jnp.int32)
    yplus = (xpos * GY + (ypos + 1) % GY)[None, :] + jnp.zeros((tiles, 1), jnp.int32)
    below = (own_tile - 1) % tiles
    above = (own_tile + 1) % tiles
    lists = jnp.stack([element_at(own_tile, own_cell), element_at(own_tile, xminus), element_at(own_tile, xplus), element_at(own_tile, yminus), element_at(own_tile, yplus), element_at(below, own_cell), element_at(above, own_cell)], axis=-1).reshape(ELEMS, 7)
    row_ids = element_at(own_tile, own_cell).reshape(ELEMS)
    return jnp.zeros((ELEMS, 7), jnp.int32).at[row_ids].set(lists)


def level_of(own_key, extent, pieces, low, high):
    def one(position, shards_of):
        heights = jax.random.uniform(jax.random.fold_in(jax.random.fold_in(own_key, 6), position), (shards_of,), jnp.float32, low / len(pieces), high / len(pieces))
        return jnp.repeat(jnp.exp(heights), extent[position] // shards_of).reshape((-1,) + (1,) * (len(extent) - position - 1))

    loudness = one(*pieces[0])
    for cut in pieces[1:]:
        loudness = loudness * one(*cut)
    return loudness


def bell_draw(rng, shape, scale, most, cuts=(), kind=jnp.bfloat16):
    level = level_of(rng, shape, cuts, -0.22, 0.18) if cuts else 1.0
    values = jax.random.normal(rng, shape, jnp.float32) * scale * level
    return jnp.minimum(jnp.maximum(values, -most), most).astype(kind)


def setup_inputs(seed: int = 0) -> dict:
    key_list = jax.random.split(jax.random.key(seed), 4)
    return {
        "orbitals": draw_orbitals(jax.random.fold_in(key_list[3], 71), 0),
        "hamiltonian": bell_draw(key_list[1], (ELEMS, 7, B, B), (7 * B) ** -0.5, 0.25, ((0, 8),)),
        "neighbours": draw_neighbours(jax.random.fold_in(key_list[3], 71), 0),
    }


def neighbour_product(hamiltonian, neighbours, field):
    width = field.shape[1]
    blocks = field.reshape(ELEMS, B, width)
    picked = blocks[neighbours].astype(jnp.float32)
    result = jnp.einsum('enab,enbc->eac', hamiltonian.astype(jnp.float32), picked)
    return result.reshape(ROWS, width)

def reference(orbitals, hamiltonian, neighbours):
    width = 256 if NORB % 256 == 0 else NORB
    count = NORB // width
    stacked = orbitals.reshape(ROWS, count, width).transpose(1, 0, 2)

    def filter_block(block):
        start = block.astype(jnp.float32)
        first = neighbour_product(hamiltonian, neighbours, block)
        first_half = first.astype(jnp.bfloat16)
        second = 2.0 * neighbour_product(hamiltonian, neighbours, first_half) - start
        second_half = second.astype(jnp.bfloat16)
        third = 2.0 * neighbour_product(hamiltonian, neighbours, second_half) - first
        return third.astype(jnp.bfloat16)
    filtered = lax.map(filter_block, stacked).transpose(1, 0, 2).reshape(ROWS, NORB)
    gram = jnp.dot(filtered.T, filtered, preferred_element_type=jnp.float32)
    level = jnp.trace(gram) / (NORB * ROWS)
    scaled = (gram / (level * ROWS)).astype(jnp.bfloat16)
    mixed = jnp.dot(filtered, scaled, preferred_element_type=jnp.float32)
    result = (1.5 * filtered.astype(jnp.float32) - 0.5 * mixed) / jnp.sqrt(level)
    return result.astype(jnp.bfloat16)
```

```python
import functools

import jax
import jax.numpy as jnp
from jax import lax
from jax.experimental import pallas as pl
from jax.experimental.pallas import tpu as pltpu
from jax.sharding import PartitionSpec as P

CHUNKS = 4
F32 = jnp.float32
BF16 = jnp.bfloat16


def dense_operator(blocks, place):
    elements, slots, size, _ = blocks.shape
    hot = place[:, :, None] == jnp.arange(elements, dtype=place.dtype)
    full = jnp.zeros((elements, size, elements, size), blocks.dtype)
    for slot in range(slots):
        mask = hot[:, slot][:, None, :, None]
        full = jnp.where(mask, blocks[:, slot][:, :, None, :], full)
    return full.reshape(elements * size, elements * size)


def product_kernel(stage, own_ref, near_ref, far_ref, field_ref, by_near_ref, by_far_ref, *refs):
    def accumulate(operator_ref, value_ref):
        return jnp.dot(operator_ref[...], value_ref[...], preferred_element_type=F32)

    total = accumulate(own_ref, field_ref) + accumulate(near_ref, by_near_ref) + accumulate(far_ref, by_far_ref)
    if stage == 0:
        wide_ref, half_ref = refs
        wide_ref[...] = total
        half_ref[...] = total.astype(BF16)
    elif stage == 1:
        before_ref, half_ref = refs
        half_ref[...] = (2.0 * total - before_ref[...].astype(F32)).astype(BF16)
    else:
        before_ref, half_ref, squares_ref = refs
        value = (2.0 * total - before_ref[...]).astype(BF16)
        half_ref[...] = value
        wide = value.astype(F32)
        squares_ref[...] = jnp.sum((wide * wide).reshape(-1, 8, wide.shape[1]), axis=0)


def product(stage, operators, field, by_near, by_far, before=None):
    rows, width = field.shape
    half = jax.ShapeDtypeStruct((rows, width), BF16)
    wide = jax.ShapeDtypeStruct((rows, width), F32)
    squares = jax.ShapeDtypeStruct((8, width), F32)
    outs = ((wide, half), half, (half, squares))[stage]
    args = (*operators, field, by_near, by_far) + (() if before is None else (before,))
    return pl.pallas_call(
        functools.partial(product_kernel, stage),
        out_shape=outs,
        in_specs=[pl.BlockSpec(memory_space=pltpu.VMEM)] * len(args),
        compiler_params=pltpu.CompilerParams(vmem_limit_bytes=32 * 1024 * 1024),
        cost_estimate=pl.CostEstimate(
            flops=6 * rows * rows * width, bytes_accessed=6 * rows * rows + 16 * rows * width, transcendentals=0
        ),
        name=f"product_{stage}",
    )(*args)


def local(orbitals, hamiltonian, neighbours):
    elements = hamiltonian.shape[0]
    rows, columns = orbitals.shape
    tiles = lax.axis_size("elem")
    groups = lax.axis_size("orb")
    lines = tiles // 2
    odd = lax.axis_index("elem") % 2

    swap = [(i, i ^ 1) for i in range(tiles)]
    forward = []
    for line in range(lines):
        forward.append((2 * line, 2 * ((line + 1) % lines)))
        forward.append((2 * line + 1, 2 * ((line - 1) % lines) + 1))

    place = neighbours % elements
    own = dense_operator(hamiltonian[:, :5], place[:, :5])
    previous, following = (dense_operator(hamiltonian[:, s : s + 1], place[:, s : s + 1]) for s in (5, 6))
    near = jnp.where(odd == 0, following, previous)
    far = jnp.where(odd == 0, previous, following)
    operators = (own, near, far)

    width = columns // CHUNKS
    start = [lax.slice_in_dim(orbitals, c * width, (c + 1) * width, axis=1) for c in range(CHUNKS)]

    def step(stage, fields, before):
        out = []
        for field, old in zip(fields, before):
            by_near = lax.ppermute(field, "elem", swap)
            by_far = lax.ppermute(by_near, "elem", forward)
            out.append(product(stage, operators, field, by_near, by_far, old))
        return out

    firsts = step(0, start, [None] * CHUNKS)
    seconds = step(1, [half for _, half in firsts], start)
    thirds = step(2, seconds, [wide for wide, _ in firsts])

    own_squares = sum(jnp.sum(squares) for _, squares in thirds)
    total = jnp.sum(lax.all_gather(jnp.full((8, 128), own_squares, F32), ("elem", "orb"))[:, 0, 0])

    pieces = []
    for value, _ in thirds:
        have = {0: value}
        bit = groups // 2
        while bit:
            peers = [(i, i ^ bit) for i in range(groups)]
            for known in list(have):
                have[known | bit] = lax.ppermute(have[known], "orb", peers)
            bit //= 2
        pieces.append(have)
    panel = jnp.concatenate([pieces[c][d] for d in range(groups) for c in range(CHUNKS)], axis=1)
    filtered = panel[:, :columns]

    rows_total = rows * tiles
    orbital_count = columns * groups
    level = total / (orbital_count * rows_total)
    partial_gram = lax.dot_general(panel, filtered, (((0,), (0,)), ((), ())), preferred_element_type=F32).astype(BF16)
    gram_part = lax.psum_scatter(partial_gram, "elem", scatter_dimension=0, tiled=True)
    scaled_part = (gram_part.astype(F32) / (level * rows_total)).astype(BF16)
    scaled = lax.all_gather(scaled_part, "elem", axis=0, tiled=True)
    mixed = jnp.dot(panel, scaled, preferred_element_type=F32)
    result = (1.5 * filtered.astype(F32) - 0.5 * mixed) / jnp.sqrt(level)
    return result.astype(BF16)


def solution(mesh):
    return jax.shard_map(
        local,
        mesh=mesh,
        in_specs=(P("elem", "orb"), P("elem", None, None, None), P("elem", None)),
        out_specs=P("elem", "orb"),
        check_vma=False,
    )
```

```python
import functools

import jax
import jax.numpy as jnp
from jax import lax
from jax.experimental import pallas as pl
from jax.experimental.pallas import tpu as pltpu
from jax.sharding import PartitionSpec as P

CHUNKS = 4
F32 = jnp.float32
BF16 = jnp.bfloat16


def product_kernel(stage, place_ref, blocks_ref, field_ref, near_ref, far_ref, *refs):
    elements, size, _ = blocks_ref.shape
    width = field_ref.shape[1]
    squares = jnp.zeros((8, width), F32)
    filler = jnp.zeros((size, width), BF16)
    for element in range(elements):
        picked = []
        for slot in range(7):
            source = field_ref if slot < 5 else near_ref if slot == 5 else far_ref
            first_row = pl.multiple_of(place_ref[element, slot] * size, size)
            picked.append(source[pl.ds(first_row, size), :])
        stacked = jnp.concatenate(picked + [filler], axis=0)
        total = jnp.dot(blocks_ref[element], stacked, preferred_element_type=F32)
        here = pl.ds(element * size, size)
        if stage == 0:
            wide_ref, half_ref = refs
            wide_ref[here, :] = total
            half_ref[here, :] = total.astype(BF16)
        elif stage == 1:
            before_ref, half_ref = refs
            half_ref[here, :] = (2.0 * total - before_ref[here, :].astype(F32)).astype(BF16)
        else:
            before_ref, half_ref, squares_ref = refs
            value = (2.0 * total - before_ref[here, :]).astype(BF16)
            half_ref[here, :] = value
            wide = value.astype(F32)
            squares += jnp.sum((wide * wide).reshape(-1, 8, width), axis=0)
    if stage == 2:
        squares_ref[...] = squares


def product(stage, place, blocks, field, by_near, by_far, before=None):
    rows, width = field.shape
    half = jax.ShapeDtypeStruct((rows, width), BF16)
    wide = jax.ShapeDtypeStruct((rows, width), F32)
    squares = jax.ShapeDtypeStruct((8, width), F32)
    outs = ((wide, half), half, (half, squares))[stage]
    args = (blocks, field, by_near, by_far) + (() if before is None else (before,))
    return pl.pallas_call(
        functools.partial(product_kernel, stage),
        out_shape=outs,
        in_specs=[pl.BlockSpec(memory_space=pltpu.SMEM)] + [pl.BlockSpec(memory_space=pltpu.VMEM)] * len(args),
        compiler_params=pltpu.CompilerParams(vmem_limit_bytes=32 * 1024 * 1024),
        cost_estimate=pl.CostEstimate(
            flops=2 * blocks.size * width, bytes_accessed=2 * blocks.size + 16 * rows * width, transcendentals=0
        ),
        name=f"product_{stage}",
    )(place, *args)


def local(orbitals, hamiltonian, neighbours):
    elements, slots, size, _ = hamiltonian.shape
    rows, columns = orbitals.shape
    tiles = lax.axis_size("elem")
    groups = lax.axis_size("orb")
    lines = tiles // 2
    my_tile = lax.axis_index("elem")
    my_group = lax.axis_index("orb")
    odd = my_tile % 2
    line = my_tile // 2

    swap = [(i, i ^ 1) for i in range(tiles)]
    around = [(2 * i + side, 2 * ((i + 1) % lines) + side) for i in range(lines) for side in (0, 1)]
    outward = [(2 * i + side, 2 * ((i + 1 - 2 * side) % lines) + side) for i in range(lines) for side in (0, 1)]

    place = neighbours % elements
    last_two = place[:, 5:]
    place = jnp.concatenate([place[:, :5], jnp.where(odd == 0, last_two[:, ::-1], last_two)], axis=1)
    by_slot = [hamiltonian[:, s] for s in range(5)]
    by_slot.append(jnp.where(odd == 0, hamiltonian[:, 6], hamiltonian[:, 5]))
    by_slot.append(jnp.where(odd == 0, hamiltonian[:, 5], hamiltonian[:, 6]))
    by_slot.append(jnp.zeros_like(by_slot[0]))
    blocks = jnp.concatenate(by_slot, axis=2)

    width = columns // CHUNKS
    start = [lax.slice_in_dim(orbitals, c * width, (c + 1) * width, axis=1) for c in range(CHUNKS)]

    def step(stage, fields, before):
        out = []
        for field, old in zip(fields, before):
            by_near = lax.ppermute(field, "elem", swap)
            by_far = lax.ppermute(by_near, "elem", outward)
            out.append(product(stage, place, blocks, field, by_near, by_far, old))
        return out

    firsts = step(0, start, [None] * CHUNKS)
    seconds = step(1, [half for _, half in firsts], start)
    thirds = step(2, seconds, [wide for wide, _ in firsts])

    pieces = []
    for value, _ in thirds:
        have = {0: value}
        bit = groups // 2
        while bit:
            peers = [(i, i ^ bit) for i in range(groups)]
            for known in list(have):
                have[known | bit] = lax.ppermute(have[known], "orb", peers)
            bit //= 2
        pieces.append(have)
    panel = [jnp.concatenate([have[d] for have in pieces], axis=1) for d in range(groups)]
    filtered = panel[0]

    total = sum(squares for _, squares in thirds)
    total = jnp.full((8, 128), jnp.sum(total), F32)
    for axis, peers in (("orb", groups), ("elem", tiles)):
        bit = 1
        while bit < peers:
            total = total + lax.ppermute(total, axis, [(i, i ^ bit) for i in range(peers)])
            bit *= 2
    rows_total = rows * tiles
    level = total[0, 0] / (columns * groups * rows_total)
    divisor = level * rows_total

    def gram_of(left, right):
        return lax.dot_general(left, right, (((0,), (0,)), ((), ())), preferred_element_type=F32).astype(BF16)

    def summed_and_scaled(value):
        height = value.shape[0] // tiles
        value = value.reshape(2, lines, height, value.shape[1])
        other = lax.ppermute(lax.dynamic_index_in_dim(value, 1 - odd, 0, keepdims=False), "elem", swap)
        mine = lax.dynamic_index_in_dim(value, odd, 0, keepdims=False)

        def pair(index):
            return sum(lax.dynamic_index_in_dim(v, index, 0, keepdims=False).astype(F32) for v in (mine, other))

        running = None
        for hop in range(1, lines):
            part = pair((line - hop) % lines)
            if running is not None:
                part = part + running.astype(F32)
            running = lax.ppermute(part.astype(BF16), "elem", around)
        part = pair(line)
        if running is not None:
            part = part + running.astype(F32)
        part = (part / divisor).astype(BF16)
        whole = lax.dynamic_update_index_in_dim(jnp.zeros_like(mine), part, line, 0)
        for hop in range(1, lines):
            part = lax.ppermute(part, "elem", around)
            whole = lax.dynamic_update_index_in_dim(whole, part, (line - hop) % lines, 0)
        far_whole = lax.ppermute(whole, "elem", swap)
        halves = [jnp.where(odd == 0, whole, far_whole), jnp.where(odd == 0, far_whole, whole)]
        return jnp.concatenate(halves, axis=0).reshape(tiles * height, -1)

    mixed = jnp.dot(filtered, summed_and_scaled(gram_of(filtered, filtered)), preferred_element_type=F32)
    middle = columns // 2
    order = sorted(range(1, groups), key=lambda d: (d == 1, d))
    for d in order:
        top_bit = 1 << (d.bit_length() - 1)
        lower = (my_group & top_bit) == 0
        left = jnp.where(lower, panel[d][:, :middle], filtered[:, middle:])
        right = jnp.where(lower, filtered, panel[d])
        half = summed_and_scaled(gram_of(left, right))
        peer_half = lax.ppermute(half, "orb", [(i, i ^ d) for i in range(groups)])
        block = jnp.concatenate(
            [jnp.where(lower, half, peer_half), jnp.where(lower, peer_half, half)], axis=0
        )
        block = jnp.where(lower, block, block.T)
        mixed = mixed + jnp.dot(panel[d], block, preferred_element_type=F32)
    result = (1.5 * filtered.astype(F32) - 0.5 * mixed) / jnp.sqrt(level)
    return result.astype(BF16)


def solution(mesh):
    return jax.shard_map(
        local,
        mesh=mesh,
        in_specs=(P("elem", "orb"), P("elem", None, None, None), P("elem", None)),
        out_specs=P("elem", "orb"),
        check_vma=False,
    )
```

```python
import functools

import jax
import jax.numpy as jnp
from jax import lax
from jax.experimental import pallas as pl
from jax.experimental.pallas import tpu as pltpu
from jax.sharding import PartitionSpec as P

CHUNKS = 4
F32 = jnp.float32
BF16 = jnp.bfloat16
VMEM_LIMIT = 48 * 1024 * 1024


class Order:
    def __init__(self, token):
        self.token = token

    def __call__(self, *values):
        *values, self.token = lax.optimization_barrier((*values, self.token))
        return values[0] if len(values) == 1 else tuple(values)


def product_kernel(stage, place_ref, blocks_ref, field_ref, near_ref, far_ref, *refs):
    elements, size, _ = blocks_ref.shape
    width = field_ref.shape[1]
    squares = jnp.zeros((8, width), F32)
    filler = jnp.zeros((size, width), BF16)
    for element in range(elements):
        picked = []
        for slot in range(7):
            source = field_ref if slot < 5 else near_ref if slot == 5 else far_ref
            first_row = pl.multiple_of(place_ref[element, slot] * size, size)
            picked.append(source[pl.ds(first_row, size), :])
        stacked = jnp.concatenate(picked + [filler], axis=0)
        total = jnp.dot(blocks_ref[element], stacked, preferred_element_type=F32)
        here = pl.ds(element * size, size)
        if stage == 0:
            wide_ref, half_ref = refs
            wide_ref[here, :] = total
            half_ref[here, :] = total.astype(BF16)
        elif stage == 1:
            before_ref, half_ref = refs
            half_ref[here, :] = (2.0 * total - before_ref[here, :].astype(F32)).astype(BF16)
        else:
            before_ref, half_ref, squares_ref = refs
            value = (2.0 * total - before_ref[here, :]).astype(BF16)
            half_ref[here, :] = value
            wide = value.astype(F32)
            squares += jnp.sum((wide * wide).reshape(-1, 8, width), axis=0)
    if stage == 2:
        squares_ref[...] = squares


def call(kernel, name, outs, scalars, args, scratch=(), aliases=None):
    return pl.pallas_call(
        kernel,
        out_shape=outs,
        in_specs=[pl.BlockSpec(memory_space=pltpu.SMEM)] * len(scalars)
        + [pl.BlockSpec(memory_space=pltpu.VMEM)] * len(args),
        scratch_shapes=list(scratch),
        input_output_aliases=aliases or {},
        compiler_params=pltpu.CompilerParams(vmem_limit_bytes=VMEM_LIMIT),
        cost_estimate=pl.CostEstimate(flops=1024, bytes_accessed=1024, transcendentals=0),
        name=name,
    )(*scalars, *args)


def product(stage, place, blocks, field, by_near, by_far, before=None):
    rows, width = field.shape
    half = jax.ShapeDtypeStruct((rows, width), BF16)
    wide = jax.ShapeDtypeStruct((rows, width), F32)
    squares = jax.ShapeDtypeStruct((8, width), F32)
    outs = ((wide, half), half, (half, squares))[stage]
    args = (blocks, field, by_near, by_far) + (() if before is None else (before,))
    kernel = functools.partial(product_kernel, stage)
    return call(kernel, f"product_{stage}", outs, (place,), args)


def put_in_place(where_ref, lines, mine_ref, far_ref, out_ref, base):
    odd, line = where_ref[0], where_ref[1]
    half = mine_ref.shape[0]
    height = half // lines
    for side, ref in ((odd, mine_ref), (1 - odd, far_ref)):
        for j in range(lines):
            number = lax.rem(line - j + lines, lines)
            first_row = pl.multiple_of(base + side * half + number * height, height)
            out_ref[pl.ds(first_row, height), :] = ref[j * height : (j + 1) * height, :]


TRANSPOSED_LEFT = (((0,), (0,)), ((), ()))
TRANSPOSED_RIGHT = (((1,), (1,)), ((), ()))


def side_by_side(refs):
    return jnp.concatenate([ref[...] for ref in refs], axis=1)


def gram_kernel(pair, where_ref, *refs):
    mine_ref, other_ref, whole = refs[-3:]
    fields = refs[:CHUNKS]
    half = whole.shape[0] // 2
    width = fields[0].shape[1]
    middle = CHUNKS * width // 2
    odd = where_ref[0]

    def fill(left, rights, count):
        for c, right in enumerate(rights):
            value = lax.dot_general(left, right[...], TRANSPOSED_LEFT, preferred_element_type=F32)
            whole[:count, c * width : (c + 1) * width] = value.astype(BF16)

    if pair:
        peers = refs[CHUNKS : 2 * CHUNKS]
        used = middle

        @pl.when(where_ref[2] == 0)
        def _():
            fill(side_by_side(peers[: CHUNKS // 2]), fields, middle)

        @pl.when(where_ref[2] == 1)
        def _():
            fill(side_by_side(fields[CHUNKS // 2 :]), peers, middle)
    else:
        used = middle + middle // 2
        upper = side_by_side(fields[CHUNKS // 2 :])
        fill(side_by_side(fields[: CHUNKS // 2]), fields, middle)
        corner = lax.dot_general(upper, upper, TRANSPOSED_LEFT, preferred_element_type=F32).astype(BF16)
        whole[middle:used, :middle] = corner[: middle // 2]
        whole[middle:used, middle:] = corner[middle // 2 :]
    if used < whole.shape[0]:
        whole[used:, :] = jnp.zeros((whole.shape[0] - used, whole.shape[1]), BF16)
    mine_ref[...] = whole[pl.ds(pl.multiple_of(odd * half, half), half), :]
    other_ref[...] = whole[pl.ds(pl.multiple_of((1 - odd) * half, half), half), :]


def own_kernel(lines, where_ref, *refs):
    fields = refs[:CHUNKS]
    mine_ref, far_ref, out_ref, block = refs[CHUNKS:]
    put_in_place(where_ref, lines, mine_ref, far_ref, block, 0)
    middle = CHUNKS * fields[0].shape[1] // 2
    lower, upper = side_by_side(fields[: CHUNKS // 2]), side_by_side(fields[CHUNKS // 2 :])
    corner = jnp.concatenate(
        [block[middle : middle + middle // 2, :middle], block[middle : middle + middle // 2, middle:]], axis=0
    )
    out_ref[:, :middle] = jnp.dot(lower, block[:middle, :middle], preferred_element_type=F32) + lax.dot_general(
        upper, block[:middle, middle:], TRANSPOSED_RIGHT, preferred_element_type=F32
    )
    out_ref[:, middle:] = jnp.dot(lower, block[:middle, middle:], preferred_element_type=F32) + jnp.dot(
        upper, corner, preferred_element_type=F32
    )


def pair_kernel(lines, last, where_ref, *refs):
    if last:
        level_ref, *refs = refs
        own = refs[CHUNKS + 5 : 2 * CHUNKS + 5]
    out_ref, block = refs[-2:]
    total_ref = refs[0]
    fields = refs[1 : CHUNKS + 1]
    mine_ref, far_ref, peer_mine_ref, peer_far_ref = refs[CHUNKS + 1 : CHUNKS + 5]
    height = block.shape[0] // 2
    width = fields[0].shape[1]
    used = CHUNKS * width // 2
    is_upper = where_ref[2]
    put_in_place(where_ref, lines, mine_ref, far_ref, block, is_upper * height)
    put_in_place(where_ref, lines, peer_mine_ref, peer_far_ref, block, (1 - is_upper) * height)

    def finish(mixed, c):
        here = slice(c * width, (c + 1) * width)
        value = total_ref[:, here] + mixed
        if last:
            value = (1.5 * own[c][...].astype(F32) - 0.5 * value) / jnp.sqrt(level_ref[0])
        out_ref[:, here] = value.astype(out_ref.dtype)

    def rows_of_block(c):
        first_row = c * width if c * width < used else height + c * width - used
        return block[first_row : first_row + width, :]

    @pl.when(is_upper == 0)
    def _():
        field = side_by_side(fields)
        for c in range(CHUNKS):
            here = slice(c * width, (c + 1) * width)
            right = jnp.concatenate([block[:used, here], block[height : height + used, here]], axis=0)
            finish(jnp.dot(field, right, preferred_element_type=F32), c)

    @pl.when(is_upper == 1)
    def _():
        field = side_by_side(fields)
        for c in range(CHUNKS):
            finish(lax.dot_general(field, rows_of_block(c), TRANSPOSED_RIGHT, preferred_element_type=F32), c)


def local(orbitals, hamiltonian, neighbours):
    elements, slots, size, _ = hamiltonian.shape
    rows, columns = orbitals.shape
    tiles = lax.axis_size("elem")
    groups = lax.axis_size("orb")
    lines = tiles // 2
    my_tile = lax.axis_index("elem")
    my_group = lax.axis_index("orb")
    odd = my_tile % 2
    line = my_tile // 2

    swap = [(i, i ^ 1) for i in range(tiles)]
    around = [(2 * i + side, 2 * ((i + 1) % lines) + side) for i in range(lines) for side in (0, 1)]
    outward = [(2 * i + side, 2 * ((i + 1 - 2 * side) % lines) + side) for i in range(lines) for side in (0, 1)]

    def to_group(value, d):
        return lax.ppermute(value, "orb", [(i, i ^ d) for i in range(groups)])

    place = neighbours % elements
    last_two = place[:, 5:]
    place = jnp.concatenate([place[:, :5], jnp.where(odd == 0, last_two[:, ::-1], last_two)], axis=1)
    by_slot = [hamiltonian[:, s] for s in range(5)]
    by_slot.append(jnp.where(odd == 0, hamiltonian[:, 6], hamiltonian[:, 5]))
    by_slot.append(jnp.where(odd == 0, hamiltonian[:, 5], hamiltonian[:, 6]))
    by_slot.append(jnp.zeros_like(by_slot[0]))
    blocks = jnp.concatenate(by_slot, axis=2)

    width = columns // CHUNKS
    fields = [lax.slice_in_dim(orbitals, c * width, (c + 1) * width, axis=1) for c in range(CHUNKS)]
    start = fields
    near = [lax.ppermute(field, "elem", swap) for field in fields]
    order = Order(jnp.zeros((8, 128), F32) + place[0, 0].astype(F32))
    blocks, place = order(blocks, place)

    jobs = [(stage, c) for stage in range(3) for c in range(CHUNKS)]
    far = {}
    firsts, squares, pieces = {}, [], [{} for _ in range(CHUNKS)]
    near = {(0, c): near[c] for c in range(CHUNKS)}
    current = {(0, c): fields[c] for c in range(CHUNKS)}

    def send_on(job):
        near[job] = order(near[job])
        far[job] = lax.ppermute(near[job], "elem", outward)

    def more_panel(c):
        for d in range(1, groups):
            if d & (d - 1):
                low = d & -d
                if d ^ low in pieces[c] and d not in pieces[c]:
                    pieces[c][d ^ low] = order(pieces[c][d ^ low])
                    pieces[c][d] = to_group(pieces[c][d ^ low], low)

    def multiply(job):
        stage, c = job
        far[job] = order(far[job])
        old = (None, start[c], firsts.get(c))[stage]
        out = product(stage, place, blocks, current[job], near[job], far[job], old)
        if stage == 0:
            firsts[c], out = order(*out)
        elif stage == 1:
            out = order(out)
        else:
            out, square = order(*out)
            squares.append(square)
            pieces[c][0] = out
            bit = groups // 2
            while bit:
                pieces[c][bit] = to_group(out, bit)
                bit //= 2
            if c:
                more_panel(c - 1)
            return
        current[(stage + 1, c)] = out
        near[(stage + 1, c)] = lax.ppermute(out, "elem", swap)

    for index, job in enumerate(jobs):
        send_on(job)
        if index:
            multiply(jobs[index - 1])
    multiply(jobs[-1])

    squares = sum(squares)
    if width % 128:
        squares = jnp.pad(squares, ((0, 0), (0, -width % 128)))
    squares = sum(squares[:, i : i + 128] for i in range(0, squares.shape[1], 128))
    gathered = lax.all_gather(squares, ("elem", "orb"))
    rows_total = rows * tiles
    level = None
    middle = columns // 2
    unit = 16 * tiles

    def is_upper(d):
        return (my_group & (1 << (d.bit_length() - 1))) != 0

    def where(d):
        return jnp.stack([odd, line, is_upper(d) if d else odd]).astype(jnp.int32)

    def all_chunks(d):
        return [pieces[c][d] for c in range(CHUNKS)]

    def gram_chunk(d):
        height = middle if d else middle + middle // 2
        height += -height % unit
        fields = all_chunks(0)
        if d:
            more_panel(CHUNKS - 1)
            fields += order(*all_chunks(d))
        half = jax.ShapeDtypeStruct((height // 2, columns), BF16)
        scratch = (pltpu.VMEM((height, columns), BF16),)
        name = "gram_pair" if d else "gram_own"
        return call(functools.partial(gram_kernel, d > 0), name, (half, half), (where(d),), fields, scratch)

    exchanged = {}

    def process(d):
        nonlocal level
        mine, other = order(*gram_chunk(d))
        other = lax.ppermute(other, "elem", swap)
        yield
        other = order(other)
        height = mine.shape[0] // lines

        def pair(index):
            return sum(lax.dynamic_slice_in_dim(v, index * height, height, 0).astype(F32) for v in (mine, other))

        running = None
        for hop in range(1, lines):
            part = pair((line - hop) % lines)
            if running is not None:
                part = part + running.astype(F32)
            running = lax.ppermute(part.astype(BF16), "elem", around)
            yield
            running = order(running)
        part = pair(line)
        if running is not None:
            part = part + running.astype(F32)
        if level is None:
            level = jnp.sum(order(gathered)) / (columns * groups * rows_total)
        part = (part / (level * rows_total)).astype(BF16)
        parts = [part]
        for hop in range(1, lines):
            part = lax.ppermute(part, "elem", around)
            yield
            part = order(part)
            parts.append(part)
        whole = jnp.concatenate(parts, axis=0)
        far_whole = lax.ppermute(whole, "elem", swap)
        if d:
            peer_whole = to_group(whole, d)
        yield
        far_whole = order(far_whole)
        if d == 0:
            exchanged[0] = (whole, far_whole)
            return
        peer_far = to_group(far_whole, d)
        yield
        peer_whole = order(peer_whole)
        peer_far = order(peer_far)
        exchanged[d] = (whole, far_whole, peer_whole, peer_far)

    queue = sorted(range(1, groups), key=lambda d: (d == 1, d))
    events = []
    for position, d in enumerate([0] + queue):
        ready = 0.0 if position == 0 else 10.0 + 0.1 * position
        times = [ready]
        reduced = 19.0 + 10.5 * position
        times += [reduced + 6.0 * hop for hop in range(2 * lines - 1)]
        times.append(max(times[-1] + 10.0, 77.0 + 10.5 * position))
        if d:
            times.append(times[-1] + 11.0 if d > 1 else times[-1] + 3.0)
        events += [(time, position, d) for time in times]
    events.sort()
    running = {d: process(d) for d in [0] + queue}
    left_over = {d: sum(1 for event in events if event[2] == d) for d in running}
    done = []
    mixed = None
    for _, _, d in events:
        next(running[d], None)
        left_over[d] -= 1
        if left_over[d]:
            continue
        done.append(d)
        parts = exchanged[d]
        last = len(done) == groups
        shape = jax.ShapeDtypeStruct((rows, columns), BF16 if last else F32)
        scratch = (pltpu.VMEM((len(parts) * parts[0].shape[0], columns), BF16),)
        if d == 0:
            args = (*all_chunks(0), *parts)
            mixed = order(call(functools.partial(own_kernel, lines), "mix_own", shape, (where(0),), args, scratch))
            continue
        args = (mixed, *all_chunks(d), *parts)
        scalars = (where(d),)
        if last:
            scalars += (level.reshape(1),)
            args += tuple(all_chunks(0))
        kernel = functools.partial(pair_kernel, lines, last)
        mixed = call(kernel, "mix_last" if last else "mix_pair", shape, scalars, args, scratch, {} if last else {1: 0})
        if not last:
            mixed = order(mixed)
    return mixed


def solution(mesh):
    return jax.shard_map(
        local,
        mesh=mesh,
        in_specs=(P("elem", "orb"), P("elem", None, None, None), P("elem", None)),
        out_specs=P("elem", "orb"),
        check_vma=False,
    )
```

```python
import functools

import jax
import jax.numpy as jnp
from jax import lax
from jax.experimental import pallas as pl
from jax.experimental.pallas import tpu as pltpu
from jax.sharding import PartitionSpec as P

CHUNKS = 4
F32 = jnp.float32
BF16 = jnp.bfloat16
VMEM_LIMIT = 48 * 1024 * 1024


class Order:
    def __init__(self, token):
        self.token = token

    def __call__(self, *values):
        *values, self.token = lax.optimization_barrier((*values, self.token))
        return values[0] if len(values) == 1 else tuple(values)


def product_kernel(stage, place_ref, blocks_ref, field_ref, near_ref, far_ref, *refs):
    elements, size, _ = blocks_ref.shape
    width = field_ref.shape[1]
    squares = jnp.zeros((8, width), F32)
    filler = jnp.zeros((size, width), BF16)
    for element in range(elements):
        picked = []
        for slot in range(7):
            source = field_ref if slot < 5 else near_ref if slot == 5 else far_ref
            first_row = pl.multiple_of(place_ref[element, slot] * size, size)
            picked.append(source[pl.ds(first_row, size), :])
        stacked = jnp.concatenate(picked + [filler], axis=0)
        total = jnp.dot(blocks_ref[element], stacked, preferred_element_type=F32)
        here = pl.ds(element * size, size)
        if stage == 0:
            wide_ref, half_ref = refs
            wide_ref[here, :] = total
            half_ref[here, :] = total.astype(BF16)
        elif stage == 1:
            before_ref, half_ref = refs
            half_ref[here, :] = (2.0 * total - before_ref[here, :].astype(F32)).astype(BF16)
        else:
            before_ref, half_ref, squares_ref = refs
            value = (2.0 * total - before_ref[here, :]).astype(BF16)
            half_ref[here, :] = value
            wide = value.astype(F32)
            squares += jnp.sum((wide * wide).reshape(-1, 8, width), axis=0)
    if stage == 2:
        squares_ref[...] = squares


def call(kernel, name, outs, scalars, args, scratch=(), aliases=None):
    return pl.pallas_call(
        kernel,
        out_shape=outs,
        in_specs=[pl.BlockSpec(memory_space=pltpu.SMEM)] * len(scalars)
        + [pl.BlockSpec(memory_space=pltpu.VMEM)] * len(args),
        scratch_shapes=list(scratch),
        input_output_aliases=aliases or {},
        compiler_params=pltpu.CompilerParams(vmem_limit_bytes=VMEM_LIMIT),
        cost_estimate=pl.CostEstimate(flops=1024, bytes_accessed=1024, transcendentals=0),
        name=name,
    )(*scalars, *args)


def product(stage, place, blocks, field, by_near, by_far, before=None):
    rows, width = field.shape
    half = jax.ShapeDtypeStruct((rows, width), BF16)
    wide = jax.ShapeDtypeStruct((rows, width), F32)
    squares = jax.ShapeDtypeStruct((8, width), F32)
    outs = ((wide, half), half, (half, squares))[stage]
    args = (blocks, field, by_near, by_far) + (() if before is None else (before,))
    kernel = functools.partial(product_kernel, stage)
    return call(kernel, f"product_{stage}", outs, (place,), args)


def number_of(line, position, lines):
    number, bit, weight = 0, 1, lines // 2
    while bit < lines:
        number = number + lax.rem(line // bit + (position // weight) % 2, 2) * weight
        bit, weight = bit * 2, weight // 2
    return number


def put_in_place(where_ref, lines, mine_ref, far_ref, out_ref, base):
    odd, line = where_ref[0], where_ref[1]
    half = mine_ref.shape[0]
    height = half // lines
    for side, ref in ((odd, mine_ref), (1 - odd, far_ref)):
        for j in range(lines):
            first_row = base + side * half + number_of(line, j, lines) * height
            out_ref[pl.ds(pl.multiple_of(first_row, height), height), :] = ref[j * height : (j + 1) * height, :]


TRANSPOSED_LEFT = (((0,), (0,)), ((), ()))
TRANSPOSED_RIGHT = (((1,), (1,)), ((), ()))


def side_by_side(refs):
    return jnp.concatenate([ref[...] for ref in refs], axis=1)


def gram_kernel(pair, where_ref, *refs):
    mine_ref, other_ref, whole = refs[-3:]
    fields = refs[:CHUNKS]
    half = whole.shape[0] // 2
    width = fields[0].shape[1]
    middle = CHUNKS * width // 2
    odd = where_ref[0]

    def fill(left, rights, count):
        for c, right in enumerate(rights):
            value = lax.dot_general(left, right[...], TRANSPOSED_LEFT, preferred_element_type=F32)
            whole[:count, c * width : (c + 1) * width] = value.astype(BF16)

    if pair:
        peers = refs[CHUNKS : 2 * CHUNKS]
        used = middle

        @pl.when(where_ref[2] == 0)
        def _():
            fill(side_by_side(peers[: CHUNKS // 2]), fields, middle)

        @pl.when(where_ref[2] == 1)
        def _():
            fill(side_by_side(fields[CHUNKS // 2 :]), peers, middle)
    else:
        used = middle + middle // 2
        upper = side_by_side(fields[CHUNKS // 2 :])
        fill(side_by_side(fields[: CHUNKS // 2]), fields, middle)
        corner = lax.dot_general(upper, upper, TRANSPOSED_LEFT, preferred_element_type=F32).astype(BF16)
        whole[middle:used, :middle] = corner[: middle // 2]
        whole[middle:used, middle:] = corner[middle // 2 :]
    if used < whole.shape[0]:
        whole[used:, :] = jnp.zeros((whole.shape[0] - used, whole.shape[1]), BF16)
    mine_ref[...] = whole[pl.ds(pl.multiple_of(odd * half, half), half), :]
    other_ref[...] = whole[pl.ds(pl.multiple_of((1 - odd) * half, half), half), :]


def own_kernel(lines, where_ref, *refs):
    fields = refs[:CHUNKS]
    mine_ref, far_ref, out_ref, block = refs[CHUNKS:]
    put_in_place(where_ref, lines, mine_ref, far_ref, block, 0)
    middle = CHUNKS * fields[0].shape[1] // 2
    lower, upper = side_by_side(fields[: CHUNKS // 2]), side_by_side(fields[CHUNKS // 2 :])
    corner = jnp.concatenate(
        [block[middle : middle + middle // 2, :middle], block[middle : middle + middle // 2, middle:]], axis=0
    )
    out_ref[:, :middle] = jnp.dot(lower, block[:middle, :middle], preferred_element_type=F32) + lax.dot_general(
        upper, block[:middle, middle:], TRANSPOSED_RIGHT, preferred_element_type=F32
    )
    out_ref[:, middle:] = jnp.dot(lower, block[:middle, middle:], preferred_element_type=F32) + jnp.dot(
        upper, corner, preferred_element_type=F32
    )


def pair_kernel(lines, last, where_ref, *refs):
    if last:
        level_ref, *refs = refs
        own = refs[CHUNKS + 5 : 2 * CHUNKS + 5]
    out_ref, block = refs[-2:]
    total_ref = refs[0]
    fields = refs[1 : CHUNKS + 1]
    mine_ref, far_ref, peer_mine_ref, peer_far_ref = refs[CHUNKS + 1 : CHUNKS + 5]
    height = block.shape[0] // 2
    width = fields[0].shape[1]
    used = CHUNKS * width // 2
    is_upper = where_ref[2]
    put_in_place(where_ref, lines, mine_ref, far_ref, block, is_upper * height)
    put_in_place(where_ref, lines, peer_mine_ref, peer_far_ref, block, (1 - is_upper) * height)

    def finish(mixed, c):
        here = slice(c * width, (c + 1) * width)
        value = total_ref[:, here] + mixed
        if last:
            value = (1.5 * own[c][...].astype(F32) - 0.5 * value) / jnp.sqrt(level_ref[0])
        out_ref[:, here] = value.astype(out_ref.dtype)

    def rows_of_block(c):
        first_row = c * width if c * width < used else height + c * width - used
        return block[first_row : first_row + width, :]

    @pl.when(is_upper == 0)
    def _():
        field = side_by_side(fields)
        for c in range(CHUNKS):
            here = slice(c * width, (c + 1) * width)
            right = jnp.concatenate([block[:used, here], block[height : height + used, here]], axis=0)
            finish(jnp.dot(field, right, preferred_element_type=F32), c)

    @pl.when(is_upper == 1)
    def _():
        field = side_by_side(fields)
        for c in range(CHUNKS):
            finish(lax.dot_general(field, rows_of_block(c), TRANSPOSED_RIGHT, preferred_element_type=F32), c)


def local(orbitals, hamiltonian, neighbours):
    elements, slots, size, _ = hamiltonian.shape
    rows, columns = orbitals.shape
    tiles = lax.axis_size("elem")
    groups = lax.axis_size("orb")
    lines = tiles // 2
    my_tile = lax.axis_index("elem")
    my_group = lax.axis_index("orb")
    odd = my_tile % 2
    line = my_tile // 2

    swap = [(i, i ^ 1) for i in range(tiles)]
    outward = [(2 * i + side, 2 * ((i + 1 - 2 * side) % lines) + side) for i in range(lines) for side in (0, 1)]

    def to_group(value, d):
        return lax.ppermute(value, "orb", [(i, i ^ d) for i in range(groups)])

    place = neighbours % elements
    last_two = place[:, 5:]
    place = jnp.concatenate([place[:, :5], jnp.where(odd == 0, last_two[:, ::-1], last_two)], axis=1)
    by_slot = [hamiltonian[:, s] for s in range(5)]
    by_slot.append(jnp.where(odd == 0, hamiltonian[:, 6], hamiltonian[:, 5]))
    by_slot.append(jnp.where(odd == 0, hamiltonian[:, 5], hamiltonian[:, 6]))
    by_slot.append(jnp.zeros_like(by_slot[0]))
    blocks = jnp.concatenate(by_slot, axis=2)

    width = columns // CHUNKS
    start = [lax.slice_in_dim(orbitals, c * width, (c + 1) * width, axis=1) for c in range(CHUNKS)]
    near = {(0, 0): lax.ppermute(start[0], "elem", swap)}
    order = Order(jnp.zeros((8, 128), F32))
    blocks, place = order(blocks, place)
    start = [start[0]] + [order(field) for field in start[1:]]
    for c in range(1, CHUNKS):
        near[(0, c)] = lax.ppermute(start[c], "elem", swap)

    jobs = [(stage, c) for stage in range(3) for c in range(CHUNKS)]
    far = {}
    firsts, squares, pieces = {}, [], [{} for _ in range(CHUNKS)]
    current = {(0, c): start[c] for c in range(CHUNKS)}

    def send_on(job):
        near[job] = order(near[job])
        far[job] = lax.ppermute(near[job], "elem", outward)

    def more_panel(c):
        for d in range(1, groups):
            if d & (d - 1):
                low = d & -d
                if d ^ low in pieces[c] and d not in pieces[c]:
                    pieces[c][d ^ low] = order(pieces[c][d ^ low])
                    pieces[c][d] = to_group(pieces[c][d ^ low], low)

    def multiply(job):
        stage, c = job
        far[job] = order(far[job])
        old = (None, start[c], firsts.get(c))[stage]
        out = product(stage, place, blocks, current[job], near[job], far[job], old)
        if stage == 0:
            firsts[c], out = order(*out)
        elif stage == 1:
            out = order(out)
        else:
            out, square = order(*out)
            squares.append(square)
            pieces[c][0] = out
            bit = groups // 2
            while bit:
                pieces[c][bit] = to_group(out, bit)
                bit //= 2
            if c:
                more_panel(c - 1)
            return
        current[(stage + 1, c)] = out
        near[(stage + 1, c)] = lax.ppermute(out, "elem", swap)

    for index, job in enumerate(jobs):
        send_on(job)
        if index:
            multiply(jobs[index - 1])
    multiply(jobs[-1])

    squares = sum(squares)
    rows_total = rows * tiles
    level = None
    middle = columns // 2
    unit = 16 * tiles

    def is_upper(d):
        return (my_group & (1 << (d.bit_length() - 1))) != 0

    def where(d):
        return jnp.stack([odd, line, is_upper(d) if d else odd]).astype(jnp.int32)

    def all_chunks(d):
        return [pieces[c][d] for c in range(CHUNKS)]

    def gram_chunk(d):
        height = middle if d else middle + middle // 2
        height += -height % unit
        fields = all_chunks(0)
        if d:
            more_panel(CHUNKS - 1)
            fields += order(*all_chunks(d))
        half = jax.ShapeDtypeStruct((height // 2, columns), BF16)
        scratch = (pltpu.VMEM((height, columns), BF16),)
        name = "gram_pair" if d else "gram_own"
        return call(functools.partial(gram_kernel, d > 0), name, (half, half), (where(d),), fields, scratch)

    exchanged = {}
    line_bits = [1 << i for i in range(lines.bit_length() - 1)]

    def over_z(value, bit):
        return lax.ppermute(value, "elem", [(i, i ^ (2 * bit)) for i in range(tiles)])

    def level_process():
        nonlocal level
        total = jnp.full((8, 128), jnp.sum(squares), F32)
        for axis, peers in (("orb", groups), ("elem", tiles)):
            bit = 1
            while bit < peers:
                other = lax.ppermute(total, axis, [(i, i ^ bit) for i in range(peers)])
                yield
                total = total + order(other)
                bit *= 2
        level = total[0, 0] / (columns * groups * rows_total)
        yield

    def process(d):
        mine, other = order(*gram_chunk(d))
        yield
        other = lax.ppermute(order(other), "elem", swap)
        yield
        terms = [(mine, 0), (order(other), 0)]
        height = mine.shape[0]
        offset = 0

        def added(first_row, count):
            return sum(lax.dynamic_slice_in_dim(v, first_row - row, count, 0).astype(F32) for v, row in terms)

        for bit in line_bits:
            height //= 2
            keep = (line // bit) % 2
            received = over_z(added(offset + (1 - keep) * height, height).astype(BF16), bit)
            offset = offset + keep * height
            yield
            terms.append((order(received), offset))
        part = (added(offset, height) / (level * rows_total)).astype(BF16)
        for bit in line_bits[::-1]:
            received = over_z(part, bit)
            yield
            part = jnp.concatenate([part, order(received)], axis=0)
        whole = order(part)
        if d:
            peer_whole = to_group(whole, d)
        yield
        far_whole = lax.ppermute(order(whole), "elem", swap)
        yield
        if d:
            peer_whole = order(peer_whole)
            yield
        far_whole = order(far_whole)
        if d == 0:
            exchanged[0] = (whole, far_whole)
            yield
            return
        peer_far = to_group(far_whole, d)
        yield
        peer_far = order(peer_far)
        exchanged[d] = (whole, far_whole, peer_whole, peer_far)
        yield

    queue = sorted(range(1, groups), key=lambda d: (d == 1, d))
    events = [(3.5 * (i + 1), -1, -1) for i in range(groups.bit_length() + tiles.bit_length() - 1)]
    free = 66.0
    for position, d in enumerate([0] + queue):
        summed = 20.0 + 12.0 * position
        hop = 9.0 if d else 11.5
        times = [0.0 if d == 0 else 10.5 if position == 1 else 20.5 + 0.2 * position]
        times.append(0.0 if d == 0 else summed - 11.9)
        times += [summed + hop * i for i in range(2 * len(line_bits) + 1)]
        sent = max(free + 0.1, times[-1])
        free = sent + (11.0 if d else 16.5)
        times.append(sent)
        if d:
            times.append(max(sent, times[-2] + (11.0 if d > 1 else 3.0)))
            times.append(max(times[-1], free))
            times.append(times[-1] + (11.0 if d > 1 else 3.0))
        else:
            times.append(free)
        events += [(time, position, d) for time in times]
    events.sort(key=lambda event: event[:2])
    running = {d: process(d) for d in [0] + queue}
    running[-1] = level_process()
    left_over = {d: sum(1 for event in events if event[2] == d) for d in running}
    done = []
    mixed = None
    for _, _, d in events:
        next(running[d], None)
        left_over[d] -= 1
        if left_over[d] or d < 0:
            continue
        done.append(d)
        parts = exchanged[d]
        last = len(done) == groups
        shape = jax.ShapeDtypeStruct((rows, columns), BF16 if last else F32)
        scratch = (pltpu.VMEM((len(parts) * parts[0].shape[0], columns), BF16),)
        if d == 0:
            args = (*all_chunks(0), *parts)
            mixed = order(call(functools.partial(own_kernel, lines), "mix_own", shape, (where(0),), args, scratch))
            continue
        args = (mixed, *all_chunks(d), *parts)
        scalars = (where(d),)
        if last:
            scalars += (level.reshape(1),)
            args += tuple(all_chunks(0))
        kernel = functools.partial(pair_kernel, lines, last)
        mixed = call(kernel, "mix_last" if last else "mix_pair", shape, scalars, args, scratch, {} if last else {1: 0})
        if not last:
            mixed = order(mixed)
    return mixed


def solution(mesh):
    return jax.shard_map(
        local,
        mesh=mesh,
        in_specs=(P("elem", "orb"), P("elem", None, None, None), P("elem", None)),
        out_specs=P("elem", "orb"),
        check_vma=False,
    )
```

```python
import functools

import jax
import jax.numpy as jnp
from jax import lax
from jax.experimental import pallas as pl
from jax.experimental.pallas import tpu as pltpu
from jax.sharding import PartitionSpec as P

CHUNKS = 4
F32 = jnp.float32
BF16 = jnp.bfloat16
VMEM_LIMIT = 48 * 1024 * 1024


class Order:
    def __init__(self, token):
        self.token = token

    def __call__(self, *values):
        *values, self.token = lax.optimization_barrier((*values, self.token))
        return values[0] if len(values) == 1 else tuple(values)


class Schedule:
    RATE = 94e3
    CORE_RATE = 400e3
    DELAY = 2.5

    def __init__(self):
        self.now = 0.0
        self.free = {}

    def spend(self, time):
        self.now += time

    def transfer(self, value, link, weight=1.0):
        self.spend(1.3)
        size = value.size * value.dtype.itemsize
        time = weight * (size / self.CORE_RATE if link == "core" else 2 * size / self.RATE)
        begin = max(self.now, self.free.get(link, 0.0))
        self.free[link] = begin + time
        return begin + time + self.DELAY

    def run(self, processes):
        ready = [0.0] * len(processes)
        alive = list(range(len(processes)))
        while alive:
            can = [i for i in alive if ready[i] <= self.now]
            if not can:
                self.now = min(ready[i] for i in alive)
                continue
            try:
                ready[can[0]] = next(processes[can[0]])
            except StopIteration:
                alive.remove(can[0])


def product_kernel(stage, place_ref, blocks_ref, field_ref, near_ref, far_ref, *refs):
    elements, size, _ = blocks_ref.shape
    width = field_ref.shape[1]
    squares = jnp.zeros((8, width), F32)
    filler = jnp.zeros((size, width), BF16)
    for element in range(elements):
        picked = []
        for slot in range(7):
            source = field_ref if slot < 5 else near_ref if slot == 5 else far_ref
            first_row = pl.multiple_of(place_ref[element, slot] * size, size)
            picked.append(source[pl.ds(first_row, size), :])
        stacked = jnp.concatenate(picked + [filler], axis=0)
        total = jnp.dot(blocks_ref[element], stacked, preferred_element_type=F32)
        here = pl.ds(element * size, size)
        if stage == 0:
            wide_ref, half_ref = refs
            wide_ref[here, :] = total
            half_ref[here, :] = total.astype(BF16)
        elif stage == 1:
            before_ref, half_ref = refs
            half_ref[here, :] = (2.0 * total - before_ref[here, :].astype(F32)).astype(BF16)
        else:
            before_ref, half_ref, squares_ref = refs
            value = (2.0 * total - before_ref[here, :]).astype(BF16)
            half_ref[here, :] = value
            wide = value.astype(F32)
            squares += jnp.sum((wide * wide).reshape(-1, 8, width), axis=0)
    if stage == 2:
        squares_ref[...] = squares


def call(kernel, name, outs, scalars, args, scratch=(), aliases=None):
    return pl.pallas_call(
        kernel,
        out_shape=outs,
        in_specs=[pl.BlockSpec(memory_space=pltpu.SMEM)] * len(scalars)
        + [pl.BlockSpec(memory_space=pltpu.VMEM)] * len(args),
        scratch_shapes=list(scratch),
        input_output_aliases=aliases or {},
        compiler_params=pltpu.CompilerParams(vmem_limit_bytes=VMEM_LIMIT),
        cost_estimate=pl.CostEstimate(flops=1024, bytes_accessed=1024, transcendentals=0),
        name=name,
    )(*scalars, *args)


def product(stage, place, blocks, field, by_near, by_far, before=None):
    rows, width = field.shape
    half = jax.ShapeDtypeStruct((rows, width), BF16)
    wide = jax.ShapeDtypeStruct((rows, width), F32)
    squares = jax.ShapeDtypeStruct((8, width), F32)
    outs = ((wide, half), half, (half, squares))[stage]
    args = (blocks, field, by_near, by_far) + (() if before is None else (before,))
    kernel = functools.partial(product_kernel, stage)
    return call(kernel, f"product_{stage}", outs, (place,), args)


def put_in_place(where_ref, masks, mine_ref, far_ref, out_ref, base):
    bits = len(masks)
    height = mine_ref.shape[0] >> (bits - 1)
    for side, ref in ((0, mine_ref), (1, far_ref)):
        for position in range(1 << (bits - 1)):
            distance = side << (bits - 1) | position
            number = 0
            for i, mask in enumerate(masks):
                apart = distance >> (bits - 1 - i) & 1
                number = 2 * number + lax.rem(where_ref[0] // mask + apart, 2)
            here = pl.ds(pl.multiple_of(base + number * height, height), height)
            out_ref[here, :] = ref[position * height : (position + 1) * height, :]


TRANSPOSED_LEFT = (((0,), (0,)), ((), ()))
TRANSPOSED_RIGHT = (((1,), (1,)), ((), ()))


def side_by_side(refs):
    return jnp.concatenate([ref[...] for ref in refs], axis=1)


def gram_kernel(pair, mask, where_ref, *refs):
    mine_ref, other_ref, whole = refs[-3:]
    fields = refs[:CHUNKS]
    half = whole.shape[0] // 2
    width = fields[0].shape[1]
    middle = CHUNKS * width // 2
    side = lax.rem(where_ref[0] // mask, 2)

    def fill(left, rights, count):
        for c, right in enumerate(rights):
            value = lax.dot_general(left, right[...], TRANSPOSED_LEFT, preferred_element_type=F32)
            whole[:count, c * width : (c + 1) * width] = value.astype(BF16)

    if pair:
        peers = refs[CHUNKS : 2 * CHUNKS]
        used = middle

        @pl.when(where_ref[1] == 0)
        def _():
            fill(side_by_side(peers[: CHUNKS // 2]), fields, middle)

        @pl.when(where_ref[1] == 1)
        def _():
            fill(side_by_side(fields[CHUNKS // 2 :]), peers, middle)
    else:
        used = middle + middle // 2
        upper = side_by_side(fields[CHUNKS // 2 :])
        fill(side_by_side(fields[: CHUNKS // 2]), fields, middle)
        corner = lax.dot_general(upper, upper, TRANSPOSED_LEFT, preferred_element_type=F32).astype(BF16)
        whole[middle:used, :middle] = corner[: middle // 2]
        whole[middle:used, middle:] = corner[middle // 2 :]
    if used < whole.shape[0]:
        whole[used:, :] = jnp.zeros((whole.shape[0] - used, whole.shape[1]), BF16)
    mine_ref[...] = whole[pl.ds(pl.multiple_of(side * half, half), half), :]
    other_ref[...] = whole[pl.ds(pl.multiple_of((1 - side) * half, half), half), :]


def mix_kernel(pair, masks, first, last, where_ref, *refs):
    level_ref, *refs = refs if last else (None, *refs)
    total_ref, *refs = (None, *refs) if first else refs
    fields, refs = refs[:CHUNKS], refs[CHUNKS:]
    out_ref, block = refs[-2:]
    own = refs[-2 - CHUNKS : -2]
    width = fields[0].shape[1]
    middle = CHUNKS * width // 2

    def finish(mixed, here):
        value = mixed if first else total_ref[:, here] + mixed
        if last:
            filtered = side_by_side(own)[:, here].astype(F32)
            value = (1.5 * filtered - 0.5 * value) / jnp.sqrt(level_ref[0])
        out_ref[:, here] = value.astype(out_ref.dtype)

    def times(left, right):
        return jnp.dot(left, right, preferred_element_type=F32)

    def times_transposed(left, right):
        return lax.dot_general(left, right, TRANSPOSED_RIGHT, preferred_element_type=F32)

    if not pair:
        put_in_place(where_ref, masks, refs[0], refs[1], block, 0)
        lower, upper = side_by_side(fields[: CHUNKS // 2]), side_by_side(fields[CHUNKS // 2 :])
        corner = block[middle : middle + middle // 2, :]
        corner = jnp.concatenate([corner[:, :middle], corner[:, middle:]], axis=0)
        finish(
            times(lower, block[:middle, :middle]) + times_transposed(upper, block[:middle, middle:]),
            slice(0, middle),
        )
        finish(times(lower, block[:middle, middle:]) + times(upper, corner), slice(middle, 2 * middle))
        return
    height = block.shape[0] // 2
    is_upper = where_ref[1]
    put_in_place(where_ref, masks, refs[0], refs[1], block, is_upper * height)
    put_in_place(where_ref, masks, refs[2], refs[3], block, (1 - is_upper) * height)

    @pl.when(is_upper == 0)
    def _():
        field = side_by_side(fields)
        for c in range(CHUNKS):
            here = slice(c * width, (c + 1) * width)
            finish(times(field, jnp.concatenate([block[:middle, here], block[height : height + middle, here]])), here)

    @pl.when(is_upper == 1)
    def _():
        field = side_by_side(fields)
        for c in range(CHUNKS):
            row = c * width if c * width < middle else height + c * width - middle
            finish(times_transposed(field, block[row : row + width, :]), slice(c * width, (c + 1) * width))


def local(orbitals, hamiltonian, neighbours):
    elements, slots, size, _ = hamiltonian.shape
    rows, columns = orbitals.shape
    tiles = lax.axis_size("elem")
    groups = lax.axis_size("orb")
    lines = tiles // 2
    my_tile = lax.axis_index("elem")
    my_group = lax.axis_index("orb")
    odd = my_tile % 2
    line = my_tile // 2

    swap = [(i, i ^ 1) for i in range(tiles)]
    outward = [(2 * i + side, 2 * ((i + 1 - 2 * side) % lines) + side) for i in range(lines) for side in (0, 1)]

    def to_group(value, d):
        return lax.ppermute(value, "orb", [(i, i ^ d) for i in range(groups)])

    place = neighbours % elements
    last_two = place[:, 5:]
    place = jnp.concatenate([place[:, :5], jnp.where(odd == 0, last_two[:, ::-1], last_two)], axis=1)
    by_slot = [hamiltonian[:, s] for s in range(5)]
    by_slot.append(jnp.where(odd == 0, hamiltonian[:, 6], hamiltonian[:, 5]))
    by_slot.append(jnp.where(odd == 0, hamiltonian[:, 5], hamiltonian[:, 6]))
    by_slot.append(jnp.zeros_like(by_slot[0]))
    blocks = jnp.concatenate(by_slot, axis=2)

    width = columns // CHUNKS
    start = [lax.slice_in_dim(orbitals, c * width, (c + 1) * width, axis=1) for c in range(CHUNKS)]
    near = {(0, 0): lax.ppermute(start[0], "elem", swap)}
    order = Order(jnp.zeros((8, 128), F32))
    blocks, place = order(blocks, place)
    start = [start[0]] + [order(field) for field in start[1:]]
    for c in range(1, CHUNKS):
        near[(0, c)] = lax.ppermute(start[c], "elem", swap)

    jobs = [(stage, c) for stage in range(3) for c in range(CHUNKS)]
    far = {}
    firsts, squares, pieces = {}, [], [{} for _ in range(CHUNKS)]
    current = {(0, c): start[c] for c in range(CHUNKS)}

    def send_on(job):
        near[job] = order(near[job])
        far[job] = lax.ppermute(near[job], "elem", outward)

    def more_panel(c):
        for d in range(1, groups):
            if d & (d - 1):
                low = d & -d
                if d ^ low in pieces[c] and d not in pieces[c]:
                    pieces[c][d ^ low] = order(pieces[c][d ^ low])
                    pieces[c][d] = to_group(pieces[c][d ^ low], low)

    def multiply(job):
        stage, c = job
        far[job] = order(far[job])
        old = (None, start[c], firsts.get(c))[stage]
        out = product(stage, place, blocks, current[job], near[job], far[job], old)
        if stage == 0:
            firsts[c], out = order(*out)
        elif stage == 1:
            out = order(out)
        else:
            out, square = order(*out)
            squares.append(square)
            pieces[c][0] = out
            bit = groups // 2
            while bit:
                pieces[c][bit] = to_group(out, bit)
                bit //= 2
            if c:
                more_panel(c - 1)
            return
        current[(stage + 1, c)] = out
        near[(stage + 1, c)] = lax.ppermute(out, "elem", swap)

    for index, job in enumerate(jobs):
        send_on(job)
        if index:
            multiply(jobs[index - 1])
    multiply(jobs[-1])

    squares = sum(squares)
    rows_total = rows * tiles
    level = None
    middle = columns // 2
    unit = 16 * tiles
    clock = Schedule()
    z_masks = [2 << i for i in range(lines.bit_length() - 1)]
    there = {d: 3.0 if d == 1 else 10.5 for d in range(1, groups)}
    mixed, mixes = None, 0

    def is_upper(d):
        return (my_group & (1 << (d.bit_length() - 1))) != 0

    def where(d):
        return jnp.stack([my_tile, is_upper(d) if d else odd]).astype(jnp.int32)

    def all_chunks(d):
        return [pieces[c][d] for c in range(CHUNKS)]

    def over_tiles(value, mask):
        sent = lax.ppermute(value, "elem", [(i, i ^ mask) for i in range(tiles)])
        if mask <= 2:
            return sent, clock.transfer(value, "y" if mask == 1 else "z")
        clock.spend(-1.3)
        return sent, max(clock.transfer(value, "z", mask / 4), clock.transfer(value, "middle", mask / 2))

    def over_groups(value, d):
        return to_group(value, d), clock.transfer(value, "core" if d == 1 else "x")

    def panel_process():
        yield 10.5
        more_panel(CHUNKS - 1)
        clock.spend(1.3)
        for d in range(1, groups):
            if d & (d - 1):
                there[d] = clock.now + 3.5

    def gram_chunk(d, mask):
        height = middle if d else middle + middle // 2
        height += -height % unit
        fields = all_chunks(0)
        if d:
            fields += order(*all_chunks(d))
        half = jax.ShapeDtypeStruct((height // 2, columns), BF16)
        scratch = (pltpu.VMEM((height, columns), BF16),)
        name = "gram_pair" if d else "gram_own"
        clock.spend(3.2 if d else 3.0)
        return call(functools.partial(gram_kernel, d > 0, mask), name, (half, half), (where(d),), fields, scratch)

    def level_process():
        nonlocal level
        yield 4.0
        total = jnp.full((8, 128), jnp.sum(squares), F32)
        for axis, peers in (("elem", tiles), ("orb", groups)):
            bit = 1
            while bit < peers:
                total = order(total)
                other = lax.ppermute(total, axis, [(i, i ^ bit) for i in range(peers)])
                clock.spend(1.5)
                yield clock.now + 3.5
                total = total + order(other)
                clock.spend(0.6)
                bit *= 2
        level = total[0, 0] / (columns * groups * rows_total)

    def process(d, masks):
        nonlocal mixed, mixes
        while d and (d not in pieces[-1] or there[d] > clock.now):
            yield max(there[d], clock.now + 0.5)
        mine, value = order(*gram_chunk(d, masks[0]))
        terms = [(mine, 0)]
        height, offset = mine.shape[0], 0

        def added(first_row, count):
            clock.spend(1.0)
            return sum(lax.dynamic_slice_in_dim(v, first_row - row, count, 0).astype(F32) for v, row in terms)

        for i, mask in enumerate(masks):
            if i:
                height //= 2
                keep = (my_tile // mask) % 2
                value = added(offset + (1 - keep) * height, height).astype(BF16)
                offset = offset + keep * height
            received, arrival = over_tiles(value, mask)
            yield arrival
            terms.append((order(received), offset))
        while level is None:
            yield clock.now + 0.5
        part = (added(offset, height) / (level * rows_total)).astype(BF16)
        for mask in masks[:0:-1]:
            received, arrival = over_tiles(part, mask)
            yield arrival
            part = jnp.concatenate([part, order(received)], axis=0)
            clock.spend(0.7)
        part = order(part)
        far, arrival = over_tiles(part, masks[0])
        if d:
            peer, peer_arrival = over_groups(part, d)
        yield arrival
        far = order(far)
        parts = (part, far)
        if d:
            peer_far, arrival = over_groups(far, d)
            yield peer_arrival
            peer = order(peer)
            yield arrival
            peer_far = order(peer_far)
            parts += (peer, peer_far)
        first, last = mixes == 0, mixes == groups - 1
        mixes += 1
        shape = jax.ShapeDtypeStruct((rows, columns), BF16 if last else F32)
        scratch = (pltpu.VMEM((len(parts) * part.shape[0], columns), BF16),)
        args = (() if first else (mixed,)) + (*all_chunks(d), *parts)
        scalars = (where(d),)
        if last:
            scalars += (level.reshape(1),)
            args += tuple(all_chunks(0))
        kernel = functools.partial(mix_kernel, d > 0, masks, first, last)
        name = "mix_pair" if d else "mix_own"
        clock.spend(5.7 if d else 4.5)
        mixed = call(kernel, name, shape, scalars, args, scratch, {} if first or last else {1: 0})
        if not last:
            mixed = order(mixed)

    y_first, z_first, z_then_y = (1, *z_masks), (*z_masks, 1), (*z_masks[:1], 1, *z_masks[1:])
    queue = sorted(range(1, groups), key=lambda d: (d == 1, d))
    processes = [panel_process(), level_process(), process(0, z_first)]
    processes += [process(d, z_then_y if i == 0 else y_first) for i, d in enumerate(queue)]
    clock.run(processes)
    return mixed


def solution(mesh):
    return jax.shard_map(
        local,
        mesh=mesh,
        in_specs=(P("elem", "orb"), P("elem", None, None, None), P("elem", None)),
        out_specs=P("elem", "orb"),
        check_vma=False,
    )
```

```python
import functools

import jax
import jax.numpy as jnp
from jax import lax
from jax.experimental import pallas as pl
from jax.experimental.pallas import tpu as pltpu
from jax.sharding import PartitionSpec as P

CHUNKS = 4
F32 = jnp.float32
BF16 = jnp.bfloat16
MIB = 1024 * 1024
EXTRA = 16


class Order:
    def __init__(self, token):
        self.token = token

    def __call__(self, *values):
        *values, self.token = lax.optimization_barrier((*values, self.token))
        return values[0] if len(values) == 1 else tuple(values)


class Schedule:
    RATE = 94e3
    CORE_RATE = 400e3
    DELAY = 2.5

    def __init__(self):
        self.now = 0.0
        self.free = {}

    def spend(self, time):
        self.now += time

    def transfer(self, value, link, weight=1.0):
        self.spend(1.3)
        size = value.size * value.dtype.itemsize
        time = weight * (size / self.CORE_RATE if link == "core" else 2 * size / self.RATE)
        begin = max(self.now, self.free.get(link, 0.0))
        self.free[link] = begin + time
        return begin + time + self.DELAY

    def run(self, processes):
        ready = [0.0] * len(processes)
        alive = list(range(len(processes)))
        while alive:
            can = [i for i in alive if ready[i] <= self.now]
            if not can:
                self.now = min(ready[i] for i in alive)
                continue
            try:
                ready[can[0]] = next(processes[can[0]])
            except StopIteration:
                alive.remove(can[0])


def product_kernel(stage, place_ref, blocks_ref, field_ref, near_ref, far_ref, *refs):
    elements, size, _ = blocks_ref.shape
    width = field_ref.shape[1]
    squares = jnp.zeros((8, width), F32)
    filler = jnp.zeros((size, width), BF16)
    for element in range(elements):
        picked = []
        for slot in range(7):
            source = field_ref if slot < 5 else near_ref if slot == 5 else far_ref
            first_row = pl.multiple_of(place_ref[element, slot] * size, size)
            picked.append(source[pl.ds(first_row, size), :])
        stacked = jnp.concatenate(picked + [filler], axis=0)
        total = jnp.dot(blocks_ref[element], stacked, preferred_element_type=F32)
        here = pl.ds(element * size, size)
        if stage == 0:
            wide_ref, half_ref = refs
            wide_ref[here, :] = total
            half_ref[here, :] = total.astype(BF16)
        elif stage == 1:
            before_ref, half_ref = refs
            half_ref[here, :] = (2.0 * total - before_ref[here, :].astype(F32)).astype(BF16)
        else:
            before_ref, earlier_ref, half_ref, squares_ref = refs
            value = (2.0 * total - before_ref[here, :]).astype(BF16)
            half_ref[here, :] = value
            wide = value.astype(F32)
            squares += jnp.sum((wide * wide).reshape(-1, 8, width), axis=0)
    if stage == 2:
        squares_ref[...] = earlier_ref[...] + squares


def call(kernel, name, outs, scalars, args, scratch=(), aliases=None, vmem=16):
    return pl.pallas_call(
        kernel,
        out_shape=outs,
        in_specs=[pl.BlockSpec(memory_space=pltpu.SMEM)] * len(scalars)
        + [pl.BlockSpec(memory_space=pltpu.VMEM)] * len(args),
        scratch_shapes=list(scratch),
        input_output_aliases=aliases or {},
        compiler_params=pltpu.CompilerParams(vmem_limit_bytes=vmem * MIB),
        cost_estimate=pl.CostEstimate(flops=1024, bytes_accessed=1024, transcendentals=0),
        name=name,
    )(*scalars, *args)


def product(stage, place, blocks, field, by_near, by_far, *before):
    rows, width = field.shape
    half = jax.ShapeDtypeStruct((rows, width), BF16)
    wide = jax.ShapeDtypeStruct((rows, width), F32)
    squares = jax.ShapeDtypeStruct((8, width), F32)
    outs = ((wide, half), half, (half, squares))[stage]
    args = (blocks, field, by_near, by_far, *before)
    kernel = functools.partial(product_kernel, stage)
    return call(kernel, f"product_{stage}", outs, (place,), args)


def put_in_place(where_ref, masks, mine_ref, far_ref, out_ref, base):
    bits = len(masks)
    height = mine_ref.shape[0] >> (bits - 1)
    for side, ref in ((0, mine_ref), (1, far_ref)):
        for position in range(1 << (bits - 1)):
            distance = side << (bits - 1) | position
            number = 0
            for i, mask in enumerate(masks):
                apart = distance >> (bits - 1 - i) & 1
                number = 2 * number + lax.rem(where_ref[0] // mask + apart, 2)
            here = pl.ds(pl.multiple_of(base + number * height, height), height)
            out_ref[here, :] = ref[position * height : (position + 1) * height, :]


TRANSPOSED_LEFT = (((0,), (0,)), ((), ()))
TRANSPOSED_RIGHT = (((1,), (1,)), ((), ()))


def extra_rows(value):
    first = lax.reduce_precision(value, 8, 7)
    second = lax.reduce_precision(value - first, 8, 7)
    third = value - first - second
    row = lax.broadcasted_iota(jnp.int32, (EXTRA, value.shape[1]), 0)
    rows = jnp.where(row == 0, first, jnp.where(row == 1, second, jnp.where(row == 2, third, 0.0)))
    return rows.astype(BF16)


def side_by_side(refs):
    return jnp.concatenate([ref[...] for ref in refs], axis=1)


def gram_kernel(pair, mask, where_ref, *refs):
    mine_ref, other_ref, whole = refs[-3:]
    fields = refs[:CHUNKS]
    half = whole.shape[0] // 2
    if mine_ref.shape[0] > half:
        carried = extra_rows(jnp.full((1, whole.shape[1]), jnp.sum(refs[2 * CHUNKS][...])))
        mine_ref[half:, :] = carried
        other_ref[half:, :] = carried
    width = fields[0].shape[1]
    middle = CHUNKS * width // 2
    side = lax.rem(where_ref[0] // mask, 2)

    def fill(left, rights, count):
        for c, right in enumerate(rights):
            value = lax.dot_general(left, right[...], TRANSPOSED_LEFT, preferred_element_type=F32)
            whole[:count, c * width : (c + 1) * width] = value.astype(BF16)

    if pair:
        peers = refs[CHUNKS : 2 * CHUNKS]
        used = middle

        @pl.when(where_ref[1] == 0)
        def _():
            fill(side_by_side(peers[: CHUNKS // 2]), fields, middle)

        @pl.when(where_ref[1] == 1)
        def _():
            fill(side_by_side(fields[CHUNKS // 2 :]), peers, middle)
    else:
        used = middle + middle // 2
        upper = side_by_side(fields[CHUNKS // 2 :])
        fill(side_by_side(fields[: CHUNKS // 2]), fields, middle)
        corner = lax.dot_general(upper, upper, TRANSPOSED_LEFT, preferred_element_type=F32).astype(BF16)
        whole[middle:used, :middle] = corner[: middle // 2]
        whole[middle:used, middle:] = corner[middle // 2 :]
    if used < whole.shape[0]:
        whole[used:, :] = jnp.zeros((whole.shape[0] - used, whole.shape[1]), BF16)
    mine_ref[:half, :] = whole[pl.ds(pl.multiple_of(side * half, half), half), :]
    other_ref[:half, :] = whole[pl.ds(pl.multiple_of((1 - side) * half, half), half), :]


def mix_kernel(pair, masks, first, last, where_ref, *refs):
    level_ref, *refs = refs if last else (None, *refs)
    total_ref, *refs = (None, *refs) if first else refs
    fields, refs = refs[:CHUNKS], refs[CHUNKS:]
    out_ref, block = refs[-2:]
    own = refs[-2 - CHUNKS : -2]
    width = fields[0].shape[1]
    middle = CHUNKS * width // 2

    def finish(mixed, here):
        value = mixed if first else total_ref[:, here] + mixed
        if last:
            filtered = side_by_side(own)[:, here].astype(F32)
            value = (1.5 * filtered - 0.5 * value) / jnp.sqrt(level_ref[0])
        out_ref[:, here] = value.astype(out_ref.dtype)

    def times(left, right):
        return jnp.dot(left, right, preferred_element_type=F32)

    def times_transposed(left, right):
        return lax.dot_general(left, right, TRANSPOSED_RIGHT, preferred_element_type=F32)

    if not pair:
        put_in_place(where_ref, masks, refs[0], refs[1], block, 0)
        lower, upper = side_by_side(fields[: CHUNKS // 2]), side_by_side(fields[CHUNKS // 2 :])
        corner = block[middle : middle + middle // 2, :]
        corner = jnp.concatenate([corner[:, :middle], corner[:, middle:]], axis=0)
        finish(
            times(lower, block[:middle, :middle]) + times_transposed(upper, block[:middle, middle:]),
            slice(0, middle),
        )
        finish(times(lower, block[:middle, middle:]) + times(upper, corner), slice(middle, 2 * middle))
        return
    height = block.shape[0] // 2
    is_upper = where_ref[1]
    put_in_place(where_ref, masks, refs[0], refs[1], block, is_upper * height)
    put_in_place(where_ref, masks, refs[2], refs[3], block, (1 - is_upper) * height)

    @pl.when(is_upper == 0)
    def _():
        field = side_by_side(fields)
        for c in range(CHUNKS):
            here = slice(c * width, (c + 1) * width)
            finish(times(field, jnp.concatenate([block[:middle, here], block[height : height + middle, here]])), here)

    @pl.when(is_upper == 1)
    def _():
        field = side_by_side(fields)
        for c in range(CHUNKS):
            row = c * width if c * width < middle else height + c * width - middle
            finish(times_transposed(field, block[row : row + width, :]), slice(c * width, (c + 1) * width))


def local(orbitals, hamiltonian, neighbours):
    elements, slots, size, _ = hamiltonian.shape
    rows, columns = orbitals.shape
    tiles = lax.axis_size("elem")
    groups = lax.axis_size("orb")
    lines = tiles // 2
    my_tile = lax.axis_index("elem")
    my_group = lax.axis_index("orb")
    odd = my_tile % 2
    line = my_tile // 2

    swap = [(i, i ^ 1) for i in range(tiles)]
    outward = [(2 * i + side, 2 * ((i + 1 - 2 * side) % lines) + side) for i in range(lines) for side in (0, 1)]

    def to_group(value, d):
        return lax.ppermute(value, "orb", [(i, i ^ d) for i in range(groups)])

    place = neighbours % elements
    last_two = place[:, 5:]
    place = jnp.concatenate([place[:, :5], jnp.where(odd == 0, last_two[:, ::-1], last_two)], axis=1)
    by_slot = [hamiltonian[:, s] for s in range(5)]
    by_slot.append(jnp.where(odd == 0, hamiltonian[:, 6], hamiltonian[:, 5]))
    by_slot.append(jnp.where(odd == 0, hamiltonian[:, 5], hamiltonian[:, 6]))
    by_slot.append(jnp.zeros_like(by_slot[0]))
    blocks = jnp.concatenate(by_slot, axis=2)

    width = columns // CHUNKS
    start = [lax.slice_in_dim(orbitals, c * width, (c + 1) * width, axis=1) for c in range(CHUNKS)]
    near = {(0, 0): lax.ppermute(start[0], "elem", swap)}
    order = Order(jnp.zeros((8, 128), F32))
    blocks, place = order(blocks, place)
    start = [start[0]] + [order(field) for field in start[1:]]
    for c in range(1, CHUNKS):
        near[(0, c)] = lax.ppermute(start[c], "elem", swap)

    jobs = [(stage, c) for stage in range(3) for c in range(CHUNKS)]
    far = {}
    firsts, squares, pieces = {}, jnp.zeros((8, width), F32), [{} for _ in range(CHUNKS)]
    current = {(0, c): start[c] for c in range(CHUNKS)}

    def send_on(job):
        near[job] = order(near[job])
        far[job] = lax.ppermute(near[job], "elem", outward)

    def more_panel(c):
        for d in range(1, groups):
            if d & (d - 1):
                low = d & -d
                if d ^ low in pieces[c] and d not in pieces[c]:
                    pieces[c][d ^ low] = order(pieces[c][d ^ low])
                    pieces[c][d] = to_group(pieces[c][d ^ low], low)

    def multiply(job):
        nonlocal squares
        stage, c = job
        far[job] = order(far[job])
        old = ((), (start[c],), (firsts.get(c), squares))[stage]
        out = product(stage, place, blocks, current[job], near[job], far[job], *old)
        if stage == 0:
            firsts[c], out = order(*out)
        elif stage == 1:
            out = order(out)
        else:
            out, squares = order(*out)
            pieces[c][0] = out
            bit = groups // 2
            while bit:
                pieces[c][bit] = to_group(out, bit)
                bit //= 2
            if c:
                more_panel(c - 1)
            return
        current[(stage + 1, c)] = out
        near[(stage + 1, c)] = lax.ppermute(out, "elem", swap)

    for index, job in enumerate(jobs):
        send_on(job)
        if index:
            multiply(jobs[index - 1])
    multiply(jobs[-1])

    rows_total = rows * tiles
    level = None
    middle = columns // 2
    unit = 16 * tiles
    clock = Schedule()
    z_masks = [2 << i for i in range(lines.bit_length() - 1)]
    there = {d: 3.0 if d == 1 else 10.5 for d in range(1, groups)}
    mixed, mixes = None, 0
    squares_ready = False

    def is_upper(d):
        return (my_group & (1 << (d.bit_length() - 1))) != 0

    def where(d):
        return jnp.stack([my_tile, is_upper(d) if d else odd]).astype(jnp.int32)

    def all_chunks(d):
        return [pieces[c][d] for c in range(CHUNKS)]

    def over_tiles(value, mask):
        sent = lax.ppermute(value, "elem", [(i, i ^ mask) for i in range(tiles)])
        if mask <= 2:
            return sent, clock.transfer(value, "y" if mask == 1 else "z")
        clock.spend(-1.3)
        return sent, max(clock.transfer(value, "z", mask / 4), clock.transfer(value, "middle", mask / 2))

    def over_groups(value, d):
        return to_group(value, d), clock.transfer(value, "core" if d == 1 else "x")

    def panel_process():
        yield 10.5
        more_panel(CHUNKS - 1)
        clock.spend(1.3)
        for d in range(1, groups):
            if d & (d - 1):
                there[d] = clock.now + 3.5

    def gram_chunk(d, mask, extra):
        height = middle if d else middle + middle // 2
        height += -height % unit
        fields = all_chunks(0)
        if d:
            fields += list(order(*all_chunks(d)))
        if extra:
            fields.append(squares)
        half = jax.ShapeDtypeStruct((height // 2 + extra, columns), BF16)
        scratch = (pltpu.VMEM((height, columns), BF16),)
        name = "gram_pair" if d else "gram_own"
        clock.spend(3.2 if d else 3.0)
        return call(functools.partial(gram_kernel, d > 0, mask), name, (half, half), (where(d),), fields, scratch)

    def level_process():
        nonlocal squares
        bit = 1
        while bit < groups:
            other = to_group(order(squares), bit)
            clock.spend(1.5)
            yield clock.now + (2.5 if bit == 1 else 7.0)
            squares = squares + order(other)
            clock.spend(0.6)
            bit *= 2
        nonlocal squares_ready
        squares_ready = True

    def process(d, masks, extra=0):
        nonlocal mixed, mixes, level
        while d and (d not in pieces[-1] or there[d] > clock.now or extra and not squares_ready):
            yield max(there[d], clock.now + 0.5)
        mine, value = order(*gram_chunk(d, masks[0], extra))
        terms = [(mine, 0)]
        height, offset = mine.shape[0] - extra, 0

        def carried(value):
            rows = lax.slice_in_dim(value, value.shape[0] - extra, value.shape[0], axis=0)
            return jnp.sum(rows.astype(F32), axis=0, keepdims=True)

        if extra:
            total = carried(mine)

        def added(first_row, count):
            clock.spend(1.0)
            return sum(lax.dynamic_slice_in_dim(v, first_row - row, count, 0).astype(F32) for v, row in terms)

        for i, mask in enumerate(masks):
            if i:
                height //= 2
                keep = (my_tile // mask) % 2
                value = added(offset + (1 - keep) * height, height).astype(BF16)
                if extra:
                    value = jnp.concatenate([value, extra_rows(total)], axis=0)
                    clock.spend(1.0)
                offset = offset + keep * height
            received, arrival = over_tiles(value, mask)
            yield arrival if i or mask > 1 else arrival - 3.0
            received = order(received)
            terms.append((received, offset))
            if extra:
                total = total + carried(received)
        if extra:
            level = total[0, 0] / (columns * groups * rows_total)
        while level is None:
            yield clock.now + 0.5
        part = (added(offset, height) / (level * rows_total)).astype(BF16)
        for mask in masks[:0:-1]:
            received, arrival = over_tiles(part, mask)
            yield arrival
            part = jnp.concatenate([part, order(received)], axis=0)
            clock.spend(0.7)
        part = order(part)
        far, arrival = over_tiles(part, masks[0])
        if d:
            peer, peer_arrival = over_groups(part, d)
        yield arrival
        far = order(far)
        parts = (part, far)
        if d:
            peer_far, arrival = over_groups(far, d)
            yield peer_arrival
            peer = order(peer)
            yield arrival
            peer_far = order(peer_far)
            parts += (peer, peer_far)
        first, last = mixes == 0, mixes == groups - 1
        mixes += 1
        shape = jax.ShapeDtypeStruct((rows, columns), BF16 if last else F32)
        scratch = (pltpu.VMEM((len(parts) * part.shape[0], columns), BF16),)
        args = (() if first else (mixed,)) + (*all_chunks(d), *parts)
        scalars = (where(d),)
        if last:
            scalars += (level.reshape(1),)
            args += tuple(all_chunks(0))
        kernel = functools.partial(mix_kernel, d > 0, masks, first, last)
        name = "mix_pair" if d else "mix_own"
        clock.spend(5.7 if d else 4.5)
        mixed = call(kernel, name, shape, scalars, args, scratch, {} if first or last else {1: 0}, 28)
        if not last:
            mixed = order(mixed)

    y_first, z_first, z_then_y = (1, *z_masks), (*z_masks, 1), (*z_masks[:1], 1, *z_masks[1:])
    queue = sorted(range(1, groups), key=lambda d: (d == 1, d))
    processes = [panel_process(), level_process(), process(0, z_first)]
    processes += [process(d, z_then_y if i == 0 else y_first, 0 if i else EXTRA) for i, d in enumerate(queue)]
    clock.run(processes)
    return mixed


def solution(mesh):
    return jax.shard_map(
        local,
        mesh=mesh,
        in_specs=(P("elem", "orb"), P("elem", None, None, None), P("elem", None)),
        out_specs=P("elem", "orb"),
        check_vma=False,
    )
```

```python
import functools

import jax
import jax.numpy as jnp
from jax import lax
from jax.experimental import pallas as pl
from jax.experimental.pallas import tpu as pltpu
from jax.sharding import PartitionSpec as P

CHUNKS = 4
F32 = jnp.float32
BF16 = jnp.bfloat16
MIB = 1024 * 1024
EXTRA = 16


class Order:
    def __init__(self, token):
        self.token = token

    def __call__(self, *values):
        *values, self.token = lax.optimization_barrier((*values, self.token))
        return values[0] if len(values) == 1 else tuple(values)


class Schedule:
    RATE = 94e3
    CORE_RATE = 400e3
    DELAY = 2.5

    def __init__(self):
        self.now = 0.0
        self.free = {}

    def spend(self, time):
        self.now += time

    def transfer(self, value, link, weight=1.0):
        self.spend(1.3)
        size = value.size * value.dtype.itemsize
        time = weight * (size / self.CORE_RATE if link == "core" else 2 * size / self.RATE)
        begin = max(self.now, self.free.get(link, 0.0))
        self.free[link] = begin + time
        return begin + time + self.DELAY

    def run(self, processes):
        ready = [0.0] * len(processes)
        alive = list(range(len(processes)))
        while alive:
            can = [i for i in alive if ready[i] <= self.now]
            if not can:
                self.now = min(ready[i] for i in alive)
                continue
            try:
                ready[can[0]] = next(processes[can[0]])
            except StopIteration:
                alive.remove(can[0])


def product_kernel(stage, place_ref, blocks_ref, field_ref, near_ref, far_ref, *refs):
    elements, size, _ = blocks_ref.shape
    width = field_ref.shape[1]
    squares = jnp.zeros((8, width), F32)
    filler = jnp.zeros((size, width), BF16)
    for element in range(elements):
        picked = []
        for slot in range(7):
            source = field_ref if slot < 5 else near_ref if slot == 5 else far_ref
            first_row = pl.multiple_of(place_ref[element, slot] * size, size)
            picked.append(source[pl.ds(first_row, size), :])
        stacked = jnp.concatenate(picked + [filler], axis=0)
        total = jnp.dot(blocks_ref[element], stacked, preferred_element_type=F32)
        here = pl.ds(element * size, size)
        if stage == 0:
            wide_ref, half_ref = refs
            wide_ref[here, :] = total
            half_ref[here, :] = total.astype(BF16)
        elif stage == 1:
            before_ref, half_ref = refs
            half_ref[here, :] = (2.0 * total - before_ref[here, :].astype(F32)).astype(BF16)
        else:
            before_ref, earlier_ref, half_ref, *squares_ref = refs
            value = (2.0 * total - before_ref[here, :]).astype(BF16)
            half_ref[here, :] = value
            wide = value.astype(F32)
            squares += jnp.sum((wide * wide).reshape(-1, 8, width), axis=0)
    if stage == 2:
        squares = earlier_ref[...] + squares
        if squares_ref:
            squares_ref[0][...] = squares
        else:
            half_ref[elements * size :, :] = extra_rows(jnp.full((1, width), jnp.sum(squares)))


def call(kernel, name, outs, scalars, args, scratch=(), aliases=None, vmem=16):
    return pl.pallas_call(
        kernel,
        out_shape=outs,
        in_specs=[pl.BlockSpec(memory_space=pltpu.SMEM)] * len(scalars)
        + [pl.BlockSpec(memory_space=pltpu.VMEM)] * len(args),
        scratch_shapes=list(scratch),
        input_output_aliases=aliases or {},
        compiler_params=pltpu.CompilerParams(vmem_limit_bytes=vmem * MIB),
        cost_estimate=pl.CostEstimate(flops=1024, bytes_accessed=1024, transcendentals=0),
        name=name,
    )(*scalars, *args)


def product(stage, place, blocks, field, by_near, by_far, *before, last=False):
    rows, width = field.shape
    ended = jax.ShapeDtypeStruct((rows + EXTRA, width), BF16)
    half = jax.ShapeDtypeStruct((rows, width), BF16)
    wide = jax.ShapeDtypeStruct((rows, width), F32)
    squares = jax.ShapeDtypeStruct((8, width), F32)
    outs = ((wide, half), half, ended if last else (half, squares))[stage]
    args = (blocks, field, by_near, by_far, *before)
    kernel = functools.partial(product_kernel, stage)
    return call(kernel, f"product_{stage}", outs, (place,), args)


def put_in_place(where_ref, masks, mine_ref, far_ref, out_ref, base):
    bits = len(masks)
    height = mine_ref.shape[0] >> (bits - 1)
    for side, ref in ((0, mine_ref), (1, far_ref)):
        for position in range(1 << (bits - 1)):
            distance = side << (bits - 1) | position
            number = 0
            for i, mask in enumerate(masks):
                apart = distance >> (bits - 1 - i) & 1
                number = 2 * number + lax.rem(where_ref[0] // mask + apart, 2)
            here = pl.ds(pl.multiple_of(base + number * height, height), height)
            out_ref[here, :] = ref[position * height : (position + 1) * height, :]


TRANSPOSED_LEFT = (((0,), (0,)), ((), ()))
TRANSPOSED_RIGHT = (((1,), (1,)), ((), ()))


def extra_rows(value):
    first = lax.reduce_precision(value, 8, 7)
    second = lax.reduce_precision(value - first, 8, 7)
    third = value - first - second
    row = lax.broadcasted_iota(jnp.int32, (EXTRA, value.shape[1]), 0)
    rows = jnp.where(row == 0, first, jnp.where(row == 1, second, jnp.where(row == 2, third, 0.0)))
    return rows.astype(BF16)


def side_by_side(refs, rows):
    return jnp.concatenate([ref[:rows, :] for ref in refs], axis=1)


def gram_kernel(pair, mask, where_ref, *refs):
    mine_ref, other_ref, whole = refs[-3:]
    fields = refs[:CHUNKS]
    rows, width = fields[0].shape
    half = whole.shape[0] // 2
    middle = CHUNKS * width // 2
    side = lax.rem(where_ref[0] // mask, 2)

    def fill(left, rights, count):
        for c, right in enumerate(rights):
            value = lax.dot_general(left, right[:rows, :], TRANSPOSED_LEFT, preferred_element_type=F32)
            whole[:count, c * width : (c + 1) * width] = value.astype(BF16)

    if pair:
        peers = refs[CHUNKS : 2 * CHUNKS]
        used = middle

        @pl.when(where_ref[1] == 0)
        def _():
            fill(side_by_side(peers[: CHUNKS // 2], rows), fields, middle)

        @pl.when(where_ref[1] == 1)
        def _():
            fill(side_by_side(fields[CHUNKS // 2 :], rows), peers, middle)
    else:
        used = middle + middle // 2
        upper = side_by_side(fields[CHUNKS // 2 :], rows)
        fill(side_by_side(fields[: CHUNKS // 2], rows), fields, middle)
        corner = lax.dot_general(upper, upper, TRANSPOSED_LEFT, preferred_element_type=F32).astype(BF16)
        whole[middle:used, :middle] = corner[: middle // 2]
        whole[middle:used, middle:] = corner[middle // 2 :]
    if used < whole.shape[0]:
        whole[used:, :] = jnp.zeros((whole.shape[0] - used, whole.shape[1]), BF16)
    mine_ref[:half, :] = whole[pl.ds(pl.multiple_of(side * half, half), half), :]
    other_ref[:half, :] = whole[pl.ds(pl.multiple_of((1 - side) * half, half), half), :]
    if mine_ref.shape[0] > half:
        ends = [fields[-1], *refs[2 * CHUNKS - 1 : -3]]
        total = sum(jnp.sum(end[rows:, :].astype(F32), axis=0, keepdims=True) for end in ends)
        carried = extra_rows(jnp.concatenate([total] * CHUNKS, axis=1))
        mine_ref[half:, :] = carried
        other_ref[half:, :] = carried


def sum_kernel(masks, hop, extra, entries, rows_total, where_ref, *refs):
    terms, outs = refs[: hop + 1], refs[hop + 1 :]
    height = terms[0].shape[0] - extra
    begins, offset = [0, 0], 0
    final = hop == len(masks)
    for i, mask in enumerate(masks[1 : hop + 1], 1):
        height //= 2
        keep = lax.rem(where_ref[0] // mask, 2)
        first_row = offset + (1 - keep) * height
        offset = offset + keep * height
        begins.append(offset)
    if final:
        first_row = offset
    step = terms[-1].shape[0] - extra if final else height
    value = 0.0
    for term, begin in zip(terms, begins):
        here = pl.ds(pl.multiple_of(first_row - begin, EXTRA), step)
        value = value + term[here, :].astype(F32)
    total = None
    if extra:
        total = sum(jnp.sum(term[-extra:, :].astype(F32), axis=0, keepdims=True) for term in terms)
    if not final:
        outs[0][:step, :] = value.astype(BF16)
        if extra:
            outs[0][step:, :] = extra_rows(total)
        return
    if extra:
        level = total / entries
        outs[1][...] = jnp.broadcast_to(level[:, :1], outs[1].shape)
    else:
        level_ref, *outs = outs
        level = level_ref[:1, :1]
    outs[0][...] = (value / (level * rows_total)).astype(BF16)


def mix_kernel(pair, masks, first, last, where_ref, *refs):
    level_ref, *refs = refs if last else (None, *refs)
    total_ref, *refs = (None, *refs) if first else refs
    fields, refs = refs[:CHUNKS], refs[CHUNKS:]
    out_ref, block = refs[-2:]
    own = refs[-2 - CHUNKS : -2]
    rows, width = fields[0].shape
    middle = CHUNKS * width // 2

    def finish(mixed, here):
        value = mixed if first else total_ref[:, here] + mixed
        if last:
            filtered = side_by_side(own, rows)[:, here].astype(F32)
            value = (1.5 * filtered - 0.5 * value) / jnp.sqrt(level_ref[:1, :1])
        out_ref[:, here] = value.astype(out_ref.dtype)

    def times(left, right):
        return jnp.dot(left, right, preferred_element_type=F32)

    def times_transposed(left, right):
        return lax.dot_general(left, right, TRANSPOSED_RIGHT, preferred_element_type=F32)

    if not pair:
        put_in_place(where_ref, masks, refs[0], refs[1], block, 0)
        lower, upper = side_by_side(fields[: CHUNKS // 2], rows), side_by_side(fields[CHUNKS // 2 :], rows)
        corner = block[middle : middle + middle // 2, :]
        corner = jnp.concatenate([corner[:, :middle], corner[:, middle:]], axis=0)
        finish(
            times(lower, block[:middle, :middle]) + times_transposed(upper, block[:middle, middle:]),
            slice(0, middle),
        )
        finish(times(lower, block[:middle, middle:]) + times(upper, corner), slice(middle, 2 * middle))
        return
    height = block.shape[0] // 2
    is_upper = where_ref[1]
    put_in_place(where_ref, masks, refs[0], refs[1], block, is_upper * height)
    put_in_place(where_ref, masks, refs[2], refs[3], block, (1 - is_upper) * height)

    @pl.when(is_upper == 0)
    def _():
        field = side_by_side(fields, rows)
        for c in range(CHUNKS):
            here = slice(c * width, (c + 1) * width)
            finish(times(field, jnp.concatenate([block[:middle, here], block[height : height + middle, here]])), here)

    @pl.when(is_upper == 1)
    def _():
        field = side_by_side(fields, rows)
        for c in range(CHUNKS):
            row = c * width if c * width < middle else height + c * width - middle
            finish(times_transposed(field, block[row : row + width, :]), slice(c * width, (c + 1) * width))


def local(orbitals, hamiltonian, neighbours):
    elements, slots, size, _ = hamiltonian.shape
    rows, columns = orbitals.shape
    tiles = lax.axis_size("elem")
    groups = lax.axis_size("orb")
    lines = tiles // 2
    my_tile = lax.axis_index("elem")
    my_group = lax.axis_index("orb")
    odd = my_tile % 2
    line = my_tile // 2

    swap = [(i, i ^ 1) for i in range(tiles)]
    outward = [(2 * i + side, 2 * ((i + 1 - 2 * side) % lines) + side) for i in range(lines) for side in (0, 1)]

    def to_group(value, d):
        return lax.ppermute(value, "orb", [(i, i ^ d) for i in range(groups)])

    place = neighbours % elements
    last_two = place[:, 5:]
    place = jnp.concatenate([place[:, :5], jnp.where(odd == 0, last_two[:, ::-1], last_two)], axis=1)
    by_slot = [hamiltonian[:, s] for s in range(5)]
    by_slot.append(jnp.where(odd == 0, hamiltonian[:, 6], hamiltonian[:, 5]))
    by_slot.append(jnp.where(odd == 0, hamiltonian[:, 5], hamiltonian[:, 6]))
    by_slot.append(jnp.zeros_like(by_slot[0]))
    blocks = jnp.concatenate(by_slot, axis=2)

    width = columns // CHUNKS
    start = [lax.slice_in_dim(orbitals, c * width, (c + 1) * width, axis=1) for c in range(CHUNKS)]
    near = {(0, 0): lax.ppermute(start[0], "elem", swap)}
    order = Order(jnp.zeros((8, 128), F32))
    blocks, place = order(blocks, place)
    start = [start[0]] + [order(field) for field in start[1:]]
    for c in range(1, CHUNKS):
        near[(0, c)] = lax.ppermute(start[c], "elem", swap)

    jobs = [(stage, c) for stage in range(3) for c in range(CHUNKS)]
    far = {}
    firsts, squares, pieces = {}, jnp.zeros((8, width), F32), [{} for _ in range(CHUNKS)]
    current = {(0, c): start[c] for c in range(CHUNKS)}

    def send_on(job):
        near[job] = order(near[job])
        far[job] = lax.ppermute(near[job], "elem", outward)

    def more_panel(c):
        for d in range(1, groups):
            if d & (d - 1):
                low = d & -d
                if d ^ low in pieces[c] and d not in pieces[c]:
                    pieces[c][d ^ low] = order(pieces[c][d ^ low])
                    pieces[c][d] = to_group(pieces[c][d ^ low], low)

    def multiply(job):
        nonlocal squares
        stage, c = job
        far[job] = order(far[job])
        old = ((), (start[c],), (firsts.get(c), squares))[stage]
        last = stage == 2 and c == CHUNKS - 1
        out = product(stage, place, blocks, current[job], near[job], far[job], *old, last=last)
        if stage == 0:
            firsts[c], out = order(*out)
        elif stage == 1:
            out = order(out)
        else:
            if last:
                out = order(out)
            else:
                out, squares = order(*out)
            pieces[c][0] = out
            bit = groups // 2
            while bit:
                pieces[c][bit] = to_group(out, bit)
                bit //= 2
            if c:
                more_panel(c - 1)
            return
        current[(stage + 1, c)] = out
        near[(stage + 1, c)] = lax.ppermute(out, "elem", swap)

    for index, job in enumerate(jobs):
        send_on(job)
        if index:
            multiply(jobs[index - 1])
    multiply(jobs[-1])

    rows_total = rows * tiles
    level = None
    middle = columns // 2
    unit = 16 * tiles
    clock = Schedule()
    z_masks = [2 << i for i in range(lines.bit_length() - 1)]
    there = {d: 3.0 if d == 1 else 10.5 for d in range(1, groups)}
    mixed, mixes = None, 0

    def is_upper(d):
        return (my_group & (1 << (d.bit_length() - 1))) != 0

    def where(d):
        return jnp.stack([my_tile, is_upper(d) if d else odd]).astype(jnp.int32)

    def all_chunks(d):
        return [pieces[c][d] for c in range(CHUNKS)]

    def over_tiles(value, mask):
        sent = lax.ppermute(value, "elem", [(i, i ^ mask) for i in range(tiles)])
        if mask <= 2:
            return sent, clock.transfer(value, "y" if mask == 1 else "z")
        clock.spend(-1.3)
        return sent, max(clock.transfer(value, "z", mask / 4), clock.transfer(value, "middle", mask / 2))

    def over_groups(value, d):
        return to_group(value, d), clock.transfer(value, "core" if d == 1 else "x")

    def panel_process():
        yield 10.5
        more_panel(CHUNKS - 1)
        clock.spend(1.3)
        for d in range(1, groups):
            if d & (d - 1):
                there[d] = clock.now + 3.5

    def gram_chunk(d, mask, extra):
        height = middle if d else middle + middle // 2
        height += -height % unit
        fields = all_chunks(0)
        if d:
            fields += list(order(*all_chunks(d)))
        if extra:
            fields += [pieces[-1][other] for other in range(1, groups) if other != d]
        half = jax.ShapeDtypeStruct((height // 2 + extra, columns), BF16)
        scratch = (pltpu.VMEM((height, columns), BF16),)
        name = "gram_pair" if d else "gram_own"
        clock.spend(3.2 if d else 3.0)
        return call(functools.partial(gram_kernel, d > 0, mask), name, (half, half), (where(d),), fields, scratch)

    def process(d, masks, extra=0, round_y=False):
        nonlocal mixed, mixes, level
        need = list(there) if extra else [d] if d else []
        while any(other not in pieces[-1] or there[other] > clock.now for other in need):
            yield clock.now + 0.5
        mine, value = order(*gram_chunk(d, masks[0], extra))
        terms = [mine]
        height = mine.shape[0] - extra

        def added(hop):
            clock.spend(0.8)
            final = hop == len(masks)
            count = height if final else height + extra
            outs = jax.ShapeDtypeStruct((count, columns), BF16)
            args = list(terms)
            if final and extra:
                outs = (outs, jax.ShapeDtypeStruct((8, 128), F32))
            elif final:
                args.append(level)
            kernel = functools.partial(
                sum_kernel, masks, hop, extra, columns * groups * rows_total, rows_total
            )
            return call(kernel, "sum_last" if final else "sum_hop", outs, (where(d),), args)

        for hop, mask in enumerate(masks):
            if hop:
                height //= 2
                value = added(hop)
            received, arrival = over_tiles(value, mask)
            yield arrival if hop or mask > 1 else arrival - (3.0 if d else 6.0)
            terms.append(order(received))
        while level is None and not extra:
            yield clock.now + 0.5
        part = added(len(masks))
        if extra:
            part, level = part
        for mask in masks[:0:-1]:
            received, arrival = over_tiles(part, mask)
            yield arrival
            part = jnp.concatenate([part, order(received)], axis=0)
            clock.spend(0.5)
        part = order(part)
        far, arrival = over_tiles(part, masks[0])
        if d:
            peer, peer_arrival = over_groups(part, d)
        if round_y:
            yield peer_arrival
            peer = order(peer)
            peer_far, peer_arrival = over_tiles(peer, masks[0])
        yield arrival
        far = order(far)
        parts = (part, far)
        if d:
            if not round_y:
                peer_far, arrival = over_groups(far, d)
                yield peer_arrival
                peer = order(peer)
                yield arrival
            else:
                yield peer_arrival
            peer_far = order(peer_far)
            parts += (peer, peer_far)
        first, last = mixes == 0, mixes == groups - 1
        mixes += 1
        shape = jax.ShapeDtypeStruct((rows, columns), BF16 if last else F32)
        scratch = (pltpu.VMEM((len(parts) * part.shape[0], columns), BF16),)
        args = (() if first else (mixed,)) + (*all_chunks(d), *parts)
        if last:
            args = (level, *args, *all_chunks(0))
        kernel = functools.partial(mix_kernel, d > 0, masks, first, last)
        name = "mix_pair" if d else "mix_own"
        clock.spend(3.2)
        mixed = call(kernel, name, shape, (where(d),), args, scratch, {} if first or last else {1: 0}, 28)
        if not last:
            mixed = order(mixed)

    y_first, z_then_y, y_then_far = (1, *z_masks), (*z_masks[:1], 1, *z_masks[1:]), (1, *z_masks[::-1])
    there[1] = 25.0
    queue = sorted(range(1, groups), key=lambda d: (d == 1, d))
    carrier = queue[min(1, len(queue) - 1)]
    processes = [panel_process()]
    for d in queue:
        first = d == queue[0] and d != carrier
        processes.append(process(d, z_then_y if first else y_first, EXTRA if d == carrier else 0, first))
    processes.append(process(0, y_then_far))
    clock.run(processes)
    return mixed


def solution(mesh):
    return jax.shard_map(
        local,
        mesh=mesh,
        in_specs=(P("elem", "orb"), P("elem", None, None, None), P("elem", None)),
        out_specs=P("elem", "orb"),
        check_vma=False,
    )
```

```python
import functools

import jax
import jax.numpy as jnp
from jax import lax
from jax.experimental import pallas as pl
from jax.experimental.pallas import tpu as pltpu
from jax.sharding import PartitionSpec as P

CHUNKS = 4
F32 = jnp.float32
BF16 = jnp.bfloat16
MIB = 1024 * 1024
EXTRA = 16


class Order:
    def __init__(self, token):
        self.token = token

    def __call__(self, *values):
        *values, self.token = lax.optimization_barrier((*values, self.token))
        return values[0] if len(values) == 1 else tuple(values)


class Schedule:
    RATE = 94e3
    CORE_RATE = 400e3
    DELAY = 2.5

    def __init__(self):
        self.now = 0.0
        self.free = {}

    def spend(self, time):
        self.now += time

    def transfer(self, value, link, weight=1.0):
        self.spend(1.3)
        size = value.size * value.dtype.itemsize
        time = weight * (size / self.CORE_RATE if link == "core" else 2 * size / self.RATE)
        begin = max(self.now, self.free.get(link, 0.0))
        self.free[link] = begin + time
        return begin + time + self.DELAY

    def run(self, processes):
        ready = [0.0] * len(processes)
        alive = list(range(len(processes)))
        while alive:
            can = [i for i in alive if ready[i] <= self.now]
            if not can:
                self.now = min(ready[i] for i in alive)
                continue
            try:
                ready[can[0]] = next(processes[can[0]])
            except StopIteration:
                alive.remove(can[0])


def product_kernel(stage, place_ref, blocks_ref, field_ref, near_ref, far_ref, *refs):
    elements, size, _ = blocks_ref.shape
    width = field_ref.shape[1]
    squares = jnp.zeros((8, width), F32)
    filler = jnp.zeros((size, width), BF16)
    for element in range(elements):
        picked = []
        for slot in range(7):
            source = field_ref if slot < 5 else near_ref if slot == 5 else far_ref
            first_row = pl.multiple_of(place_ref[element, slot] * size, size)
            picked.append(source[pl.ds(first_row, size), :])
        stacked = jnp.concatenate(picked + [filler], axis=0)
        total = jnp.dot(blocks_ref[element], stacked, preferred_element_type=F32)
        here = pl.ds(element * size, size)
        if stage == 0:
            wide_ref, half_ref = refs
            wide_ref[here, :] = total
            half_ref[here, :] = total.astype(BF16)
        elif stage == 1:
            before_ref, half_ref = refs
            half_ref[here, :] = (2.0 * total - before_ref[here, :].astype(F32)).astype(BF16)
        else:
            before_ref, earlier_ref, half_ref, *squares_ref = refs
            value = (2.0 * total - before_ref[here, :]).astype(BF16)
            half_ref[here, :] = value
            wide = value.astype(F32)
            squares += jnp.sum((wide * wide).reshape(-1, 8, width), axis=0)
    if stage == 2:
        squares = earlier_ref[...] + squares
        if squares_ref:
            squares_ref[0][...] = squares
        else:
            half_ref[elements * size :, :] = extra_rows(jnp.full((1, width), jnp.sum(squares)))


def call(kernel, name, outs, scalars, args, scratch=(), aliases=None, vmem=16, moved=1024):
    return pl.pallas_call(
        kernel,
        out_shape=outs,
        in_specs=[pl.BlockSpec(memory_space=pltpu.SMEM)] * len(scalars)
        + [pl.BlockSpec(memory_space=pltpu.VMEM)] * len(args),
        scratch_shapes=list(scratch),
        input_output_aliases=aliases or {},
        compiler_params=pltpu.CompilerParams(vmem_limit_bytes=vmem * MIB),
        cost_estimate=pl.CostEstimate(flops=1024, bytes_accessed=moved, transcendentals=0),
        name=name,
    )(*scalars, *args)


def product(stage, place, blocks, field, by_near, by_far, *before, last=False):
    rows, width = field.shape
    ended = jax.ShapeDtypeStruct((rows + EXTRA, width), BF16)
    half = jax.ShapeDtypeStruct((rows, width), BF16)
    wide = jax.ShapeDtypeStruct((rows, width), F32)
    squares = jax.ShapeDtypeStruct((8, width), F32)
    outs = ((wide, half), half, ended if last else (half, squares))[stage]
    args = (blocks, field, by_near, by_far, *before)
    kernel = functools.partial(product_kernel, stage)
    return call(kernel, f"product_{stage}", outs, (place,), args)


def put_in_place(where_ref, masks, mine_ref, far_ref, out_ref, base):
    bits = len(masks)
    height = mine_ref.shape[0] >> (bits - 1)
    for side, ref in ((0, mine_ref), (1, far_ref)):
        for position in range(1 << (bits - 1)):
            distance = side << (bits - 1) | position
            number = 0
            for i, mask in enumerate(masks):
                apart = distance >> (bits - 1 - i) & 1
                number = 2 * number + lax.rem(where_ref[0] // mask + apart, 2)
            here = pl.ds(pl.multiple_of(base + number * height, height), height)
            out_ref[here, :] = ref[position * height : (position + 1) * height, :]


TRANSPOSED_LEFT = (((0,), (0,)), ((), ()))
TRANSPOSED_RIGHT = (((1,), (1,)), ((), ()))


def extra_rows(value):
    first = lax.reduce_precision(value, 8, 7)
    second = lax.reduce_precision(value - first, 8, 7)
    third = value - first - second
    row = lax.broadcasted_iota(jnp.int32, (EXTRA, value.shape[1]), 0)
    rows = jnp.where(row == 0, first, jnp.where(row == 1, second, jnp.where(row == 2, third, 0.0)))
    return rows.astype(BF16)


def side_by_side(refs, rows):
    return jnp.concatenate([ref[:rows, :] for ref in refs], axis=1)


def gram_kernel(pair, mask, where_ref, *refs):
    mine_ref, other_ref, whole = refs[-3:]
    fields = refs[:CHUNKS]
    rows, width = fields[0].shape
    half = whole.shape[0] // 2
    middle = CHUNKS * width // 2
    side = lax.rem(where_ref[0] // mask, 2)

    def fill(left, rights, count):
        for c, right in enumerate(rights):
            value = lax.dot_general(left, right[:rows, :], TRANSPOSED_LEFT, preferred_element_type=F32)
            whole[:count, c * width : (c + 1) * width] = value.astype(BF16)

    if pair:
        peers = refs[CHUNKS : 2 * CHUNKS]
        used = middle

        @pl.when(where_ref[1] == 0)
        def _():
            fill(side_by_side(peers[: CHUNKS // 2], rows), fields, middle)

        @pl.when(where_ref[1] == 1)
        def _():
            fill(side_by_side(fields[CHUNKS // 2 :], rows), peers, middle)
    else:
        used = middle + middle // 2
        upper = side_by_side(fields[CHUNKS // 2 :], rows)
        fill(side_by_side(fields[: CHUNKS // 2], rows), fields, middle)
        corner = lax.dot_general(upper, upper, TRANSPOSED_LEFT, preferred_element_type=F32).astype(BF16)
        whole[middle:used, :middle] = corner[: middle // 2]
        whole[middle:used, middle:] = corner[middle // 2 :]
    if used < whole.shape[0]:
        whole[used:, :] = jnp.zeros((whole.shape[0] - used, whole.shape[1]), BF16)
    mine_ref[:half, :] = whole[pl.ds(pl.multiple_of(side * half, half), half), :]
    other_ref[:half, :] = whole[pl.ds(pl.multiple_of((1 - side) * half, half), half), :]
    if mine_ref.shape[0] > half:
        ends = [fields[-1], *refs[2 * CHUNKS - 1 : -3]]
        total = sum(jnp.sum(end[rows:, :].astype(F32), axis=0, keepdims=True) for end in ends)
        carried = extra_rows(jnp.concatenate([total] * CHUNKS, axis=1))
        mine_ref[half:, :] = carried
        other_ref[half:, :] = carried


def sum_kernel(masks, hop, extra, entries, rows_total, where_ref, *refs):
    terms, outs = refs[: hop + 1], refs[hop + 1 :]
    height = terms[0].shape[0] - extra
    begins, offset = [0, 0], 0
    final = hop == len(masks)
    for i, mask in enumerate(masks[1 : hop + 1], 1):
        height //= 2
        keep = lax.rem(where_ref[0] // mask, 2)
        first_row = offset + (1 - keep) * height
        offset = offset + keep * height
        begins.append(offset)
    if final:
        first_row = offset
    step = terms[-1].shape[0] - extra if final else height
    value = 0.0
    for term, begin in zip(terms, begins):
        here = pl.ds(pl.multiple_of(first_row - begin, EXTRA), step)
        value = value + term[here, :].astype(F32)
    total = None
    if extra:
        total = sum(jnp.sum(term[-extra:, :].astype(F32), axis=0, keepdims=True) for term in terms)
    if not final:
        outs[0][:step, :] = value.astype(BF16)
        if extra:
            outs[0][step:, :] = extra_rows(total)
        return
    if extra:
        level = total / entries
        outs[1][...] = jnp.broadcast_to(level[:, :1], outs[1].shape)
    else:
        level_ref, *outs = outs
        level = level_ref[:1, :1]
    outs[0][...] = (value / (level * rows_total)).astype(BF16)


def mix_kernel(pair, masks, first, last, where_ref, *refs):
    level_ref, *refs = refs if last else (None, *refs)
    total_ref, *refs = (None, *refs) if first else refs
    fields, refs = refs[:CHUNKS], refs[CHUNKS:]
    out_ref, block = refs[-2:]
    own = refs[-2 - CHUNKS : -2]
    rows, width = fields[0].shape
    middle = CHUNKS * width // 2

    def finish(mixed, here):
        value = mixed if first else total_ref[:, here] + mixed
        if last:
            filtered = side_by_side(own, rows)[:, here].astype(F32)
            value = (1.5 * filtered - 0.5 * value) / jnp.sqrt(level_ref[:1, :1])
        out_ref[:, here] = value.astype(out_ref.dtype)

    def times(left, right):
        return jnp.dot(left, right, preferred_element_type=F32)

    def times_transposed(left, right):
        return lax.dot_general(left, right, TRANSPOSED_RIGHT, preferred_element_type=F32)

    if not pair:
        put_in_place(where_ref, masks, refs[0], refs[1], block, 0)
        lower, upper = side_by_side(fields[: CHUNKS // 2], rows), side_by_side(fields[CHUNKS // 2 :], rows)
        corner = block[middle : middle + middle // 2, :]
        corner = jnp.concatenate([corner[:, :middle], corner[:, middle:]], axis=0)
        finish(
            times(lower, block[:middle, :middle]) + times_transposed(upper, block[:middle, middle:]),
            slice(0, middle),
        )
        finish(times(lower, block[:middle, middle:]) + times(upper, corner), slice(middle, 2 * middle))
        return
    height = block.shape[0] // 2
    is_upper = where_ref[1]
    put_in_place(where_ref, masks, refs[0], refs[1], block, is_upper * height)
    put_in_place(where_ref, masks, refs[2], refs[3], block, (1 - is_upper) * height)

    @pl.when(is_upper == 0)
    def _():
        field = side_by_side(fields, rows)
        for c in range(CHUNKS):
            here = slice(c * width, (c + 1) * width)
            finish(times(field, jnp.concatenate([block[:middle, here], block[height : height + middle, here]])), here)

    @pl.when(is_upper == 1)
    def _():
        field = side_by_side(fields, rows)
        for c in range(CHUNKS):
            row = c * width if c * width < middle else height + c * width - middle
            finish(times_transposed(field, block[row : row + width, :]), slice(c * width, (c + 1) * width))


def local(orbitals, hamiltonian, neighbours):
    elements, slots, size, _ = hamiltonian.shape
    rows, columns = orbitals.shape
    tiles = lax.axis_size("elem")
    groups = lax.axis_size("orb")
    lines = tiles // 2
    my_tile = lax.axis_index("elem")
    my_group = lax.axis_index("orb")
    odd = my_tile % 2
    line = my_tile // 2

    swap = [(i, i ^ 1) for i in range(tiles)]
    outward = [(2 * i + side, 2 * ((i + 1 - 2 * side) % lines) + side) for i in range(lines) for side in (0, 1)]

    def to_group(value, d):
        return lax.ppermute(value, "orb", [(i, i ^ d) for i in range(groups)])

    place = neighbours % elements
    last_two = place[:, 5:]
    place = jnp.concatenate([place[:, :5], jnp.where(odd == 0, last_two[:, ::-1], last_two)], axis=1)
    by_slot = [hamiltonian[:, s] for s in range(5)]
    by_slot.append(jnp.where(odd == 0, hamiltonian[:, 6], hamiltonian[:, 5]))
    by_slot.append(jnp.where(odd == 0, hamiltonian[:, 5], hamiltonian[:, 6]))
    by_slot.append(jnp.zeros_like(by_slot[0]))
    blocks = jnp.concatenate(by_slot, axis=2)

    width = columns // CHUNKS
    start = [lax.slice_in_dim(orbitals, c * width, (c + 1) * width, axis=1) for c in range(CHUNKS)]
    near = {(0, 0): lax.ppermute(start[0], "elem", swap)}
    order = Order(jnp.zeros((8, 128), F32))
    blocks, place = order(blocks, place)
    start = [start[0]] + [order(field) for field in start[1:]]
    for c in range(1, CHUNKS):
        near[(0, c)] = lax.ppermute(start[c], "elem", swap)

    jobs = [(stage, c) for stage in range(3) for c in range(CHUNKS)]
    far = {}
    firsts, squares, pieces = {}, jnp.zeros((8, width), F32), [{} for _ in range(CHUNKS)]
    current = {(0, c): start[c] for c in range(CHUNKS)}

    def send_on(job):
        near[job] = order(near[job])
        far[job] = lax.ppermute(near[job], "elem", outward)

    def more_panel(c):
        for d in range(1, groups):
            if d & (d - 1):
                low = d & -d
                if d ^ low in pieces[c] and d not in pieces[c]:
                    pieces[c][d ^ low] = order(pieces[c][d ^ low])
                    pieces[c][d] = to_group(pieces[c][d ^ low], low)

    def settle(c, some=lambda d: True):
        for d in [d for d in pieces[c] if d and some(d)]:
            pieces[c][d] = order(pieces[c][d])

    def multiply(job):
        nonlocal squares
        stage, c = job
        far[job] = order(far[job])
        old = ((), (start[c],), (firsts.get(c), squares))[stage]
        last = stage == 2 and c == CHUNKS - 1
        out = product(stage, place, blocks, current[job], near[job], far[job], *old, last=last)
        if stage == 0:
            firsts[c], out = order(*out)
        elif stage == 1:
            out = order(out)
        else:
            if last:
                out = order(out)
            else:
                out, squares = order(*out)
            pieces[c][0] = out
            bit = groups // 2
            while bit:
                pieces[c][bit] = to_group(out, bit)
                bit //= 2
            if c:
                more_panel(c - 1)
                settle(c - 1, lambda d: not d & (d - 1))
            if c > 1:
                settle(c - 2)
            return
        current[(stage + 1, c)] = out
        near[(stage + 1, c)] = lax.ppermute(out, "elem", swap)

    for index, job in enumerate(jobs):
        send_on(job)
        if index:
            multiply(jobs[index - 1])
    multiply(jobs[-1])

    rows_total = rows * tiles
    level = None
    middle = columns // 2
    unit = 16 * tiles
    clock = Schedule()
    z_masks = [2 << i for i in range(lines.bit_length() - 1)]
    there = {d: 3.0 if d == 1 else 10.5 for d in range(1, groups)}
    mixed, mixes = None, 0

    def is_upper(d):
        return (my_group & (1 << (d.bit_length() - 1))) != 0

    def where(d):
        return jnp.stack([my_tile, is_upper(d) if d else odd]).astype(jnp.int32)

    def all_chunks(d):
        return [pieces[c][d] for c in range(CHUNKS)]

    def over_tiles(value, mask):
        sent = lax.ppermute(value, "elem", [(i, i ^ mask) for i in range(tiles)])
        if mask <= 2:
            return sent, clock.transfer(value, "y" if mask == 1 else "z")
        clock.spend(-1.3)
        return sent, max(clock.transfer(value, "z", mask / 4), clock.transfer(value, "middle", mask / 2))

    def over_groups(value, d):
        return to_group(value, d), clock.transfer(value, "core" if d == 1 else "x")

    def panel_process():
        yield 10.5
        more_panel(CHUNKS - 1)
        settle(CHUNKS - 1, lambda d: not d & (d - 1))
        settle(CHUNKS - 2)
        clock.spend(1.3)
        for d in range(1, groups):
            if d & (d - 1):
                there[d] = clock.now + 3.5

    def gram_chunk(d, mask, extra):
        height = middle if d else middle + middle // 2
        height += -height % unit
        fields = all_chunks(0)
        if d:
            fields += list(order(*all_chunks(d)))
        if extra:
            fields += [pieces[-1][other] for other in range(1, groups) if other != d]
        half = jax.ShapeDtypeStruct((height // 2 + extra, columns), BF16)
        scratch = (pltpu.VMEM((height, columns), BF16),)
        name = "gram_pair" if d else "gram_own"
        clock.spend(3.2 if d else 3.0)
        return call(
            functools.partial(gram_kernel, d > 0, mask), name, (half, half), (where(d),), fields, scratch, moved=5 * MIB
        )

    def process(d, masks, extra=0, round_y=False):
        nonlocal mixed, mixes, level
        need = list(there) if extra else [d] if d else []
        while any(other not in pieces[-1] or there[other] > clock.now for other in need):
            yield clock.now + 0.5
        mine, value = order(*gram_chunk(d, masks[0], extra))
        terms = [mine]
        height = mine.shape[0] - extra

        def added(hop):
            clock.spend(0.8)
            final = hop == len(masks)
            count = height if final else height + extra
            outs = jax.ShapeDtypeStruct((count, columns), BF16)
            args = list(terms)
            if final and extra:
                outs = (outs, jax.ShapeDtypeStruct((8, 128), F32))
            elif final:
                args.append(level)
            kernel = functools.partial(
                sum_kernel, masks, hop, extra, columns * groups * rows_total, rows_total
            )
            return call(kernel, "sum_last" if final else "sum_hop", outs, (where(d),), args)

        for hop, mask in enumerate(masks):
            if hop:
                height //= 2
                value = order(added(hop))
            received, arrival = over_tiles(value, mask)
            yield arrival if hop or mask > 1 else arrival - (3.0 if d else 6.0)
            terms.append(order(received))
        while level is None and not extra:
            yield clock.now + 0.5
        part = added(len(masks))
        if extra:
            part, level = order(*part)
        else:
            part = order(part)
        for mask in masks[:0:-1]:
            received, arrival = over_tiles(part, mask)
            yield arrival
            part = order(jnp.concatenate([part, order(received)], axis=0))
            clock.spend(0.5)
        far, arrival = over_tiles(part, masks[0])
        if d:
            peer, peer_arrival = over_groups(part, d)
        if round_y:
            yield peer_arrival
            peer = order(peer)
            peer_far, peer_arrival = over_tiles(peer, masks[0])
        elif d:
            yield peer_arrival - 3.0
            peer = order(peer)
        yield arrival
        far = order(far)
        parts = (part, far)
        if d:
            if not round_y:
                peer_far, peer_arrival = over_groups(far, d)
            yield peer_arrival
            peer_far = order(peer_far)
            parts += (peer, peer_far)
        first, last = mixes == 0, mixes == groups - 1
        mixes += 1
        shape = jax.ShapeDtypeStruct((rows, columns), BF16 if last else F32)
        scratch = (pltpu.VMEM((len(parts) * part.shape[0], columns), BF16),)
        args = (() if first else (mixed,)) + (*all_chunks(d), *parts)
        if last:
            args = (level, *args, *all_chunks(0))
        kernel = functools.partial(mix_kernel, d > 0, masks, first, last)
        name = "mix_pair" if d else "mix_own"
        clock.spend(3.2)
        mixed = call(kernel, name, shape, (where(d),), args, scratch, {} if first or last else {1: 0}, 28, 5 * MIB)
        if not last:
            mixed = order(mixed)

    y_first, z_then_y, y_then_far = (1, *z_masks), (*z_masks[:1], 1, *z_masks[1:]), (1, *z_masks[::-1])
    there[1] = 25.0
    queue = sorted(range(1, groups), key=lambda d: (d == 1, d))
    carrier = queue[min(1, len(queue) - 1)]
    processes = [panel_process()]
    for d in queue:
        first = d == queue[0] and d != carrier
        processes.append(process(d, z_then_y if first else y_first, EXTRA if d == carrier else 0, first))
    processes.append(process(0, y_then_far))
    clock.run(processes)
    return mixed


def solution(mesh):
    return jax.shard_map(
        local,
        mesh=mesh,
        in_specs=(P("elem", "orb"), P("elem", None, None, None), P("elem", None)),
        out_specs=P("elem", "orb"),
        check_vma=False,
    )
```

```python
import functools

import jax
import jax.numpy as jnp
from jax import lax
from jax.experimental import pallas as pl
from jax.experimental.pallas import tpu as pltpu
from jax.sharding import PartitionSpec as P

CHUNKS = 4
F32 = jnp.float32
BF16 = jnp.bfloat16
MIB = 1024 * 1024
EXTRA = 16


class Order:
    def __init__(self, token):
        self.token = token

    def __call__(self, *values):
        *values, self.token = lax.optimization_barrier((*values, self.token))
        return values[0] if len(values) == 1 else tuple(values)


class Schedule:
    RATE = 94e3
    CORE_RATE = 400e3
    DELAY = 2.5

    def __init__(self):
        self.now = 0.0
        self.free = {}

    def spend(self, time):
        self.now += time

    def transfer(self, value, link, weight=1.0):
        self.spend(1.3)
        size = value.size * value.dtype.itemsize
        time = weight * (size / self.CORE_RATE if link == "core" else 2 * size / self.RATE)
        begin = max(self.now, self.free.get(link, 0.0))
        self.free[link] = begin + time
        return begin + time + self.DELAY

    def run(self, processes):
        ready = [0.0] * len(processes)
        alive = list(range(len(processes)))
        while alive:
            can = [i for i in alive if ready[i] <= self.now]
            if not can:
                self.now = min(ready[i] for i in alive)
                continue
            try:
                ready[can[0]] = next(processes[can[0]])
            except StopIteration:
                alive.remove(can[0])


def product_kernel(stage, place_ref, blocks_ref, field_ref, near_ref, far_ref, *refs):
    elements, size, _ = blocks_ref.shape
    width = field_ref.shape[1]
    squares = jnp.zeros((8, width), F32)
    filler = jnp.zeros((size, width), BF16)
    for element in range(elements):
        picked = []
        for slot in range(7):
            source = field_ref if slot < 5 else near_ref if slot == 5 else far_ref
            first_row = pl.multiple_of(place_ref[element, slot] * size, size)
            picked.append(source[pl.ds(first_row, size), :])
        stacked = jnp.concatenate(picked + [filler], axis=0)
        total = jnp.dot(blocks_ref[element], stacked, preferred_element_type=F32)
        here = pl.ds(element * size, size)
        if stage == 0:
            wide_ref, half_ref = refs
            wide_ref[here, :] = total
            half_ref[here, :] = total.astype(BF16)
        elif stage == 1:
            before_ref, half_ref = refs
            half_ref[here, :] = (2.0 * total - before_ref[here, :].astype(F32)).astype(BF16)
        else:
            before_ref, earlier_ref, half_ref, *squares_ref = refs
            value = (2.0 * total - before_ref[here, :]).astype(BF16)
            half_ref[here, :] = value
            wide = value.astype(F32)
            squares += jnp.sum((wide * wide).reshape(-1, 8, width), axis=0)
    if stage == 2:
        squares = earlier_ref[...] + squares
        if squares_ref:
            squares_ref[0][...] = squares
        else:
            half_ref[elements * size :, :] = extra_rows(jnp.full((1, width), jnp.sum(squares)))


def call(kernel, name, outs, scalars, args, scratch=(), aliases=None, vmem=16, moved=1024):
    return pl.pallas_call(
        kernel,
        out_shape=outs,
        in_specs=[pl.BlockSpec(memory_space=pltpu.SMEM)] * len(scalars)
        + [pl.BlockSpec(memory_space=pltpu.VMEM)] * len(args),
        scratch_shapes=list(scratch),
        input_output_aliases=aliases or {},
        compiler_params=pltpu.CompilerParams(vmem_limit_bytes=vmem * MIB),
        cost_estimate=pl.CostEstimate(flops=1024, bytes_accessed=moved, transcendentals=0),
        name=name,
    )(*scalars, *args)


def product(stage, place, blocks, field, by_near, by_far, *before, last=False):
    rows, width = field.shape
    ended = jax.ShapeDtypeStruct((rows + EXTRA, width), BF16)
    half = jax.ShapeDtypeStruct((rows, width), BF16)
    wide = jax.ShapeDtypeStruct((rows, width), F32)
    squares = jax.ShapeDtypeStruct((8, width), F32)
    outs = ((wide, half), half, ended if last else (half, squares))[stage]
    args = (blocks, field, by_near, by_far, *before)
    kernel = functools.partial(product_kernel, stage)
    return call(kernel, f"product_{stage}", outs, (place,), args)


def put_in_place(where_ref, masks, mine_ref, far_ref, out_ref, base):
    bits = len(masks)
    height = mine_ref.shape[0] >> (bits - 1)
    for side, ref in ((0, mine_ref), (1, far_ref)):
        for position in range(1 << (bits - 1)):
            distance = side << (bits - 1) | position
            number = 0
            for i, mask in enumerate(masks):
                apart = distance >> (bits - 1 - i) & 1
                number = 2 * number + lax.rem(where_ref[0] // mask + apart, 2)
            here = pl.ds(pl.multiple_of(base + number * height, height), height)
            out_ref[here, :] = ref[position * height : (position + 1) * height, :]


TRANSPOSED_LEFT = (((0,), (0,)), ((), ()))
TRANSPOSED_RIGHT = (((1,), (1,)), ((), ()))


def extra_rows(value):
    first = lax.reduce_precision(value, 8, 7)
    second = lax.reduce_precision(value - first, 8, 7)
    third = value - first - second
    row = lax.broadcasted_iota(jnp.int32, (EXTRA, value.shape[1]), 0)
    rows = jnp.where(row == 0, first, jnp.where(row == 1, second, jnp.where(row == 2, third, 0.0)))
    return rows.astype(BF16)


def side_by_side(refs, rows):
    return jnp.concatenate([ref[:rows, :] for ref in refs], axis=1)


def gram_kernel(pair, mask, where_ref, *refs):
    mine_ref, other_ref, whole = refs[-3:]
    fields = refs[:CHUNKS]
    rows, width = fields[0].shape
    half = whole.shape[0] // 2
    middle = CHUNKS * width // 2
    side = lax.rem(where_ref[0] // mask, 2)

    def fill(left, rights, count):
        for c, right in enumerate(rights):
            value = lax.dot_general(left, right[:rows, :], TRANSPOSED_LEFT, preferred_element_type=F32)
            whole[:count, c * width : (c + 1) * width] = value.astype(BF16)

    if pair:
        peers = refs[CHUNKS : 2 * CHUNKS]
        used = middle

        @pl.when(where_ref[1] == 0)
        def _():
            fill(side_by_side(peers[: CHUNKS // 2], rows), fields, middle)

        @pl.when(where_ref[1] == 1)
        def _():
            fill(side_by_side(fields[CHUNKS // 2 :], rows), peers, middle)
    else:
        used = middle + middle // 2
        upper = side_by_side(fields[CHUNKS // 2 :], rows)
        fill(side_by_side(fields[: CHUNKS // 2], rows), fields, middle)
        corner = lax.dot_general(upper, upper, TRANSPOSED_LEFT, preferred_element_type=F32).astype(BF16)
        whole[middle:used, :middle] = corner[: middle // 2]
        whole[middle:used, middle:] = corner[middle // 2 :]
    if used < whole.shape[0]:
        whole[used:, :] = jnp.zeros((whole.shape[0] - used, whole.shape[1]), BF16)
    mine_ref[:half, :] = whole[pl.ds(pl.multiple_of(side * half, half), half), :]
    other_ref[:half, :] = whole[pl.ds(pl.multiple_of((1 - side) * half, half), half), :]
    if mine_ref.shape[0] > half:
        ends = [fields[-1], *refs[2 * CHUNKS - 1 : -3]]
        total = sum(jnp.sum(end[rows:, :].astype(F32), axis=0, keepdims=True) for end in ends)
        carried = extra_rows(jnp.concatenate([total] * CHUNKS, axis=1))
        mine_ref[half:, :] = carried
        other_ref[half:, :] = carried


def sum_kernel(masks, hop, extra, entries, rows_total, where_ref, *refs):
    terms, outs = refs[: hop + 1], refs[hop + 1 :]
    height = terms[0].shape[0] - extra
    begins, offset = [0, 0], 0
    final = hop == len(masks)
    for i, mask in enumerate(masks[1 : hop + 1], 1):
        height //= 2
        keep = lax.rem(where_ref[0] // mask, 2)
        first_row = offset + (1 - keep) * height
        offset = offset + keep * height
        begins.append(offset)
    if final:
        first_row = offset
    step = terms[-1].shape[0] - extra if final else height
    value = 0.0
    for term, begin in zip(terms, begins):
        here = pl.ds(pl.multiple_of(first_row - begin, EXTRA), step)
        value = value + term[here, :].astype(F32)
    total = None
    if extra:
        total = sum(jnp.sum(term[-extra:, :].astype(F32), axis=0, keepdims=True) for term in terms)
    if not final:
        outs[0][:step, :] = value.astype(BF16)
        if extra:
            outs[0][step:, :] = extra_rows(total)
        return
    if extra:
        level = total / entries
        outs[1][...] = jnp.broadcast_to(level[:, :1], outs[1].shape)
    else:
        level_ref, *outs = outs
        level = level_ref[:1, :1]
    outs[0][...] = (value / (level * rows_total)).astype(BF16)


def mix_kernel(pair, masks, first, last, where_ref, *refs):
    level_ref, *refs = refs if last else (None, *refs)
    total_ref, *refs = (None, *refs) if first else refs
    fields, refs = refs[:CHUNKS], refs[CHUNKS:]
    out_ref, block = refs[-2:]
    own = refs[-2 - CHUNKS : -2]
    rows, width = fields[0].shape
    middle = CHUNKS * width // 2

    def finish(mixed, here):
        value = mixed if first else total_ref[:, here] + mixed
        if last:
            filtered = side_by_side(own, rows)[:, here].astype(F32)
            value = (1.5 * filtered - 0.5 * value) / jnp.sqrt(level_ref[:1, :1])
        out_ref[:, here] = value.astype(out_ref.dtype)

    def times(left, right):
        return jnp.dot(left, right, preferred_element_type=F32)

    def times_transposed(left, right):
        return lax.dot_general(left, right, TRANSPOSED_RIGHT, preferred_element_type=F32)

    if not pair:
        put_in_place(where_ref, masks, refs[0], refs[1], block, 0)
        lower, upper = side_by_side(fields[: CHUNKS // 2], rows), side_by_side(fields[CHUNKS // 2 :], rows)
        corner = block[middle : middle + middle // 2, :]
        corner = jnp.concatenate([corner[:, :middle], corner[:, middle:]], axis=0)
        finish(
            times(lower, block[:middle, :middle]) + times_transposed(upper, block[:middle, middle:]),
            slice(0, middle),
        )
        finish(times(lower, block[:middle, middle:]) + times(upper, corner), slice(middle, 2 * middle))
        return
    height = block.shape[0] // 2
    is_upper = where_ref[1]
    put_in_place(where_ref, masks, refs[0], refs[1], block, is_upper * height)
    put_in_place(where_ref, masks, refs[2], refs[3], block, (1 - is_upper) * height)

    @pl.when(is_upper == 0)
    def _():
        field = side_by_side(fields, rows)
        for c in range(CHUNKS):
            here = slice(c * width, (c + 1) * width)
            finish(times(field, jnp.concatenate([block[:middle, here], block[height : height + middle, here]])), here)

    @pl.when(is_upper == 1)
    def _():
        field = side_by_side(fields, rows)
        for c in range(CHUNKS):
            row = c * width if c * width < middle else height + c * width - middle
            finish(times_transposed(field, block[row : row + width, :]), slice(c * width, (c + 1) * width))


def local(orbitals, hamiltonian, neighbours):
    elements, slots, size, _ = hamiltonian.shape
    rows, columns = orbitals.shape
    tiles = lax.axis_size("elem")
    groups = lax.axis_size("orb")
    lines = tiles // 2
    my_tile = lax.axis_index("elem")
    my_group = lax.axis_index("orb")
    odd = my_tile % 2
    line = my_tile // 2

    swap = [(i, i ^ 1) for i in range(tiles)]
    outward = [(2 * i + side, 2 * ((i + 1 - 2 * side) % lines) + side) for i in range(lines) for side in (0, 1)]

    def to_group(value, d):
        return lax.ppermute(value, "orb", [(i, i ^ d) for i in range(groups)])

    place = neighbours % elements
    last_two = place[:, 5:]
    place = jnp.concatenate([place[:, :5], jnp.where(odd == 0, last_two[:, ::-1], last_two)], axis=1)
    by_slot = [hamiltonian[:, s] for s in range(5)]
    by_slot.append(jnp.where(odd == 0, hamiltonian[:, 6], hamiltonian[:, 5]))
    by_slot.append(jnp.where(odd == 0, hamiltonian[:, 5], hamiltonian[:, 6]))
    by_slot.append(jnp.zeros_like(by_slot[0]))
    blocks = jnp.concatenate(by_slot, axis=2)

    width = columns // CHUNKS
    start = [lax.slice_in_dim(orbitals, c * width, (c + 1) * width, axis=1) for c in range(CHUNKS)]
    near = {(0, 0): lax.ppermute(start[0], "elem", swap)}
    order = Order(jnp.zeros((8, 128), F32))
    blocks, place = order(blocks, place)
    start = [start[0]] + [order(field) for field in start[1:]]
    for c in range(1, CHUNKS):
        near[(0, c)] = lax.ppermute(start[c], "elem", swap)

    jobs = [(stage, c) for stage in range(3) for c in range(CHUNKS)]
    far = {}
    firsts, squares, pieces = {}, jnp.zeros((8, width), F32), [{} for _ in range(CHUNKS)]
    current = {(0, c): start[c] for c in range(CHUNKS)}

    def send_on(job):
        near[job] = order(near[job])
        far[job] = lax.ppermute(near[job], "elem", outward)

    def more_panel(c):
        for d in range(1, groups):
            if d & (d - 1):
                low = d & -d
                if d ^ low in pieces[c] and d not in pieces[c]:
                    pieces[c][d ^ low] = order(pieces[c][d ^ low])
                    pieces[c][d] = to_group(pieces[c][d ^ low], low)

    def settle(c, some=lambda d: True):
        for d in [d for d in pieces[c] if d and some(d)]:
            pieces[c][d] = order(pieces[c][d])

    def multiply(job):
        nonlocal squares
        stage, c = job
        far[job] = order(far[job])
        old = ((), (start[c],), (firsts.get(c), squares))[stage]
        last = stage == 2 and c == CHUNKS - 1
        out = product(stage, place, blocks, current[job], near[job], far[job], *old, last=last)
        if stage == 0:
            firsts[c], out = order(*out)
        elif stage == 1:
            out = order(out)
        else:
            if last:
                out = order(out)
            else:
                out, squares = order(*out)
            pieces[c][0] = out
            bit = groups // 2
            while bit:
                pieces[c][bit] = to_group(out, bit)
                bit //= 2
            if c > 1:
                more_panel(c - 2)
                settle(c - 2, lambda d: not d & (d - 1))
            return
        current[(stage + 1, c)] = out
        near[(stage + 1, c)] = lax.ppermute(out, "elem", swap)

    for index, job in enumerate(jobs):
        send_on(job)
        if index:
            multiply(jobs[index - 1])
    multiply(jobs[-1])

    rows_total = rows * tiles
    level = None
    middle = columns // 2
    unit = 16 * tiles
    clock = Schedule()
    z_masks = [2 << i for i in range(lines.bit_length() - 1)]
    there = {d: 3.0 if d == 1 else 10.5 for d in range(1, groups)}
    mixed, mixes = None, 0

    def is_upper(d):
        return (my_group & (1 << (d.bit_length() - 1))) != 0

    def where(d):
        return jnp.stack([my_tile, is_upper(d) if d else odd]).astype(jnp.int32)

    def all_chunks(d):
        return [pieces[c][d] for c in range(CHUNKS)]

    def over_tiles(value, mask):
        sent = lax.ppermute(value, "elem", [(i, i ^ mask) for i in range(tiles)])
        if mask <= 2:
            return sent, clock.transfer(value, "y" if mask == 1 else "z")
        clock.spend(-1.3)
        return sent, max(clock.transfer(value, "z", mask / 4), clock.transfer(value, "middle", mask / 2))

    def over_groups(value, d):
        return to_group(value, d), clock.transfer(value, "core" if d == 1 else "x")

    def panel_process():
        yield 4.0
        for c in range(CHUNKS - 1):
            more_panel(c)
            settle(c)
        yield 10.5
        more_panel(CHUNKS - 1)
        settle(CHUNKS - 1, lambda d: not d & (d - 1))
        clock.spend(1.3)
        for d in range(1, groups):
            if d & (d - 1):
                there[d] = clock.now + 3.5

    def gram_chunk(d, mask, extra):
        height = middle if d else middle + middle // 2
        height += -height % unit
        fields = all_chunks(0)
        if d:
            fields += list(order(*all_chunks(d)))
        if extra:
            fields += [pieces[-1][other] for other in range(1, groups) if other != d]
        half = jax.ShapeDtypeStruct((height // 2 + extra, columns), BF16)
        scratch = (pltpu.VMEM((height, columns), BF16),)
        name = "gram_pair" if d else "gram_own"
        clock.spend(3.2 if d else 3.0)
        return call(
            functools.partial(gram_kernel, d > 0, mask), name, (half, half), (where(d),), fields, scratch, moved=5 * MIB
        )

    sent = [None]

    def process(d, masks, extra=0, round_y=False, behind=None):
        nonlocal mixed, mixes, level
        need = list(there) if extra else [d] if d else []
        while any(other not in pieces[-1] or there[other] > clock.now for other in need):
            yield clock.now + 0.5
        mine, value = order(*gram_chunk(d, masks[0], extra))
        terms = [mine]
        height = mine.shape[0] - extra

        def added(hop):
            clock.spend(0.8)
            final = hop == len(masks)
            count = height if final else height + extra
            outs = jax.ShapeDtypeStruct((count, columns), BF16)
            args = list(terms)
            if final and extra:
                outs = (outs, jax.ShapeDtypeStruct((8, 128), F32))
            elif final:
                args.append(level)
            kernel = functools.partial(
                sum_kernel, masks, hop, extra, columns * groups * rows_total, rows_total
            )
            return call(kernel, "sum_last" if final else "sum_hop", outs, (where(d),), args)

        for hop, mask in enumerate(masks):
            if hop:
                height //= 2
                value = order(added(hop))
            received, arrival = over_tiles(value, mask)
            yield arrival if hop or mask > 1 else arrival - (3.0 if d else 6.0)
            terms.append(order(received))
        while level is None and not extra:
            yield clock.now + 0.5
        part = added(len(masks))
        if extra:
            part, level = order(*part)
        else:
            part = order(part)
        for mask in masks[:0:-1]:
            received, arrival = over_tiles(part, mask)
            yield arrival
            part = order(jnp.concatenate([part, order(received)], axis=0))
            clock.spend(0.5)
        while behind not in sent:
            yield clock.now + 0.5
        part = order(part)
        far, arrival = over_tiles(part, masks[0])
        sent.append(d)
        if d:
            peer, peer_arrival = over_groups(part, d)
        if round_y:
            clock.now = max(clock.now, arrival)
            far = order(far)
            yield peer_arrival
            peer = order(peer)
            peer_far, peer_arrival = over_tiles(peer, masks[0])
        elif d:
            yield peer_arrival - 3.0
            peer = order(peer)
            yield arrival
            far = order(far)
        else:
            yield arrival
            far = order(far)
        parts = (part, far)
        if d:
            if not round_y:
                peer_far, peer_arrival = over_groups(far, d)
            yield peer_arrival
            peer_far = order(peer_far)
            parts += (peer, peer_far)
        first, last = mixes == 0, mixes == groups - 1
        mixes += 1
        shape = jax.ShapeDtypeStruct((rows, columns), BF16 if last else F32)
        scratch = (pltpu.VMEM((len(parts) * part.shape[0], columns), BF16),)
        args = (() if first else (mixed,)) + (*all_chunks(d), *parts)
        if last:
            args = (level, *args, *all_chunks(0))
        kernel = functools.partial(mix_kernel, d > 0, masks, first, last)
        name = "mix_pair" if d else "mix_own"
        clock.spend(3.2)
        mixed = call(kernel, name, shape, (where(d),), args, scratch, {} if first or last else {1: 0}, 28, 5 * MIB)
        if not last:
            mixed = order(mixed)

    y_first, z_then_y, y_then_far = (1, *z_masks), (*z_masks[:1], 1, *z_masks[1:]), (1, *z_masks[::-1])
    there[1] = 25.0
    queue = sorted(range(1, groups), key=lambda d: (d == 1, d))
    carrier = queue[min(1, len(queue) - 1)]
    processes = [panel_process()]
    for d in queue:
        first = d == queue[0] and d != carrier
        behind = carrier if d == 1 and d != carrier else None
        processes.append(process(d, z_then_y if first else y_first, EXTRA if d == carrier else 0, first, behind))
    processes.append(process(0, y_then_far, behind=1))
    clock.run(processes)
    return mixed


def solution(mesh):
    return jax.shard_map(
        local,
        mesh=mesh,
        in_specs=(P("elem", "orb"), P("elem", None, None, None), P("elem", None)),
        out_specs=P("elem", "orb"),
        check_vma=False,
    )
```

```python
import functools

import jax
import jax.numpy as jnp
from jax import lax
from jax.experimental import pallas as pl
from jax.experimental.pallas import tpu as pltpu
from jax.sharding import PartitionSpec as P

CHUNKS = 4
F32 = jnp.float32
BF16 = jnp.bfloat16
MIB = 1024 * 1024
EXTRA = 16


class Order:
    def __init__(self, token):
        self.token = token

    def __call__(self, *values):
        *values, self.token = lax.optimization_barrier((*values, self.token))
        return values[0] if len(values) == 1 else tuple(values)


class Schedule:
    RATE = 94e3
    CORE_RATE = 400e3
    DELAY = 2.5

    def __init__(self):
        self.now = 0.0
        self.free = {}

    def spend(self, time):
        self.now += time

    def transfer(self, value, link, weight=1.0):
        self.spend(1.3)
        size = value.size * value.dtype.itemsize
        time = weight * (size / self.CORE_RATE if link == "core" else 2 * size / self.RATE)
        begin = max(self.now, self.free.get(link, 0.0))
        self.free[link] = begin + time
        return begin + time + self.DELAY

    def run(self, processes):
        ready = [0.0] * len(processes)
        alive = list(range(len(processes)))
        while alive:
            can = [i for i in alive if ready[i] <= self.now]
            if not can:
                self.now = min(ready[i] for i in alive)
                continue
            try:
                ready[can[0]] = next(processes[can[0]])
            except StopIteration:
                alive.remove(can[0])


def product_kernel(stage, place_ref, blocks_ref, field_ref, near_ref, far_ref, *refs):
    elements, size, _ = blocks_ref.shape
    width = field_ref.shape[1]
    squares = jnp.zeros((8, width), F32)
    filler = jnp.zeros((size, width), BF16)
    for element in range(elements):
        picked = []
        for slot in range(7):
            source = field_ref if slot < 5 else near_ref if slot == 5 else far_ref
            first_row = pl.multiple_of(place_ref[element, slot] * size, size)
            picked.append(source[pl.ds(first_row, size), :])
        stacked = jnp.concatenate(picked + [filler], axis=0)
        total = jnp.dot(blocks_ref[element], stacked, preferred_element_type=F32)
        here = pl.ds(element * size, size)
        if stage == 0:
            wide_ref, half_ref = refs
            wide_ref[here, :] = total
            half_ref[here, :] = total.astype(BF16)
        elif stage == 1:
            before_ref, half_ref = refs
            half_ref[here, :] = (2.0 * total - before_ref[here, :].astype(F32)).astype(BF16)
        else:
            before_ref, earlier_ref, half_ref, *squares_ref = refs
            value = (2.0 * total - before_ref[here, :]).astype(BF16)
            half_ref[here, :] = value
            wide = value.astype(F32)
            squares += jnp.sum((wide * wide).reshape(-1, 8, width), axis=0)
    if stage == 2:
        squares = earlier_ref[...] + squares
        if squares_ref:
            squares_ref[0][...] = squares
        else:
            half_ref[elements * size :, :] = extra_rows(jnp.full((1, width), jnp.sum(squares)))


def call(kernel, name, outs, scalars, args, scratch=(), aliases=None, vmem=16, moved=1024):
    return pl.pallas_call(
        kernel,
        out_shape=outs,
        in_specs=[pl.BlockSpec(memory_space=pltpu.SMEM)] * len(scalars)
        + [pl.BlockSpec(memory_space=pltpu.VMEM)] * len(args),
        scratch_shapes=list(scratch),
        input_output_aliases=aliases or {},
        compiler_params=pltpu.CompilerParams(vmem_limit_bytes=vmem * MIB),
        cost_estimate=pl.CostEstimate(flops=1024, bytes_accessed=moved, transcendentals=0),
        name=name,
    )(*scalars, *args)


def product(stage, place, blocks, field, by_near, by_far, *before, last=False):
    rows, width = field.shape
    ended = jax.ShapeDtypeStruct((rows + EXTRA, width), BF16)
    half = jax.ShapeDtypeStruct((rows, width), BF16)
    wide = jax.ShapeDtypeStruct((rows, width), F32)
    squares = jax.ShapeDtypeStruct((8, width), F32)
    outs = ((wide, half), half, ended if last else (half, squares))[stage]
    args = (blocks, field, by_near, by_far, *before)
    kernel = functools.partial(product_kernel, stage)
    return call(kernel, f"product_{stage}", outs, (place,), args)


def put_in_place(where_ref, masks, mine_ref, far_ref, out_ref, base):
    bits = len(masks)
    height = mine_ref.shape[0] >> (bits - 1)
    for side, ref in ((0, mine_ref), (1, far_ref)):
        for position in range(1 << (bits - 1)):
            distance = side << (bits - 1) | position
            number = 0
            for i, mask in enumerate(masks):
                apart = distance >> (bits - 1 - i) & 1
                number = 2 * number + lax.rem(where_ref[0] // mask + apart, 2)
            here = pl.ds(pl.multiple_of(base + number * height, height), height)
            out_ref[here, :] = ref[position * height : (position + 1) * height, :]


TRANSPOSED_LEFT = (((0,), (0,)), ((), ()))
TRANSPOSED_RIGHT = (((1,), (1,)), ((), ()))


def extra_rows(value):
    first = lax.reduce_precision(value, 8, 7)
    second = lax.reduce_precision(value - first, 8, 7)
    third = value - first - second
    row = lax.broadcasted_iota(jnp.int32, (EXTRA, value.shape[1]), 0)
    rows = jnp.where(row == 0, first, jnp.where(row == 1, second, jnp.where(row == 2, third, 0.0)))
    return rows.astype(BF16)


def gram_kernel(pair, cut, mask, extra, where_ref, *refs):
    refs = list(refs)
    whole = refs.pop()
    field = refs.pop(0) if pair else None
    chunks = [refs.pop(0) for _ in range(CHUNKS)] if cut else []
    others = [refs.pop(0) for _ in range(extra)]
    if cut:
        joined = refs.pop()
        rows, width = chunks[0].shape
        joined[rows:, :] = jnp.zeros((EXTRA, joined.shape[1]), BF16)
        for c, chunk in enumerate(chunks):
            joined[: chunk.shape[0], c * width : (c + 1) * width] = chunk[...]
    else:
        joined = refs.pop(0)
        rows, width = joined.shape[0] - EXTRA, joined.shape[1] // CHUNKS
    field = joined if field is None else field
    mine_ref, other_ref = refs
    half = whole.shape[0] // 2
    middle = CHUNKS * width // 2
    side = lax.rem(where_ref[0] // mask, 2)

    def fill(left, right, count):
        for c in range(CHUNKS):
            here = slice(c * width, (c + 1) * width)
            value = lax.dot_general(left, right[:rows, here], TRANSPOSED_LEFT, preferred_element_type=F32)
            whole[:count, here] = value.astype(BF16)

    if pair:
        used = middle

        @pl.when(where_ref[1] == 0)
        def _():
            fill(joined[:rows, :middle], field, middle)

        @pl.when(where_ref[1] == 1)
        def _():
            fill(field[:rows, middle:], joined, middle)
    else:
        used = middle + middle // 2
        upper = field[:rows, middle:]
        fill(field[:rows, :middle], field, middle)
        corner = lax.dot_general(upper, upper, TRANSPOSED_LEFT, preferred_element_type=F32).astype(BF16)
        whole[middle:used, :middle] = corner[: middle // 2]
        whole[middle:used, middle:] = corner[middle // 2 :]
    if used < whole.shape[0]:
        whole[used:, :] = jnp.zeros((whole.shape[0] - used, whole.shape[1]), BF16)
    mine_ref[:half, :] = whole[pl.ds(pl.multiple_of(side * half, half), half), :]
    other_ref[:half, :] = whole[pl.ds(pl.multiple_of((1 - side) * half, half), half), :]
    if mine_ref.shape[0] > half:
        ends = [field, joined, *others]
        total = sum(jnp.sum(end[rows:, -width:].astype(F32), axis=0, keepdims=True) for end in ends)
        carried = extra_rows(jnp.concatenate([total] * CHUNKS, axis=1))
        mine_ref[half:, :] = carried
        other_ref[half:, :] = carried


def sum_kernel(masks, hop, extra, entries, rows_total, where_ref, *refs):
    terms, outs = refs[: hop + 1], refs[hop + 1 :]
    height = terms[0].shape[0] - extra
    begins, offset = [0, 0], 0
    final = hop == len(masks)
    for i, mask in enumerate(masks[1 : hop + 1], 1):
        height //= 2
        keep = lax.rem(where_ref[0] // mask, 2)
        first_row = offset + (1 - keep) * height
        offset = offset + keep * height
        begins.append(offset)
    if final:
        first_row = offset
    step = terms[-1].shape[0] - extra if final else height
    value = 0.0
    for term, begin in zip(terms, begins):
        here = pl.ds(pl.multiple_of(first_row - begin, EXTRA), step)
        value = value + term[here, :].astype(F32)
    total = None
    if extra:
        total = sum(jnp.sum(term[-extra:, :].astype(F32), axis=0, keepdims=True) for term in terms)
    if not final:
        outs[0][:step, :] = value.astype(BF16)
        if extra:
            outs[0][step:, :] = extra_rows(total)
        return
    if extra:
        level = total / entries
        outs[1][...] = jnp.broadcast_to(level[:, :1], outs[1].shape)
    else:
        level_ref, *outs = outs
        level = level_ref[:1, :1]
    outs[0][...] = (value / (level * rows_total)).astype(BF16)


def mix_kernel(pair, masks, first, last, where_ref, *refs):
    level_ref, *refs = refs if last else (None, *refs)
    total_ref, *refs = (None, *refs) if first else refs
    field, *refs = refs
    out_ref, block = refs[-2:]
    own = refs[-3]
    rows, width = field.shape[0] - EXTRA, field.shape[1] // CHUNKS
    middle = CHUNKS * width // 2

    def finish(mixed, here):
        value = mixed if first else total_ref[:, here] + mixed
        if last:
            value = (1.5 * own[:rows, here].astype(F32) - 0.5 * value) / jnp.sqrt(level_ref[:1, :1])
        out_ref[:, here] = value.astype(out_ref.dtype)

    def times(left, right):
        return jnp.dot(left, right, preferred_element_type=F32)

    def times_transposed(left, right):
        return lax.dot_general(left, right, TRANSPOSED_RIGHT, preferred_element_type=F32)

    if not pair:
        put_in_place(where_ref, masks, refs[0], refs[1], block, 0)
        lower, upper = field[:rows, :middle], field[:rows, middle:]
        corner = block[middle : middle + middle // 2, :]
        corner = jnp.concatenate([corner[:, :middle], corner[:, middle:]], axis=0)
        finish(
            times(lower, block[:middle, :middle]) + times_transposed(upper, block[:middle, middle:]),
            slice(0, middle),
        )
        finish(times(lower, block[:middle, middle:]) + times(upper, corner), slice(middle, 2 * middle))
        return
    height = block.shape[0] // 2
    is_upper = where_ref[1]
    put_in_place(where_ref, masks, refs[0], refs[1], block, is_upper * height)
    put_in_place(where_ref, masks, refs[2], refs[3], block, (1 - is_upper) * height)

    @pl.when(is_upper == 0)
    def _():
        for c in range(CHUNKS):
            here = slice(c * width, (c + 1) * width)
            right = jnp.concatenate([block[:middle, here], block[height : height + middle, here]])
            finish(times(field[:rows, :], right), here)

    @pl.when(is_upper == 1)
    def _():
        for c in range(CHUNKS):
            row = c * width if c * width < middle else height + c * width - middle
            finish(
                times_transposed(field[:rows, :], block[row : row + width, :]), slice(c * width, (c + 1) * width)
            )


def local(orbitals, hamiltonian, neighbours):
    elements, slots, size, _ = hamiltonian.shape
    rows, columns = orbitals.shape
    tiles = lax.axis_size("elem")
    groups = lax.axis_size("orb")
    lines = tiles // 2
    my_tile = lax.axis_index("elem")
    my_group = lax.axis_index("orb")
    odd = my_tile % 2
    line = my_tile // 2

    swap = [(i, i ^ 1) for i in range(tiles)]
    outward = [(2 * i + side, 2 * ((i + 1 - 2 * side) % lines) + side) for i in range(lines) for side in (0, 1)]

    def to_group(value, d):
        return lax.ppermute(value, "orb", [(i, i ^ d) for i in range(groups)])

    place = neighbours % elements
    last_two = place[:, 5:]
    place = jnp.concatenate([place[:, :5], jnp.where(odd == 0, last_two[:, ::-1], last_two)], axis=1)
    by_slot = [hamiltonian[:, s] for s in range(5)]
    by_slot.append(jnp.where(odd == 0, hamiltonian[:, 6], hamiltonian[:, 5]))
    by_slot.append(jnp.where(odd == 0, hamiltonian[:, 5], hamiltonian[:, 6]))
    by_slot.append(jnp.zeros_like(by_slot[0]))
    blocks = jnp.concatenate(by_slot, axis=2)

    width = columns // CHUNKS
    start = [lax.slice_in_dim(orbitals, c * width, (c + 1) * width, axis=1) for c in range(CHUNKS)]
    near = {(0, 0): lax.ppermute(start[0], "elem", swap)}
    order = Order(jnp.zeros((8, 128), F32))
    blocks, place = order(blocks, place)
    start = [start[0]] + [order(field) for field in start[1:]]
    for c in range(1, CHUNKS):
        near[(0, c)] = lax.ppermute(start[c], "elem", swap)

    jobs = [(stage, c) for stage in range(3) for c in range(CHUNKS)]
    far = {}
    firsts, squares, pieces = {}, jnp.zeros((8, width), F32), [{} for _ in range(CHUNKS)]
    current = {(0, c): start[c] for c in range(CHUNKS)}

    def send_on(job):
        near[job] = order(near[job])
        far[job] = lax.ppermute(near[job], "elem", outward)

    def pass_on(c):
        bit = groups // 2
        while bit > 1:
            if bit | 1 not in pieces[c]:
                pieces[c][bit] = order(pieces[c][bit])
                low = 1
                while low < bit:
                    pieces[c][bit | low] = to_group(pieces[c][bit], low)
                    low *= 2
            bit //= 2

    def multiply(job):
        nonlocal squares
        stage, c = job
        far[job] = order(far[job])
        old = ((), (start[c],), (firsts.get(c), squares))[stage]
        last = stage == 2 and c == CHUNKS - 1
        out = product(stage, place, blocks, current[job], near[job], far[job], *old, last=last)
        if stage == 0:
            firsts[c], out = order(*out)
        elif stage == 1:
            out = order(out)
        else:
            if last:
                out = order(out)
            else:
                out, squares = order(*out)
            pieces[c][0] = out
            bit = groups // 2
            while bit > 1:
                pieces[c][bit] = to_group(out, bit)
                bit //= 2
            for earlier in range(max(c - 2, 0), c if c == CHUNKS - 1 else c - 1):
                pass_on(earlier)
            return
        current[(stage + 1, c)] = out
        near[(stage + 1, c)] = lax.ppermute(out, "elem", swap)

    for index, job in enumerate(jobs):
        send_on(job)
        if index:
            multiply(jobs[index - 1])
    multiply(jobs[-1])

    rows_total = rows * tiles
    level = None
    middle = columns // 2
    unit = 16 * tiles
    clock = Schedule()
    z_masks = [2 << i for i in range(lines.bit_length() - 1)]
    panel, there = {}, {}
    mixed, mixes = None, 0

    def is_upper(d):
        return (my_group & (1 << (d.bit_length() - 1))) != 0

    def where(d):
        return jnp.stack([my_tile, is_upper(d) if d else odd]).astype(jnp.int32)

    def over_tiles(value, mask):
        sent = lax.ppermute(value, "elem", [(i, i ^ mask) for i in range(tiles)])
        if mask <= 2:
            return sent, clock.transfer(value, "y" if mask == 1 else "z")
        clock.spend(-1.3)
        return sent, max(clock.transfer(value, "z", mask / 4), clock.transfer(value, "middle", mask / 2))

    def over_groups(value, d):
        return to_group(value, d), clock.transfer(value, "core" if d == 1 else "x")

    def gram_chunk(d, mask, extra):
        height = middle if d else middle + middle // 2
        height += -height % unit
        cut = d not in panel
        args = [panel[0]] if d else []
        if cut:
            if d:
                pass_on(CHUNKS - 1)
                for other in pieces[-1]:
                    there.setdefault(other, max(clock.now + 4.0, 20.0))
            args += order(*[pieces[c][d] for c in range(CHUNKS)])
        others = [pieces[-1].get(other, panel.get(other)) for other in range(1, groups) if other != d] if extra else []
        args += others
        if not cut:
            args.append(panel[d])
        half = jax.ShapeDtypeStruct((height // 2 + extra, columns), BF16)
        outs = (half, half)
        if cut:
            outs += (jax.ShapeDtypeStruct((rows + EXTRA, columns), BF16),)
        scratch = (pltpu.VMEM((height, columns), BF16),)
        name = "gram_pair" if d else "gram_own"
        clock.spend(3.2 if d else 3.0)
        kernel = functools.partial(gram_kernel, d > 0, cut, mask, len(others))
        outs = order(*call(kernel, name, outs, (where(d),), args, scratch))
        if cut:
            panel[d] = outs[2]
            there[d] = clock.now
        for low in (1 << i for i in range(groups.bit_length() - 1)):
            if d | low not in pieces[-1] and (low < d & -d or low == 1 and d == 0):
                panel[d | low] = to_group(panel[d], low)
                there[d | low] = clock.transfer(panel[d], "core" if low == 1 else "x")
                if d == 0:
                    there[low] = min(there[low], 9.5)
        return outs[:2]

    sent = [None]

    def process(d, masks, extra=0, round_y=False, behind=None):
        nonlocal mixed, mixes, level
        if d:
            need = range(groups) if extra else (0,) if d != 1 and not d & (d - 1) else (0, d)
            upper = d != 1 and not d & (d - 1)
            while upper and clock.now < 10.5 or any(there.get(other, 1e9) > clock.now for other in need):
                yield clock.now + 0.5
            if d in panel:
                panel[d] = order(panel[d])
        mine, value = gram_chunk(d, masks[0], extra)
        terms = [mine]
        height = mine.shape[0] - extra

        def added(hop):
            clock.spend(0.8)
            final = hop == len(masks)
            count = height if final else height + extra
            outs = jax.ShapeDtypeStruct((count, columns), BF16)
            args = list(terms)
            if final and extra:
                outs = (outs, jax.ShapeDtypeStruct((8, 128), F32))
            elif final:
                args.append(level)
            kernel = functools.partial(
                sum_kernel, masks, hop, extra, columns * groups * rows_total, rows_total
            )
            return call(kernel, "sum_last" if final else "sum_hop", outs, (where(d),), args)

        for hop, mask in enumerate(masks):
            if hop:
                height //= 2
                value = order(added(hop))
            received, arrival = over_tiles(value, mask)
            yield arrival if hop else arrival - (3.0 if d else 6.0)
            clock.now = max(clock.now, arrival)
            terms.append(order(received))
        while level is None and not extra:
            yield clock.now + 0.5
        part = added(len(masks))
        if extra:
            part, level = order(*part)
        else:
            part = order(part)
        for mask in masks[:0:-1]:
            received, arrival = over_tiles(part, mask)
            yield arrival
            part = order(jnp.concatenate([part, order(received)], axis=0))
            clock.spend(0.5)
        while behind not in sent:
            yield clock.now + 0.5
        part = order(part)
        far, arrival = over_tiles(part, masks[0])
        sent.append(d)
        if d:
            peer, peer_arrival = over_groups(part, d)
        if round_y:
            clock.now = max(clock.now, arrival)
            far = order(far)
            yield peer_arrival
            peer = order(peer)
            peer_far, peer_arrival = over_tiles(peer, masks[0])
        elif d:
            yield peer_arrival - 3.0
            peer = order(peer)
            yield arrival
            far = order(far)
        else:
            yield arrival
            far = order(far)
        parts = (part, far)
        if d:
            if not round_y:
                peer_far, peer_arrival = over_groups(far, d)
            yield peer_arrival
            peer_far = order(peer_far)
            parts += (peer, peer_far)
        first, last = mixes == 0, mixes == groups - 1
        mixes += 1
        shape = jax.ShapeDtypeStruct((rows, columns), BF16 if last else F32)
        scratch = (pltpu.VMEM((len(parts) * part.shape[0], columns), BF16),)
        args = (() if first else (mixed,)) + (panel[d], *parts)
        if last:
            args = (level, *args, panel[0])
        kernel = functools.partial(mix_kernel, d > 0, masks, first, last)
        name = "mix_pair" if d else "mix_own"
        clock.spend(3.2)
        mixed = call(kernel, name, shape, (where(d),), args, scratch, {} if first or last else {1: 0}, 28, 5 * MIB)
        if not last:
            mixed = order(mixed)

    y_first, z_first, z_then_y = (1, *z_masks), (*z_masks, 1), (*z_masks[:1], 1, *z_masks[1:])
    queue = sorted(range(1, groups), key=lambda d: (d != 1, -d))
    carrier = queue[min(1, len(queue) - 1)]
    processes = []
    for d in queue:
        processes.append(process(d, z_first if d == 1 else y_first, EXTRA if d == carrier else 0))
    processes.append(process(0, z_then_y))
    clock.run(processes)
    return mixed


def solution(mesh):
    return jax.shard_map(
        local,
        mesh=mesh,
        in_specs=(P("elem", "orb"), P("elem", None, None, None), P("elem", None)),
        out_specs=P("elem", "orb"),
        check_vma=False,
    )
```

```python
import functools

import jax
import jax.numpy as jnp
from jax import lax
from jax.experimental import pallas as pl
from jax.experimental.pallas import tpu as pltpu
from jax.sharding import PartitionSpec as P

CHUNKS = 4
F32 = jnp.float32
BF16 = jnp.bfloat16
MIB = 1024 * 1024
EXTRA = 16


class Order:
    def __init__(self, token):
        self.token = token

    def __call__(self, *values):
        *values, self.token = lax.optimization_barrier((*values, self.token))
        return values[0] if len(values) == 1 else tuple(values)


class Schedule:
    RATE = 94e3
    CORE_RATE = 400e3
    DELAY = 2.5

    def __init__(self):
        self.now = 0.0
        self.free = {}

    def spend(self, time):
        self.now += time

    def transfer(self, value, link, weight=1.0):
        self.spend(1.3)
        size = value.size * value.dtype.itemsize
        time = weight * (size / self.CORE_RATE if link == "core" else 2 * size / self.RATE)
        begin = max(self.now, self.free.get(link, 0.0))
        self.free[link] = begin + time
        return begin + time + self.DELAY

    def run(self, processes):
        ready = [0.0] * len(processes)
        alive = list(range(len(processes)))
        while alive:
            can = [i for i in alive if ready[i] <= self.now]
            if not can:
                self.now = min(ready[i] for i in alive)
                continue
            try:
                ready[can[0]] = next(processes[can[0]])
            except StopIteration:
                alive.remove(can[0])


def product_kernel(stage, place_ref, blocks_ref, field_ref, near_ref, far_ref, *refs):
    elements, size, _ = blocks_ref.shape
    width = field_ref.shape[1]
    squares = jnp.zeros((8, width), F32)
    filler = jnp.zeros((size, width), BF16)
    for element in range(elements):
        picked = []
        for slot in range(7):
            source = field_ref if slot < 5 else near_ref if slot == 5 else far_ref
            first_row = pl.multiple_of(place_ref[element, slot] * size, size)
            picked.append(source[pl.ds(first_row, size), :])
        stacked = jnp.concatenate(picked + [filler], axis=0)
        total = jnp.dot(blocks_ref[element], stacked, preferred_element_type=F32)
        here = pl.ds(element * size, size)
        if stage == 0:
            wide_ref, half_ref = refs
            wide_ref[here, :] = total
            half_ref[here, :] = total.astype(BF16)
        elif stage == 1:
            before_ref, half_ref = refs
            half_ref[here, :] = (2.0 * total - before_ref[here, :].astype(F32)).astype(BF16)
        else:
            before_ref, earlier_ref, half_ref, *squares_ref = refs
            value = (2.0 * total - before_ref[here, :]).astype(BF16)
            half_ref[here, :] = value
            wide = value.astype(F32)
            squares += jnp.sum((wide * wide).reshape(-1, 8, width), axis=0)
    if stage == 2:
        squares = earlier_ref[...] + squares
        if squares_ref:
            squares_ref[0][...] = squares
        else:
            half_ref[elements * size :, :] = extra_rows(jnp.full((1, width), jnp.sum(squares)))


def call(kernel, name, outs, scalars, args, scratch=(), aliases=None, vmem=16, moved=1024):
    return pl.pallas_call(
        kernel,
        out_shape=outs,
        in_specs=[pl.BlockSpec(memory_space=pltpu.SMEM)] * len(scalars)
        + [pl.BlockSpec(memory_space=pltpu.VMEM)] * len(args),
        scratch_shapes=list(scratch),
        input_output_aliases=aliases or {},
        compiler_params=pltpu.CompilerParams(vmem_limit_bytes=vmem * MIB),
        cost_estimate=pl.CostEstimate(flops=1024, bytes_accessed=moved, transcendentals=0),
        name=name,
    )(*scalars, *args)


def product(stage, place, blocks, field, by_near, by_far, *before, last=False):
    rows, width = field.shape
    ended = jax.ShapeDtypeStruct((rows + EXTRA, width), BF16)
    half = jax.ShapeDtypeStruct((rows, width), BF16)
    wide = jax.ShapeDtypeStruct((rows, width), F32)
    squares = jax.ShapeDtypeStruct((8, width), F32)
    outs = ((wide, half), half, ended if last else (half, squares))[stage]
    args = (blocks, field, by_near, by_far, *before)
    kernel = functools.partial(product_kernel, stage)
    return call(kernel, f"product_{stage}", outs, (place,), args)


def put_in_place(where_ref, masks, mine_ref, far_ref, out_ref, base):
    bits = len(masks)
    height = mine_ref.shape[0] >> (bits - 1)
    for side, ref in ((0, mine_ref), (1, far_ref)):
        for position in range(1 << (bits - 1)):
            distance = side << (bits - 1) | position
            number = 0
            for i, mask in enumerate(masks):
                apart = distance >> (bits - 1 - i) & 1
                number = 2 * number + lax.rem(where_ref[0] // mask + apart, 2)
            here = pl.ds(pl.multiple_of(base + number * height, height), height)
            out_ref[here, :] = ref[position * height : (position + 1) * height, :]


TRANSPOSED_LEFT = (((0,), (0,)), ((), ()))
TRANSPOSED_RIGHT = (((1,), (1,)), ((), ()))


def extra_rows(value):
    first = lax.reduce_precision(value, 8, 7)
    second = lax.reduce_precision(value - first, 8, 7)
    third = value - first - second
    row = lax.broadcasted_iota(jnp.int32, (EXTRA, value.shape[1]), 0)
    rows = jnp.where(row == 0, first, jnp.where(row == 1, second, jnp.where(row == 2, third, 0.0)))
    return rows.astype(BF16)


def side_by_side(refs, rows):
    return jnp.concatenate([ref[:rows, :] for ref in refs], axis=1)


def gram_kernel(pair, mask, where_ref, *refs):
    mine_ref, other_ref, whole = refs[-3:]
    fields = refs[:CHUNKS]
    rows, width = fields[0].shape
    half = whole.shape[0] // 2
    middle = CHUNKS * width // 2
    side = lax.rem(where_ref[0] // mask, 2)

    def fill(left, rights, count):
        for c, right in enumerate(rights):
            value = lax.dot_general(left, right[:rows, :], TRANSPOSED_LEFT, preferred_element_type=F32)
            whole[:count, c * width : (c + 1) * width] = value.astype(BF16)

    if pair:
        peers = refs[CHUNKS : 2 * CHUNKS]
        used = middle

        @pl.when(where_ref[1] == 0)
        def _():
            fill(side_by_side(peers[: CHUNKS // 2], rows), fields, middle)

        @pl.when(where_ref[1] == 1)
        def _():
            fill(side_by_side(fields[CHUNKS // 2 :], rows), peers, middle)
    else:
        used = middle + middle // 2
        upper = side_by_side(fields[CHUNKS // 2 :], rows)
        fill(side_by_side(fields[: CHUNKS // 2], rows), fields, middle)
        corner = lax.dot_general(upper, upper, TRANSPOSED_LEFT, preferred_element_type=F32).astype(BF16)
        whole[middle:used, :middle] = corner[: middle // 2]
        whole[middle:used, middle:] = corner[middle // 2 :]
    if used < whole.shape[0]:
        whole[used:, :] = jnp.zeros((whole.shape[0] - used, whole.shape[1]), BF16)
    mine_ref[:half, :] = whole[pl.ds(pl.multiple_of(side * half, half), half), :]
    other_ref[:half, :] = whole[pl.ds(pl.multiple_of((1 - side) * half, half), half), :]
    if mine_ref.shape[0] > half:
        ends = [fields[-1], *refs[2 * CHUNKS - 1 : -3]]
        total = sum(jnp.sum(end[rows:, :].astype(F32), axis=0, keepdims=True) for end in ends)
        carried = extra_rows(jnp.concatenate([total] * CHUNKS, axis=1))
        mine_ref[half:, :] = carried
        other_ref[half:, :] = carried


def sum_kernel(masks, hop, extra, entries, rows_total, where_ref, *refs):
    terms, outs = refs[: hop + 1], refs[hop + 1 :]
    height = terms[0].shape[0] - extra
    begins, offset = [0, 0], 0
    final = hop == len(masks)
    for i, mask in enumerate(masks[1 : hop + 1], 1):
        height //= 2
        keep = lax.rem(where_ref[0] // mask, 2)
        first_row = offset + (1 - keep) * height
        offset = offset + keep * height
        begins.append(offset)
    if final:
        first_row = offset
    step = terms[-1].shape[0] - extra if final else height
    value = 0.0
    for term, begin in zip(terms, begins):
        here = pl.ds(pl.multiple_of(first_row - begin, EXTRA), step)
        value = value + term[here, :].astype(F32)
    total = None
    if extra:
        total = sum(jnp.sum(term[-extra:, :].astype(F32), axis=0, keepdims=True) for term in terms)
    if not final:
        outs[0][:step, :] = value.astype(BF16)
        if extra:
            outs[0][step:, :] = extra_rows(total)
        return
    if extra:
        level = total / entries
        outs[1][...] = jnp.broadcast_to(level[:, :1], outs[1].shape)
    else:
        level_ref, *outs = outs
        level = level_ref[:1, :1]
    outs[0][...] = (value / (level * rows_total)).astype(BF16)


def mix_kernel(pair, masks, first, last, where_ref, *refs):
    level_ref, *refs = refs if last else (None, *refs)
    total_ref, *refs = (None, *refs) if first else refs
    fields, refs = refs[:CHUNKS], refs[CHUNKS:]
    out_ref, block = refs[-2:]
    own = refs[-2 - CHUNKS : -2]
    rows, width = fields[0].shape
    middle = CHUNKS * width // 2

    def finish(mixed, here):
        value = mixed if first else total_ref[:, here] + mixed
        if last:
            filtered = side_by_side(own, rows)[:, here].astype(F32)
            value = (1.5 * filtered - 0.5 * value) / jnp.sqrt(level_ref[:1, :1])
        out_ref[:, here] = value.astype(out_ref.dtype)

    def times(left, right):
        return jnp.dot(left, right, preferred_element_type=F32)

    def times_transposed(left, right):
        return lax.dot_general(left, right, TRANSPOSED_RIGHT, preferred_element_type=F32)

    if not pair:
        put_in_place(where_ref, masks, refs[0], refs[1], block, 0)
        lower, upper = side_by_side(fields[: CHUNKS // 2], rows), side_by_side(fields[CHUNKS // 2 :], rows)
        corner = block[middle : middle + middle // 2, :]
        corner = jnp.concatenate([corner[:, :middle], corner[:, middle:]], axis=0)
        finish(
            times(lower, block[:middle, :middle]) + times_transposed(upper, block[:middle, middle:]),
            slice(0, middle),
        )
        finish(times(lower, block[:middle, middle:]) + times(upper, corner), slice(middle, 2 * middle))
        return
    height = block.shape[0] // 2
    is_upper = where_ref[1]
    put_in_place(where_ref, masks, refs[0], refs[1], block, is_upper * height)
    put_in_place(where_ref, masks, refs[2], refs[3], block, (1 - is_upper) * height)

    @pl.when(is_upper == 0)
    def _():
        field = side_by_side(fields, rows)
        for c in range(CHUNKS):
            here = slice(c * width, (c + 1) * width)
            finish(times(field, jnp.concatenate([block[:middle, here], block[height : height + middle, here]])), here)

    @pl.when(is_upper == 1)
    def _():
        field = side_by_side(fields, rows)
        for c in range(CHUNKS):
            row = c * width if c * width < middle else height + c * width - middle
            finish(times_transposed(field, block[row : row + width, :]), slice(c * width, (c + 1) * width))


def local(orbitals, hamiltonian, neighbours):
    elements, slots, size, _ = hamiltonian.shape
    rows, columns = orbitals.shape
    tiles = lax.axis_size("elem")
    groups = lax.axis_size("orb")
    lines = tiles // 2
    my_tile = lax.axis_index("elem")
    my_group = lax.axis_index("orb")
    odd = my_tile % 2
    line = my_tile // 2

    swap = [(i, i ^ 1) for i in range(tiles)]
    outward = [(2 * i + side, 2 * ((i + 1 - 2 * side) % lines) + side) for i in range(lines) for side in (0, 1)]

    def to_group(value, d):
        return lax.ppermute(value, "orb", [(i, i ^ d) for i in range(groups)])

    place = neighbours % elements
    last_two = place[:, 5:]
    place = jnp.concatenate([place[:, :5], jnp.where(odd == 0, last_two[:, ::-1], last_two)], axis=1)
    by_slot = [hamiltonian[:, s] for s in range(5)]
    by_slot.append(jnp.where(odd == 0, hamiltonian[:, 6], hamiltonian[:, 5]))
    by_slot.append(jnp.where(odd == 0, hamiltonian[:, 5], hamiltonian[:, 6]))
    by_slot.append(jnp.zeros_like(by_slot[0]))
    blocks = jnp.concatenate(by_slot, axis=2)

    width = columns // CHUNKS
    start = [lax.slice_in_dim(orbitals, c * width, (c + 1) * width, axis=1) for c in range(CHUNKS)]
    near = {(0, 0): lax.ppermute(start[0], "elem", swap)}
    order = Order(jnp.zeros((8, 128), F32))
    blocks, place = order(blocks, place)
    start = [start[0]] + [order(field) for field in start[1:]]
    for c in range(1, CHUNKS):
        near[(0, c)] = lax.ppermute(start[c], "elem", swap)

    jobs = [(stage, c) for stage in range(3) for c in range(CHUNKS)]
    far = {}
    firsts, squares, pieces = {}, jnp.zeros((8, width), F32), [{} for _ in range(CHUNKS)]
    current = {(0, c): start[c] for c in range(CHUNKS)}

    def send_on(job):
        near[job] = order(near[job])
        far[job] = lax.ppermute(near[job], "elem", outward)

    def more_panel(c):
        for d in range(1, groups):
            if d & (d - 1):
                low = d & -d
                if d ^ low in pieces[c] and d not in pieces[c]:
                    pieces[c][d ^ low] = order(pieces[c][d ^ low])
                    pieces[c][d] = to_group(pieces[c][d ^ low], low)

    def settle(c, some=lambda d: True):
        for d in [d for d in pieces[c] if d and some(d)]:
            pieces[c][d] = order(pieces[c][d])

    def multiply(job):
        nonlocal squares
        stage, c = job
        far[job] = order(far[job])
        old = ((), (start[c],), (firsts.get(c), squares))[stage]
        last = stage == 2 and c == CHUNKS - 1
        out = product(stage, place, blocks, current[job], near[job], far[job], *old, last=last)
        if stage == 0:
            firsts[c], out = order(*out)
        elif stage == 1:
            out = order(out)
        else:
            if last:
                out = order(out)
            else:
                out, squares = order(*out)
            pieces[c][0] = out
            bit = groups // 2
            while bit:
                pieces[c][bit] = to_group(out, bit)
                bit //= 2
            if c > 1:
                more_panel(c - 2)
                settle(c - 2, lambda d: not d & (d - 1))
            return
        current[(stage + 1, c)] = out
        near[(stage + 1, c)] = lax.ppermute(out, "elem", swap)

    for index, job in enumerate(jobs):
        send_on(job)
        if index:
            multiply(jobs[index - 1])
    multiply(jobs[-1])

    rows_total = rows * tiles
    level = None
    middle = columns // 2
    unit = 16 * tiles
    clock = Schedule()
    z_masks = [2 << i for i in range(lines.bit_length() - 1)]
    there = {d: 3.0 if d == 1 else 10.5 for d in range(1, groups)}
    mixed, mixes = None, 0

    def is_upper(d):
        return (my_group & (1 << (d.bit_length() - 1))) != 0

    def where(d):
        return jnp.stack([my_tile, is_upper(d) if d else odd]).astype(jnp.int32)

    def all_chunks(d):
        return [pieces[c][d] for c in range(CHUNKS)]

    def over_tiles(value, mask):
        sent = lax.ppermute(value, "elem", [(i, i ^ mask) for i in range(tiles)])
        if mask <= 2:
            return sent, clock.transfer(value, "y" if mask == 1 else "z")
        clock.spend(-1.3)
        return sent, max(clock.transfer(value, "z", mask / 4), clock.transfer(value, "middle", mask / 2))

    def over_groups(value, d):
        return to_group(value, d), clock.transfer(value, "core" if d == 1 else "x")

    def panel_process():
        yield 10.5
        for c in range(CHUNKS - 1):
            more_panel(c)
            settle(c, lambda d: not d & (d - 1))
        more_panel(CHUNKS - 1)
        settle(CHUNKS - 1, lambda d: not d & (d - 1))
        clock.spend(1.3)
        for d in range(1, groups):
            if d & (d - 1):
                there[d] = clock.now + 3.5

    def gram_chunk(d, mask, extra):
        height = middle if d else middle + middle // 2
        height += -height % unit
        fields = all_chunks(0)
        if d:
            fields += list(order(*all_chunks(d)))
        if extra:
            fields += [pieces[-1][other] for other in range(1, groups) if other != d]
        half = jax.ShapeDtypeStruct((height // 2 + extra, columns), BF16)
        scratch = (pltpu.VMEM((height, columns), BF16),)
        name = "gram_pair" if d else "gram_own"
        clock.spend(3.2 if d else 3.0)
        return call(
            functools.partial(gram_kernel, d > 0, mask), name, (half, half), (where(d),), fields, scratch, moved=5 * MIB
        )

    sent = [None]

    def process(d, masks, extra=0, round_y=False, behind=None):
        nonlocal mixed, mixes, level
        need = list(there) if extra else [d] if d else []
        while any(other not in pieces[-1] or there[other] > clock.now for other in need):
            yield clock.now + 0.5
        mine, value = order(*gram_chunk(d, masks[0], extra))
        terms = [mine]
        height = mine.shape[0] - extra

        def added(hop):
            clock.spend(0.8)
            final = hop == len(masks)
            count = height if final else height + extra
            outs = jax.ShapeDtypeStruct((count, columns), BF16)
            args = list(terms)
            if final and extra:
                outs = (outs, jax.ShapeDtypeStruct((8, 128), F32))
            elif final:
                args.append(level)
            kernel = functools.partial(
                sum_kernel, masks, hop, extra, columns * groups * rows_total, rows_total
            )
            return call(kernel, "sum_last" if final else "sum_hop", outs, (where(d),), args)

        for hop, mask in enumerate(masks):
            if hop:
                height //= 2
                value = order(added(hop))
            received, arrival = over_tiles(value, mask)
            yield arrival if hop or mask > 1 else arrival - (3.0 if d else 6.0)
            terms.append(order(received))
        while level is None and not extra:
            yield clock.now + 0.5
        part = added(len(masks))
        if extra:
            part, level = order(*part)
        else:
            part = order(part)
        for mask in masks[:0:-1]:
            received, arrival = over_tiles(part, mask)
            yield arrival
            part = order(jnp.concatenate([part, order(received)], axis=0))
            clock.spend(0.5)
        while behind not in sent:
            yield clock.now + 0.5
        part = order(part)
        far, arrival = over_tiles(part, masks[0])
        sent.append(d)
        if d:
            peer, peer_arrival = over_groups(part, d)
        if round_y:
            clock.now = max(clock.now, arrival)
            far = order(far)
            yield peer_arrival
            peer = order(peer)
            peer_far, peer_arrival = over_tiles(peer, masks[0])
        elif d:
            yield peer_arrival - 3.0
            peer = order(peer)
            yield arrival + (6.0 if d == 1 else 0.0)
            far = order(far)
        else:
            yield arrival
            far = order(far)
        parts = (part, far)
        if d:
            if not round_y:
                peer_far, peer_arrival = over_groups(far, d)
            yield peer_arrival
        while mixes < turn[d]:
            yield clock.now + 0.5
        if d:
            peer_far = order(peer_far)
            parts += (peer, peer_far)
        first, last = mixes == 0, mixes == groups - 1
        mixes += 1
        shape = jax.ShapeDtypeStruct((rows, columns), BF16 if last else F32)
        scratch = (pltpu.VMEM((len(parts) * part.shape[0], columns), BF16),)
        args = (() if first else (mixed,)) + (*all_chunks(d), *parts)
        if last:
            args = (level, *args, *all_chunks(0))
        kernel = functools.partial(mix_kernel, d > 0, masks, first, last)
        name = "mix_pair" if d else "mix_own"
        clock.spend(3.2)
        mixed = call(kernel, name, shape, (where(d),), args, scratch, {} if first or last else {1: 0}, 28, 5 * MIB)
        if not last:
            mixed = order(mixed)

    y_first, z_then_y, y_then_far = (1, *z_masks), (*z_masks[:1], 1, *z_masks[1:]), (1, *z_masks[::-1])
    there[1] = 25.0
    queue = sorted(range(1, groups), key=lambda d: (d == 1, d))
    turn = {d: place for place, d in enumerate(sorted(range(groups), key=lambda d: (d != 1, d)))}
    carrier = queue[min(1, len(queue) - 1)]
    processes = [panel_process()]
    for d in queue:
        first = d == queue[0] and d != carrier
        behind = carrier if d == 1 and d != carrier else None
        processes.append(process(d, z_then_y if first else y_first, EXTRA if d == carrier else 0, first, behind))
    processes.append(process(0, y_then_far, behind=1))
    clock.run(processes)
    return mixed


def solution(mesh):
    return jax.shard_map(
        local,
        mesh=mesh,
        in_specs=(P("elem", "orb"), P("elem", None, None, None), P("elem", None)),
        out_specs=P("elem", "orb"),
        check_vma=False,
    )
```

```python
import functools

import jax
import jax.numpy as jnp
from jax import lax
from jax.experimental import pallas as pl
from jax.experimental.pallas import tpu as pltpu
from jax.sharding import PartitionSpec as P

CHUNKS = 4
F32 = jnp.float32
BF16 = jnp.bfloat16
MIB = 1024 * 1024
EXTRA = 16


class Order:
    def __init__(self, token):
        self.token = token

    def __call__(self, *values):
        *values, self.token = lax.optimization_barrier((*values, self.token))
        return values[0] if len(values) == 1 else tuple(values)


class Schedule:
    RATE = 94e3
    CORE_RATE = 400e3
    DELAY = 2.5

    def __init__(self):
        self.now = 0.0
        self.free = {}

    def spend(self, time):
        self.now += time

    def transfer(self, value, link, weight=1.0):
        self.spend(1.3)
        size = value.size * value.dtype.itemsize
        time = weight * (size / self.CORE_RATE if link == "core" else 2 * size / self.RATE)
        begin = max(self.now, self.free.get(link, 0.0))
        self.free[link] = begin + time
        return begin + time + self.DELAY

    def run(self, processes):
        ready = [0.0] * len(processes)
        alive = list(range(len(processes)))
        while alive:
            can = [i for i in alive if ready[i] <= self.now]
            if not can:
                self.now = min(ready[i] for i in alive)
                continue
            try:
                ready[can[0]] = next(processes[can[0]])
            except StopIteration:
                alive.remove(can[0])


def product_kernel(stage, place_ref, blocks_ref, field_ref, near_ref, far_ref, *refs):
    elements, size, _ = blocks_ref.shape
    width = field_ref.shape[1]
    squares = jnp.zeros((8, width), F32)
    filler = jnp.zeros((size, width), BF16)
    for element in range(elements):
        picked = []
        for slot in range(7):
            source = field_ref if slot < 5 else near_ref if slot == 5 else far_ref
            first_row = pl.multiple_of(place_ref[element, slot] * size, size)
            picked.append(source[pl.ds(first_row, size), :])
        stacked = jnp.concatenate(picked + [filler], axis=0)
        total = jnp.dot(blocks_ref[element], stacked, preferred_element_type=F32)
        here = pl.ds(element * size, size)
        if stage == 0:
            wide_ref, half_ref = refs
            wide_ref[here, :] = total
            half_ref[here, :] = total.astype(BF16)
        elif stage == 1:
            before_ref, half_ref = refs
            half_ref[here, :] = (2.0 * total - before_ref[here, :].astype(F32)).astype(BF16)
        else:
            before_ref, earlier_ref, half_ref, *squares_ref = refs
            value = (2.0 * total - before_ref[here, :]).astype(BF16)
            half_ref[here, :] = value
            wide = value.astype(F32)
            squares += jnp.sum((wide * wide).reshape(-1, 8, width), axis=0)
    if stage == 2:
        squares = earlier_ref[...] + squares
        if squares_ref:
            squares_ref[0][...] = squares
        else:
            half_ref[elements * size :, :] = extra_rows(jnp.full((1, width), jnp.sum(squares)))


def call(kernel, name, outs, scalars, args, scratch=(), aliases=None, vmem=16, moved=1024):
    return pl.pallas_call(
        kernel,
        out_shape=outs,
        in_specs=[pl.BlockSpec(memory_space=pltpu.SMEM)] * len(scalars)
        + [pl.BlockSpec(memory_space=pltpu.VMEM)] * len(args),
        scratch_shapes=list(scratch),
        input_output_aliases=aliases or {},
        compiler_params=pltpu.CompilerParams(vmem_limit_bytes=vmem * MIB),
        cost_estimate=pl.CostEstimate(flops=1024, bytes_accessed=moved, transcendentals=0),
        name=name,
    )(*scalars, *args)


def product(stage, place, blocks, field, by_near, by_far, *before, last=False):
    rows, width = field.shape
    ended = jax.ShapeDtypeStruct((rows + EXTRA, width), BF16)
    half = jax.ShapeDtypeStruct((rows, width), BF16)
    wide = jax.ShapeDtypeStruct((rows, width), F32)
    squares = jax.ShapeDtypeStruct((8, width), F32)
    outs = ((wide, half), half, ended if last else (half, squares))[stage]
    args = (blocks, field, by_near, by_far, *before)
    kernel = functools.partial(product_kernel, stage)
    return call(kernel, f"product_{stage}", outs, (place,), args)


def put_in_place(where_ref, masks, mine_ref, far_ref, out_ref, base):
    bits = len(masks)
    height = mine_ref.shape[0] >> (bits - 1)
    for side, ref in ((0, mine_ref), (1, far_ref)):
        for position in range(1 << (bits - 1)):
            distance = side << (bits - 1) | position
            number = 0
            for i, mask in enumerate(masks):
                apart = distance >> (bits - 1 - i) & 1
                number = 2 * number + lax.rem(where_ref[0] // mask + apart, 2)
            here = pl.ds(pl.multiple_of(base + number * height, height), height)
            out_ref[here, :] = ref[position * height : (position + 1) * height, :]


TRANSPOSED_LEFT = (((0,), (0,)), ((), ()))
TRANSPOSED_RIGHT = (((1,), (1,)), ((), ()))


def extra_rows(value):
    first = lax.reduce_precision(value, 8, 7)
    second = lax.reduce_precision(value - first, 8, 7)
    third = value - first - second
    row = lax.broadcasted_iota(jnp.int32, (EXTRA, value.shape[1]), 0)
    rows = jnp.where(row == 0, first, jnp.where(row == 1, second, jnp.where(row == 2, third, 0.0)))
    return rows.astype(BF16)


def side_by_side(refs, rows):
    return jnp.concatenate([ref[:rows, :] for ref in refs], axis=1)


def gram_kernel(pair, mask, where_ref, *refs):
    mine_ref, other_ref, whole = refs[-3:]
    fields = refs[:CHUNKS]
    rows, width = fields[0].shape
    half = whole.shape[0] // 2
    middle = CHUNKS * width // 2
    side = lax.rem(where_ref[0] // mask, 2)

    def fill(left, rights, count):
        for c, right in enumerate(rights):
            value = lax.dot_general(left, right[:rows, :], TRANSPOSED_LEFT, preferred_element_type=F32)
            whole[:count, c * width : (c + 1) * width] = value.astype(BF16)

    if pair:
        peers = refs[CHUNKS : 2 * CHUNKS]
        used = middle

        @pl.when(where_ref[1] == 0)
        def _():
            fill(side_by_side(peers[: CHUNKS // 2], rows), fields, middle)

        @pl.when(where_ref[1] == 1)
        def _():
            fill(side_by_side(fields[CHUNKS // 2 :], rows), peers, middle)
    else:
        used = middle + middle // 2
        upper = side_by_side(fields[CHUNKS // 2 :], rows)
        fill(side_by_side(fields[: CHUNKS // 2], rows), fields, middle)
        corner = lax.dot_general(upper, upper, TRANSPOSED_LEFT, preferred_element_type=F32).astype(BF16)
        whole[middle:used, :middle] = corner[: middle // 2]
        whole[middle:used, middle:] = corner[middle // 2 :]
    if used < whole.shape[0]:
        whole[used:, :] = jnp.zeros((whole.shape[0] - used, whole.shape[1]), BF16)
    mine_ref[:half, :] = whole[pl.ds(pl.multiple_of(side * half, half), half), :]
    other_ref[:half, :] = whole[pl.ds(pl.multiple_of((1 - side) * half, half), half), :]
    if mine_ref.shape[0] > half:
        ends = [fields[-1], *refs[2 * CHUNKS - 1 : -3]]
        total = sum(jnp.sum(end[rows:, :].astype(F32), axis=0, keepdims=True) for end in ends)
        carried = extra_rows(jnp.concatenate([total] * CHUNKS, axis=1))
        mine_ref[half:, :] = carried
        other_ref[half:, :] = carried


def sum_kernel(masks, hop, extra, entries, rows_total, where_ref, *refs):
    terms, outs = refs[: hop + 1], refs[hop + 1 :]
    height = terms[0].shape[0] - extra
    begins, offset = [0, 0], 0
    final = hop == len(masks)
    for i, mask in enumerate(masks[1 : hop + 1], 1):
        height //= 2
        keep = lax.rem(where_ref[0] // mask, 2)
        first_row = offset + (1 - keep) * height
        offset = offset + keep * height
        begins.append(offset)
    if final:
        first_row = offset
    step = terms[-1].shape[0] - extra if final else height
    value = 0.0
    for term, begin in zip(terms, begins):
        here = pl.ds(pl.multiple_of(first_row - begin, EXTRA), step)
        value = value + term[here, :].astype(F32)
    total = None
    if extra:
        total = sum(jnp.sum(term[-extra:, :].astype(F32), axis=0, keepdims=True) for term in terms)
    if not final:
        outs[0][:step, :] = value.astype(BF16)
        if extra:
            outs[0][step:, :] = extra_rows(total)
        return
    if extra:
        level = total / entries
        outs[1][...] = jnp.broadcast_to(level[:, :1], outs[1].shape)
    else:
        level_ref, *outs = outs
        level = level_ref[:1, :1]
    outs[0][...] = (value / (level * rows_total)).astype(BF16)


def mix_kernel(pair, masks, first, last, where_ref, *refs):
    level_ref, *refs = refs if last else (None, *refs)
    total_ref, *refs = (None, *refs) if first else refs
    fields, refs = refs[:CHUNKS], refs[CHUNKS:]
    out_ref, block = refs[-2:]
    own = refs[-2 - CHUNKS : -2]
    rows, width = fields[0].shape
    middle = CHUNKS * width // 2

    def finish(mixed, here):
        value = mixed if first else total_ref[:, here] + mixed
        if last:
            filtered = side_by_side(own, rows)[:, here].astype(F32)
            value = (1.5 * filtered - 0.5 * value) / jnp.sqrt(level_ref[:1, :1])
        out_ref[:, here] = value.astype(out_ref.dtype)

    def times(left, right):
        return jnp.dot(left, right, preferred_element_type=F32)

    def times_transposed(left, right):
        return lax.dot_general(left, right, TRANSPOSED_RIGHT, preferred_element_type=F32)

    if not pair:
        put_in_place(where_ref, masks, refs[0], refs[1], block, 0)
        lower, upper = side_by_side(fields[: CHUNKS // 2], rows), side_by_side(fields[CHUNKS // 2 :], rows)
        corner = block[middle : middle + middle // 2, :]
        corner = jnp.concatenate([corner[:, :middle], corner[:, middle:]], axis=0)
        finish(
            times(lower, block[:middle, :middle]) + times_transposed(upper, block[:middle, middle:]),
            slice(0, middle),
        )
        finish(times(lower, block[:middle, middle:]) + times(upper, corner), slice(middle, 2 * middle))
        return
    height = block.shape[0] // 2
    is_upper = where_ref[1]
    put_in_place(where_ref, masks, refs[0], refs[1], block, is_upper * height)
    put_in_place(where_ref, masks, refs[2], refs[3], block, (1 - is_upper) * height)

    @pl.when(is_upper == 0)
    def _():
        field = side_by_side(fields, rows)
        for c in range(CHUNKS):
            here = slice(c * width, (c + 1) * width)
            finish(times(field, jnp.concatenate([block[:middle, here], block[height : height + middle, here]])), here)

    @pl.when(is_upper == 1)
    def _():
        field = side_by_side(fields, rows)
        for c in range(CHUNKS):
            row = c * width if c * width < middle else height + c * width - middle
            finish(times_transposed(field, block[row : row + width, :]), slice(c * width, (c + 1) * width))


def local(orbitals, hamiltonian, neighbours):
    elements, slots, size, _ = hamiltonian.shape
    rows, columns = orbitals.shape
    tiles = lax.axis_size("elem")
    groups = lax.axis_size("orb")
    lines = tiles // 2
    my_tile = lax.axis_index("elem")
    my_group = lax.axis_index("orb")
    odd = my_tile % 2
    line = my_tile // 2

    swap = [(i, i ^ 1) for i in range(tiles)]
    outward = [(2 * i + side, 2 * ((i + 1 - 2 * side) % lines) + side) for i in range(lines) for side in (0, 1)]

    def to_group(value, d):
        return lax.ppermute(value, "orb", [(i, i ^ d) for i in range(groups)])

    place = neighbours % elements
    last_two = place[:, 5:]
    place = jnp.concatenate([place[:, :5], jnp.where(odd == 0, last_two[:, ::-1], last_two)], axis=1)
    by_slot = [hamiltonian[:, s] for s in range(5)]
    by_slot.append(jnp.where(odd == 0, hamiltonian[:, 6], hamiltonian[:, 5]))
    by_slot.append(jnp.where(odd == 0, hamiltonian[:, 5], hamiltonian[:, 6]))
    by_slot.append(jnp.zeros_like(by_slot[0]))
    blocks = jnp.concatenate(by_slot, axis=2)

    width = columns // CHUNKS
    start = [lax.slice_in_dim(orbitals, c * width, (c + 1) * width, axis=1) for c in range(CHUNKS)]
    near = {(0, 0): lax.ppermute(start[0], "elem", swap)}
    order = Order(jnp.zeros((8, 128), F32))
    blocks, place = order(blocks, place)
    start = [start[0]] + [order(field) for field in start[1:]]
    for c in range(1, CHUNKS):
        near[(0, c)] = lax.ppermute(start[c], "elem", swap)

    jobs = [(stage, c) for stage in range(3) for c in range(CHUNKS)]
    far = {}
    firsts, squares, pieces = {}, jnp.zeros((8, width), F32), [{} for _ in range(CHUNKS)]
    current = {(0, c): start[c] for c in range(CHUNKS)}

    def send_on(job):
        near[job] = order(near[job])
        far[job] = lax.ppermute(near[job], "elem", outward)

    def more_panel(c):
        for d in range(1, groups):
            if d & (d - 1):
                low = d & -d
                if d ^ low in pieces[c] and d not in pieces[c]:
                    pieces[c][d ^ low] = order(pieces[c][d ^ low])
                    pieces[c][d] = to_group(pieces[c][d ^ low], low)

    def settle(c, some=lambda d: True):
        for d in [d for d in pieces[c] if d and some(d)]:
            pieces[c][d] = order(pieces[c][d])

    def multiply(job):
        nonlocal squares
        stage, c = job
        far[job] = order(far[job])
        old = ((), (start[c],), (firsts.get(c), squares))[stage]
        last = stage == 2 and c == CHUNKS - 1
        out = product(stage, place, blocks, current[job], near[job], far[job], *old, last=last)
        if stage == 0:
            firsts[c], out = order(*out)
        elif stage == 1:
            out = order(out)
        else:
            if last:
                out = order(out)
            else:
                out, squares = order(*out)
            pieces[c][0] = out
            bit = groups // 2
            while bit:
                pieces[c][bit] = to_group(out, bit)
                bit //= 2
            if c > 1:
                more_panel(c - 2)
                settle(c - 2, lambda d: not d & (d - 1))
            if last:
                more_panel(c - 1)
            return
        current[(stage + 1, c)] = out
        near[(stage + 1, c)] = lax.ppermute(out, "elem", swap)

    for index, job in enumerate(jobs):
        send_on(job)
        if index:
            multiply(jobs[index - 1])
    multiply(jobs[-1])

    rows_total = rows * tiles
    level = None
    middle = columns // 2
    unit = 16 * tiles
    clock = Schedule()
    z_masks = [2 << i for i in range(lines.bit_length() - 1)]
    there = {d: 3.0 if d == 1 else 10.5 for d in range(1, groups)}
    mixed, mixes = None, 0

    def is_upper(d):
        return (my_group & (1 << (d.bit_length() - 1))) != 0

    def where(d):
        return jnp.stack([my_tile, is_upper(d) if d else odd]).astype(jnp.int32)

    def all_chunks(d):
        return [pieces[c][d] for c in range(CHUNKS)]

    def over_tiles(value, mask):
        sent = lax.ppermute(value, "elem", [(i, i ^ mask) for i in range(tiles)])
        if mask <= 2:
            return sent, clock.transfer(value, "y" if mask == 1 else "z")
        clock.spend(-1.3)
        return sent, max(clock.transfer(value, "z", mask / 4), clock.transfer(value, "middle", mask / 2))

    def over_groups(value, d):
        return to_group(value, d), clock.transfer(value, "core" if d == 1 else "x")

    def panel_process():
        yield 10.5
        for c in range(CHUNKS - 1):
            more_panel(c)
            settle(c, lambda d: not d & (d - 1))
        more_panel(CHUNKS - 1)
        settle(CHUNKS - 1, lambda d: not d & (d - 1))
        clock.spend(1.3)
        for d in range(1, groups):
            if d & (d - 1):
                there[d] = clock.now + 3.5

    def gram_chunk(d, mask, extra):
        height = middle if d else middle + middle // 2
        height += -height % unit
        fields = all_chunks(0)
        if d:
            fields += list(order(*all_chunks(d)))
        if extra:
            fields += [pieces[-1][other] for other in range(1, groups) if other != d]
        half = jax.ShapeDtypeStruct((height // 2 + extra, columns), BF16)
        scratch = (pltpu.VMEM((height, columns), BF16),)
        name = "gram_pair" if d else "gram_own"
        clock.spend(3.2 if d else 3.0)
        return call(
            functools.partial(gram_kernel, d > 0, mask), name, (half, half), (where(d),), fields, scratch, moved=5 * MIB
        )

    sent = [None]

    def process(d, masks, extra=0, round_y=False, behind=None):
        nonlocal mixed, mixes, level
        need = list(there) if extra else [d] if d else []
        while any(other not in pieces[-1] or there[other] > clock.now for other in need):
            yield clock.now + 0.5
        mine, value = order(*gram_chunk(d, masks[0], extra))
        terms = [mine]
        height = mine.shape[0] - extra

        def added(hop):
            clock.spend(0.8)
            final = hop == len(masks)
            count = height if final else height + extra
            outs = jax.ShapeDtypeStruct((count, columns), BF16)
            args = list(terms)
            if final and extra:
                outs = (outs, jax.ShapeDtypeStruct((8, 128), F32))
            elif final:
                args.append(level)
            kernel = functools.partial(
                sum_kernel, masks, hop, extra, columns * groups * rows_total, rows_total
            )
            return call(kernel, "sum_last" if final else "sum_hop", outs, (where(d),), args)

        for hop, mask in enumerate(masks):
            if hop:
                height //= 2
                value = order(added(hop))
            received, arrival = over_tiles(value, mask)
            yield arrival if hop or mask > 1 else arrival - (3.0 if d else 6.0)
            terms.append(order(received))
        while level is None and not extra:
            yield clock.now + 0.5
        part = added(len(masks))
        if extra:
            part, level = order(*part)
        else:
            part = order(part)
        for mask in masks[:0:-1]:
            received, arrival = over_tiles(part, mask)
            yield arrival
            part = order(jnp.concatenate([part, order(received)], axis=0))
            clock.spend(0.5)
        while behind not in sent:
            yield clock.now + 0.5
        part = order(part)
        far, arrival = over_tiles(part, masks[0])
        sent.append(d)
        if d:
            peer, peer_arrival = over_groups(part, d)
        if round_y:
            clock.now = max(clock.now, arrival)
            far = order(far)
            yield peer_arrival
            peer = order(peer)
            peer_far, peer_arrival = over_tiles(peer, masks[0])
        elif d:
            yield peer_arrival - 3.0
            peer = order(peer)
            yield arrival + (6.0 if d == 1 else 0.0)
            far = order(far)
        else:
            yield arrival
            while mixes < turn[d]:
                yield clock.now + 0.5
            far = order(far)
        parts = (part, far)
        if d:
            if not round_y:
                peer_far, peer_arrival = over_groups(far, d)
            yield peer_arrival
        while mixes < turn[d]:
            yield clock.now + 0.5
        if d:
            peer_far = order(peer_far)
            parts += (peer, peer_far)
        first, last = mixes == 0, mixes == groups - 1
        mixes += 1
        shape = jax.ShapeDtypeStruct((rows, columns), BF16 if last else F32)
        scratch = (pltpu.VMEM((len(parts) * part.shape[0], columns), BF16),)
        args = (() if first else (mixed,)) + (*all_chunks(d), *parts)
        if last:
            args = (level, *args, *all_chunks(0))
        kernel = functools.partial(mix_kernel, d > 0, masks, first, last)
        name = "mix_pair" if d else "mix_own"
        clock.spend(3.2)
        mixed = call(kernel, name, shape, (where(d),), args, scratch, {} if first or last else {1: 0}, 28, 5 * MIB)
        if not last:
            mixed = order(mixed)

    y_first, z_then_y, y_then_far = (1, *z_masks), (*z_masks[:1], 1, *z_masks[1:]), (1, *z_masks[::-1])
    there[1] = 25.0
    queue = sorted(range(1, groups), key=lambda d: (d == 1, d))
    turn = {d: place for place, d in enumerate([queue[-1], *queue[:-2], 0, *queue[-2:-1]])}
    carrier = queue[min(1, len(queue) - 1)]
    processes = [panel_process()]
    for d in queue:
        first = d == queue[0] and d != carrier
        behind = carrier if d == 1 and d != carrier else None
        processes.append(process(d, z_then_y if first else y_first, EXTRA if d == carrier else 0, first, behind))
    processes.append(process(0, y_then_far, behind=1))
    clock.run(processes)
    return mixed


def solution(mesh):
    return jax.shard_map(
        local,
        mesh=mesh,
        in_specs=(P("elem", "orb"), P("elem", None, None, None), P("elem", None)),
        out_specs=P("elem", "orb"),
        check_vma=False,
    )
```

```python
import functools

import jax
import jax.numpy as jnp
from jax import lax
from jax.experimental import pallas as pl
from jax.experimental.pallas import tpu as pltpu
from jax.sharding import PartitionSpec as P

CHUNKS = 4
F32 = jnp.float32
BF16 = jnp.bfloat16
MIB = 1024 * 1024
EXTRA = 16


class Order:
    def __init__(self, token):
        self.token = token

    def __call__(self, *values):
        *values, self.token = lax.optimization_barrier((*values, self.token))
        return values[0] if len(values) == 1 else tuple(values)


class Schedule:
    RATE = 94e3
    CORE_RATE = 400e3
    DELAY = 2.5

    def __init__(self):
        self.now = 0.0
        self.free = {}

    def spend(self, time):
        self.now += time

    def transfer(self, value, link, weight=1.0):
        self.spend(1.3)
        size = value.size * value.dtype.itemsize
        time = weight * (size / self.CORE_RATE if link == "core" else 2 * size / self.RATE)
        begin = max(self.now, self.free.get(link, 0.0))
        self.free[link] = begin + time
        return begin + time + self.DELAY

    def run(self, processes):
        ready = [0.0] * len(processes)
        alive = list(range(len(processes)))
        while alive:
            can = [i for i in alive if ready[i] <= self.now]
            if not can:
                self.now = min(ready[i] for i in alive)
                continue
            try:
                ready[can[0]] = next(processes[can[0]])
            except StopIteration:
                alive.remove(can[0])


def product_kernel(stage, place_ref, blocks_ref, field_ref, near_ref, far_ref, *refs):
    elements, size, _ = blocks_ref.shape
    width = field_ref.shape[1]
    squares = jnp.zeros((8, width), F32)
    filler = jnp.zeros((size, width), BF16)
    for element in range(elements):
        picked = []
        for slot in range(7):
            source = field_ref if slot < 5 else near_ref if slot == 5 else far_ref
            first_row = pl.multiple_of(place_ref[element, slot] * size, size)
            picked.append(source[pl.ds(first_row, size), :])
        stacked = jnp.concatenate(picked + [filler], axis=0)
        total = jnp.dot(blocks_ref[element], stacked, preferred_element_type=F32)
        here = pl.ds(element * size, size)
        if stage == 0:
            wide_ref, half_ref = refs
            wide_ref[here, :] = total
            half_ref[here, :] = total.astype(BF16)
        elif stage == 1:
            before_ref, half_ref = refs
            half_ref[here, :] = (2.0 * total - before_ref[here, :].astype(F32)).astype(BF16)
        else:
            before_ref, earlier_ref, half_ref, *squares_ref = refs
            value = (2.0 * total - before_ref[here, :]).astype(BF16)
            half_ref[here, :] = value
            wide = value.astype(F32)
            squares += jnp.sum((wide * wide).reshape(-1, 8, width), axis=0)
    if stage == 2:
        squares = earlier_ref[...] + squares
        if squares_ref:
            squares_ref[0][...] = squares
        else:
            half_ref[elements * size :, :] = extra_rows(jnp.full((1, width), jnp.sum(squares)))


def call(kernel, name, outs, scalars, args, scratch=(), aliases=None, vmem=10, moved=1024):
    return pl.pallas_call(
        kernel,
        out_shape=outs,
        in_specs=[pl.BlockSpec(memory_space=pltpu.SMEM)] * len(scalars)
        + [pl.BlockSpec(memory_space=pltpu.VMEM)] * len(args),
        scratch_shapes=list(scratch),
        input_output_aliases=aliases or {},
        compiler_params=pltpu.CompilerParams(vmem_limit_bytes=vmem * MIB),
        cost_estimate=pl.CostEstimate(flops=1024, bytes_accessed=moved, transcendentals=0),
        name=name,
    )(*scalars, *args)


def product(stage, place, blocks, field, by_near, by_far, *before, last=False):
    rows, width = field.shape
    ended = jax.ShapeDtypeStruct((rows + EXTRA, width), BF16)
    half = jax.ShapeDtypeStruct((rows, width), BF16)
    wide = jax.ShapeDtypeStruct((rows, width), F32)
    squares = jax.ShapeDtypeStruct((8, width), F32)
    outs = ((wide, half), half, ended if last else (half, squares))[stage]
    args = (blocks, field, by_near, by_far, *before)
    kernel = functools.partial(product_kernel, stage)
    return call(kernel, f"product_{stage}", outs, (place,), args)


def put_in_place(where_ref, masks, mine_ref, far_ref, out_ref, base):
    bits = len(masks)
    height = mine_ref.shape[0] >> (bits - 1)
    for side, ref in ((0, mine_ref), (1, far_ref)):
        for position in range(1 << (bits - 1)):
            distance = side << (bits - 1) | position
            number = 0
            for i, mask in enumerate(masks):
                apart = distance >> (bits - 1 - i) & 1
                number = 2 * number + lax.rem(where_ref[0] // mask + apart, 2)
            here = pl.ds(pl.multiple_of(base + number * height, height), height)
            out_ref[here, :] = ref[position * height : (position + 1) * height, :]


TRANSPOSED_LEFT = (((0,), (0,)), ((), ()))
TRANSPOSED_RIGHT = (((1,), (1,)), ((), ()))


def extra_rows(value):
    first = lax.reduce_precision(value, 8, 7)
    second = lax.reduce_precision(value - first, 8, 7)
    third = value - first - second
    row = lax.broadcasted_iota(jnp.int32, (EXTRA, value.shape[1]), 0)
    rows = jnp.where(row == 0, first, jnp.where(row == 1, second, jnp.where(row == 2, third, 0.0)))
    return rows.astype(BF16)


def side_by_side(refs, rows):
    return jnp.concatenate([ref[:rows, :] for ref in refs], axis=1)


def gram_kernel(pair, mask, where_ref, *refs):
    mine_ref, other_ref, whole = refs[-3:]
    fields = refs[:CHUNKS]
    rows, width = fields[0].shape
    half = whole.shape[0] // 2
    middle = CHUNKS * width // 2
    side = lax.rem(where_ref[0] // mask, 2)

    def fill(left, rights, count):
        for c, right in enumerate(rights):
            value = lax.dot_general(left, right[:rows, :], TRANSPOSED_LEFT, preferred_element_type=F32)
            whole[:count, c * width : (c + 1) * width] = value.astype(BF16)

    if pair:
        peers = refs[CHUNKS : 2 * CHUNKS]
        used = middle

        @pl.when(where_ref[1] == 0)
        def _():
            fill(side_by_side(peers[: CHUNKS // 2], rows), fields, middle)

        @pl.when(where_ref[1] == 1)
        def _():
            fill(side_by_side(fields[CHUNKS // 2 :], rows), peers, middle)
    else:
        used = middle + middle // 2
        upper = side_by_side(fields[CHUNKS // 2 :], rows)
        fill(side_by_side(fields[: CHUNKS // 2], rows), fields, middle)
        corner = lax.dot_general(upper, upper, TRANSPOSED_LEFT, preferred_element_type=F32).astype(BF16)
        whole[middle:used, :middle] = corner[: middle // 2]
        whole[middle:used, middle:] = corner[middle // 2 :]
    if used < whole.shape[0]:
        whole[used:, :] = jnp.zeros((whole.shape[0] - used, whole.shape[1]), BF16)
    mine_ref[:half, :] = whole[pl.ds(pl.multiple_of(side * half, half), half), :]
    other_ref[:half, :] = whole[pl.ds(pl.multiple_of((1 - side) * half, half), half), :]
    if mine_ref.shape[0] > half:
        ends = [fields[-1], *refs[2 * CHUNKS - 1 : -3]]
        total = sum(jnp.sum(end[rows:, :].astype(F32), axis=0, keepdims=True) for end in ends)
        carried = extra_rows(jnp.concatenate([total] * CHUNKS, axis=1))
        mine_ref[half:, :] = carried
        other_ref[half:, :] = carried


def join_kernel(upper_ref, lower_ref, out_ref):
    height = upper_ref.shape[0]
    out_ref[:height, :] = upper_ref[...]
    out_ref[height:, :] = lower_ref[...]


def sum_kernel(masks, hop, extra, entries, rows_total, where_ref, *refs):
    terms, outs = refs[: hop + 1], refs[hop + 1 :]
    height = terms[0].shape[0] - extra
    begins, offset = [0, 0], 0
    final = hop == len(masks)
    for i, mask in enumerate(masks[1 : hop + 1], 1):
        height //= 2
        keep = lax.rem(where_ref[0] // mask, 2)
        first_row = offset + (1 - keep) * height
        offset = offset + keep * height
        begins.append(offset)
    if final:
        first_row = offset
    step = terms[-1].shape[0] - extra if final else height
    value = 0.0
    for term, begin in zip(terms, begins):
        here = pl.ds(pl.multiple_of(first_row - begin, EXTRA), step)
        value = value + term[here, :].astype(F32)
    total = None
    if extra:
        total = sum(jnp.sum(term[-extra:, :].astype(F32), axis=0, keepdims=True) for term in terms)
    if not final:
        outs[0][:step, :] = value.astype(BF16)
        if extra:
            outs[0][step:, :] = extra_rows(total)
        return
    if extra:
        level = total / entries
        outs[1][...] = jnp.broadcast_to(level[:, :1], outs[1].shape)
    else:
        level_ref, *outs = outs
        level = level_ref[:1, :1]
    outs[0][...] = (value / (level * rows_total)).astype(BF16)


def mix_kernel(pair, masks, first, last, where_ref, *refs):
    level_ref, *refs = refs if last else (None, *refs)
    total_ref, *refs = (None, *refs) if first else refs
    fields, refs = refs[:CHUNKS], refs[CHUNKS:]
    out_ref, block = refs[-2:]
    own = refs[-2 - CHUNKS : -2]
    rows, width = fields[0].shape
    middle = CHUNKS * width // 2

    def finish(mixed, here):
        value = mixed if first else total_ref[:, here] + mixed
        if last:
            filtered = side_by_side(own, rows)[:, here].astype(F32)
            value = (1.5 * filtered - 0.5 * value) / jnp.sqrt(level_ref[:1, :1])
        out_ref[:, here] = value.astype(out_ref.dtype)

    def times(left, right):
        return jnp.dot(left, right, preferred_element_type=F32)

    def times_transposed(left, right):
        return lax.dot_general(left, right, TRANSPOSED_RIGHT, preferred_element_type=F32)

    if not pair:
        put_in_place(where_ref, masks, refs[0], refs[1], block, 0)
        lower, upper = side_by_side(fields[: CHUNKS // 2], rows), side_by_side(fields[CHUNKS // 2 :], rows)
        corner = block[middle : middle + middle // 2, :]
        corner = jnp.concatenate([corner[:, :middle], corner[:, middle:]], axis=0)
        finish(
            times(lower, block[:middle, :middle]) + times_transposed(upper, block[:middle, middle:]),
            slice(0, middle),
        )
        finish(times(lower, block[:middle, middle:]) + times(upper, corner), slice(middle, 2 * middle))
        return
    height = block.shape[0] // 2
    is_upper = where_ref[1]
    put_in_place(where_ref, masks, refs[0], refs[1], block, is_upper * height)
    put_in_place(where_ref, masks, refs[2], refs[3], block, (1 - is_upper) * height)

    @pl.when(is_upper == 0)
    def _():
        field = side_by_side(fields, rows)
        for c in range(CHUNKS):
            here = slice(c * width, (c + 1) * width)
            finish(times(field, jnp.concatenate([block[:middle, here], block[height : height + middle, here]])), here)

    @pl.when(is_upper == 1)
    def _():
        field = side_by_side(fields, rows)
        for c in range(CHUNKS):
            row = c * width if c * width < middle else height + c * width - middle
            finish(times_transposed(field, block[row : row + width, :]), slice(c * width, (c + 1) * width))


def local(orbitals, hamiltonian, neighbours):
    elements, slots, size, _ = hamiltonian.shape
    rows, columns = orbitals.shape
    tiles = lax.axis_size("elem")
    groups = lax.axis_size("orb")
    lines = tiles // 2
    my_tile = lax.axis_index("elem")
    my_group = lax.axis_index("orb")
    odd = my_tile % 2
    line = my_tile // 2

    swap = [(i, i ^ 1) for i in range(tiles)]
    outward = [(2 * i + side, 2 * ((i + 1 - 2 * side) % lines) + side) for i in range(lines) for side in (0, 1)]

    def to_group(value, d):
        return lax.ppermute(value, "orb", [(i, i ^ d) for i in range(groups)])

    place = neighbours % elements
    last_two = place[:, 5:]
    place = jnp.concatenate([place[:, :5], jnp.where(odd == 0, last_two[:, ::-1], last_two)], axis=1)
    by_slot = [hamiltonian[:, s] for s in range(5)]
    by_slot.append(jnp.where(odd == 0, hamiltonian[:, 6], hamiltonian[:, 5]))
    by_slot.append(jnp.where(odd == 0, hamiltonian[:, 5], hamiltonian[:, 6]))
    by_slot.append(jnp.zeros_like(by_slot[0]))
    blocks = jnp.concatenate(by_slot, axis=2)

    width = columns // CHUNKS
    start = [lax.slice_in_dim(orbitals, c * width, (c + 1) * width, axis=1) for c in range(CHUNKS)]
    near = {(0, 0): lax.ppermute(start[0], "elem", swap)}
    order = Order(jnp.zeros((8, 128), F32))
    positions = [
        jnp.stack([my_tile, my_group >> max(d.bit_length() - 1, 0) & 1]).astype(jnp.int32) for d in range(groups)
    ]
    blocks, place, *positions = order(blocks, place, *positions)
    start = [start[0]] + [order(field) for field in start[1:]]
    for c in range(1, CHUNKS):
        near[(0, c)] = lax.ppermute(start[c], "elem", swap)

    jobs = [(stage, c) for stage in range(3) for c in range(CHUNKS)]
    far = {}
    firsts, squares, pieces = {}, jnp.zeros((8, width), F32), [{} for _ in range(CHUNKS)]
    current = {(0, c): start[c] for c in range(CHUNKS)}

    def send_on(job):
        near[job] = order(near[job])
        far[job] = lax.ppermute(near[job], "elem", outward)

    def more_panel(c):
        for d in range(1, groups):
            if d & (d - 1):
                low = d & -d
                if d ^ low in pieces[c] and d not in pieces[c]:
                    pieces[c][d ^ low] = order(pieces[c][d ^ low])
                    pieces[c][d] = to_group(pieces[c][d ^ low], low)

    def settle(c, some=lambda d: True):
        for d in [d for d in pieces[c] if d and some(d)]:
            pieces[c][d] = order(pieces[c][d])

    def multiply(job):
        nonlocal squares
        stage, c = job
        far[job] = order(far[job])
        old = ((), (start[c],), (firsts.get(c), squares))[stage]
        last = stage == 2 and c == CHUNKS - 1
        out = product(stage, place, blocks, current[job], near[job], far[job], *old, last=last)
        if stage == 0:
            firsts[c], out = order(*out)
        elif stage == 1:
            out = order(out)
        else:
            if last:
                out = order(out)
            else:
                out, squares = order(*out)
            pieces[c][0] = out
            bit = groups // 2
            while bit:
                pieces[c][bit] = to_group(out, bit)
                bit //= 2
            if c > 1:
                more_panel(c - 2)
                settle(c - 2, lambda d: not d & (d - 1))
            if last:
                more_panel(c - 1)
            return
        current[(stage + 1, c)] = out
        near[(stage + 1, c)] = lax.ppermute(out, "elem", swap)

    for index, job in enumerate(jobs):
        send_on(job)
        if index:
            multiply(jobs[index - 1])
    multiply(jobs[-1])

    rows_total = rows * tiles
    level = None
    middle = columns // 2
    unit = 16 * tiles
    clock = Schedule()
    z_masks = [2 << i for i in range(lines.bit_length() - 1)]
    there = {d: 3.0 if d == 1 else 10.5 for d in range(1, groups)}
    mixed, mixes = None, 0

    def where(d):
        return positions[d]

    def all_chunks(d):
        return [pieces[c][d] for c in range(CHUNKS)]

    def over_tiles(value, mask):
        sent = lax.ppermute(value, "elem", [(i, i ^ mask) for i in range(tiles)])
        if mask <= 2:
            return sent, clock.transfer(value, "y" if mask == 1 else "z")
        clock.spend(-1.3)
        return sent, max(clock.transfer(value, "z", mask / 4), clock.transfer(value, "middle", mask / 2))

    def over_groups(value, d):
        return to_group(value, d), clock.transfer(value, "core" if d == 1 else "x")

    def panel_process():
        yield 10.5
        for c in range(CHUNKS - 1):
            more_panel(c)
            settle(c, lambda d: not d & (d - 1))
        more_panel(CHUNKS - 1)
        settle(CHUNKS - 1, lambda d: not d & (d - 1))
        clock.spend(1.3)
        for d in range(1, groups):
            if d & (d - 1):
                there[d] = clock.now + 3.5

    def gram_chunk(d, mask, extra):
        height = middle if d else middle + middle // 2
        height += -height % unit
        fields = all_chunks(0)
        if d:
            fields += list(order(*all_chunks(d)))
        if extra:
            fields += [pieces[-1][other] for other in range(1, groups) if other != d]
        half = jax.ShapeDtypeStruct((height // 2 + extra, columns), BF16)
        scratch = (pltpu.VMEM((height, columns), BF16),)
        name = "gram_pair" if d else "gram_own"
        clock.spend(3.2 if d else 3.0)
        return call(
            functools.partial(gram_kernel, d > 0, mask), name, (half, half), (where(d),), fields, scratch, moved=5 * MIB
        )

    sent = [None]

    def process(d, masks, extra=0, round_y=False, behind=None):
        nonlocal mixed, mixes, level
        need = list(there) if extra else [d] if d else []
        while any(other not in pieces[-1] or there[other] > clock.now for other in need):
            yield clock.now + 0.5
        mine, value = order(*gram_chunk(d, masks[0], extra))
        terms = [mine]
        height = mine.shape[0] - extra

        def added(hop):
            clock.spend(0.8)
            final = hop == len(masks)
            count = height if final else height + extra
            outs = jax.ShapeDtypeStruct((count, columns), BF16)
            args = list(terms)
            if final and extra:
                outs = (outs, jax.ShapeDtypeStruct((8, 128), F32))
            elif final:
                args.append(level)
            kernel = functools.partial(
                sum_kernel, masks, hop, extra, columns * groups * rows_total, rows_total
            )
            return call(kernel, "sum_last" if final else "sum_hop", outs, (where(d),), args)

        for hop, mask in enumerate(masks):
            if hop:
                height //= 2
                value = order(added(hop))
            received, arrival = over_tiles(value, mask)
            yield arrival if hop or mask > 1 else arrival - (3.0 if d else 6.0)
            terms.append(order(received))
        while level is None and not extra:
            yield clock.now + 0.5
        part = added(len(masks))
        if extra:
            part, level = order(*part)
        else:
            part = order(part)
        for mask in masks[:0:-1]:
            received, arrival = over_tiles(part, mask)
            yield arrival
            joined = jax.ShapeDtypeStruct((2 * part.shape[0], columns), BF16)
            part = order(call(join_kernel, "join", joined, (), (part, order(received))))
            clock.spend(0.5)
        while behind not in sent:
            yield clock.now + 0.5
        part = order(part)
        far, arrival = over_tiles(part, masks[0])
        sent.append(d)
        if d:
            peer, peer_arrival = over_groups(part, d)
        if round_y:
            clock.now = max(clock.now, arrival)
            far = order(far)
            yield peer_arrival
            peer = order(peer)
            peer_far, peer_arrival = over_tiles(peer, masks[0])
        elif d:
            yield peer_arrival - 3.0
            peer = order(peer)
            yield arrival + (6.0 if d == 1 else 0.0)
            far = order(far)
        else:
            yield arrival
            while mixes < turn[d]:
                yield clock.now + 0.5
            far = order(far)
        parts = (part, far)
        if d:
            if not round_y:
                peer_far, peer_arrival = over_groups(far, d)
            yield peer_arrival
        while mixes < turn[d]:
            yield clock.now + 0.5
        if d:
            peer_far = order(peer_far)
            parts += (peer, peer_far)
        first, last = mixes == 0, mixes == groups - 1
        mixes += 1
        shape = jax.ShapeDtypeStruct((rows, columns), BF16 if last else F32)
        scratch = (pltpu.VMEM((len(parts) * part.shape[0], columns), BF16),)
        args = (() if first else (mixed,)) + (*all_chunks(d), *parts)
        if last:
            args = (level, *args, *all_chunks(0))
        kernel = functools.partial(mix_kernel, d > 0, masks, first, last)
        name = "mix_pair" if d else "mix_own"
        clock.spend(3.2)
        mixed = call(kernel, name, shape, (where(d),), args, scratch, {} if first or last else {1: 0}, 20, 5 * MIB)
        if not last:
            mixed = order(mixed)

    y_first, z_then_y, y_then_far = (1, *z_masks), (*z_masks[:1], 1, *z_masks[1:]), (1, *z_masks[::-1])
    there[1] = 25.0
    queue = sorted(range(1, groups), key=lambda d: (d == 1, d))
    turn = {d: place for place, d in enumerate([queue[-1], *queue[:-2], 0, *queue[-2:-1]])}
    carrier = queue[min(1, len(queue) - 1)]
    processes = [panel_process()]
    for d in queue:
        first = d == queue[0] and d != carrier
        behind = carrier if d == 1 and d != carrier else None
        processes.append(process(d, z_then_y if first else y_first, EXTRA if d == carrier else 0, first, behind))
    processes.append(process(0, y_then_far, behind=1))
    clock.run(processes)
    return mixed


def solution(mesh):
    return jax.shard_map(
        local,
        mesh=mesh,
        in_specs=(P("elem", "orb"), P("elem", None, None, None), P("elem", None)),
        out_specs=P("elem", "orb"),
        check_vma=False,
    )
```

```python
import functools

import jax
import jax.numpy as jnp
from jax import lax
from jax.experimental import pallas as pl
from jax.experimental.pallas import tpu as pltpu
from jax.sharding import PartitionSpec as P

CHUNKS = 4
F32 = jnp.float32
BF16 = jnp.bfloat16
MIB = 1024 * 1024
EXTRA = 16


class Order:
    def __init__(self, token):
        self.token = token

    def __call__(self, *values):
        *values, self.token = lax.optimization_barrier((*values, self.token))
        return values[0] if len(values) == 1 else tuple(values)


class Schedule:
    RATE = 94e3
    CORE_RATE = 400e3
    DELAY = 2.5

    def __init__(self):
        self.now = 0.0
        self.free = {}

    def spend(self, time):
        self.now += time

    def transfer(self, value, link, weight=1.0):
        self.spend(1.3)
        size = value.size * value.dtype.itemsize
        time = weight * (size / self.CORE_RATE if link == "core" else 2 * size / self.RATE)
        begin = max(self.now, self.free.get(link, 0.0))
        self.free[link] = begin + time
        return begin + time + self.DELAY

    def run(self, processes):
        ready = [0.0] * len(processes)
        alive = list(range(len(processes)))
        while alive:
            can = [i for i in alive if ready[i] <= self.now]
            if not can:
                self.now = min(ready[i] for i in alive)
                continue
            try:
                ready[can[0]] = next(processes[can[0]])
            except StopIteration:
                alive.remove(can[0])


def product_kernel(stage, place_ref, blocks_ref, field_ref, near_ref, far_ref, *refs):
    elements, size, _ = blocks_ref.shape
    width = field_ref.shape[1]
    squares = jnp.zeros((8, width), F32)
    filler = jnp.zeros((size, width), BF16)
    for element in range(elements):
        picked = []
        for slot in range(7):
            source = field_ref if slot < 5 else near_ref if slot == 5 else far_ref
            first_row = pl.multiple_of(place_ref[element, slot] * size, size)
            picked.append(source[pl.ds(first_row, size), :])
        stacked = jnp.concatenate(picked + [filler], axis=0)
        total = jnp.dot(blocks_ref[element], stacked, preferred_element_type=F32)
        here = pl.ds(element * size, size)
        if stage == 0:
            wide_ref, half_ref = refs
            wide_ref[here, :] = total
            half_ref[here, :] = total.astype(BF16)
        elif stage == 1:
            before_ref, half_ref = refs
            half_ref[here, :] = (2.0 * total - before_ref[here, :].astype(F32)).astype(BF16)
        else:
            before_ref, earlier_ref, half_ref, *squares_ref = refs
            value = (2.0 * total - before_ref[here, :]).astype(BF16)
            half_ref[here, :] = value
            wide = value.astype(F32)
            squares += jnp.sum((wide * wide).reshape(-1, 8, width), axis=0)
    if stage == 2:
        squares = earlier_ref[...] + squares
        if squares_ref:
            squares_ref[0][...] = squares
        else:
            half_ref[elements * size :, :] = extra_rows(jnp.full((1, width), jnp.sum(squares)))


def call(kernel, name, outs, scalars, args, scratch=(), aliases=None, vmem=10, moved=1024):
    return pl.pallas_call(
        kernel,
        out_shape=outs,
        in_specs=[pl.BlockSpec(memory_space=pltpu.SMEM)] * len(scalars)
        + [pl.BlockSpec(memory_space=pltpu.VMEM)] * len(args),
        scratch_shapes=list(scratch),
        input_output_aliases=aliases or {},
        compiler_params=pltpu.CompilerParams(vmem_limit_bytes=vmem * MIB),
        cost_estimate=pl.CostEstimate(flops=1024, bytes_accessed=moved, transcendentals=0),
        name=name,
    )(*scalars, *args)


def product(stage, place, blocks, field, by_near, by_far, *before, last=False):
    rows, width = field.shape
    ended = jax.ShapeDtypeStruct((rows + EXTRA, width), BF16)
    half = jax.ShapeDtypeStruct((rows, width), BF16)
    wide = jax.ShapeDtypeStruct((rows, width), F32)
    squares = jax.ShapeDtypeStruct((8, width), F32)
    outs = ((wide, half), half, ended if last else (half, squares))[stage]
    args = (blocks, field, by_near, by_far, *before)
    kernel = functools.partial(product_kernel, stage)
    return call(kernel, f"product_{stage}", outs, (place,), args)


def put_in_place(where_ref, masks, mine_ref, far_ref, out_ref, base):
    bits = len(masks)
    height = mine_ref.shape[0] >> (bits - 1)
    for side, ref in ((0, mine_ref), (1, far_ref)):
        for position in range(1 << (bits - 1)):
            distance = side << (bits - 1) | position
            number = 0
            for i, mask in enumerate(masks):
                apart = distance >> (bits - 1 - i) & 1
                number = 2 * number + lax.rem(where_ref[0] // mask + apart, 2)
            here = pl.ds(pl.multiple_of(base + number * height, height), height)
            out_ref[here, :] = ref[position * height : (position + 1) * height, :]


TRANSPOSED_LEFT = (((0,), (0,)), ((), ()))
TRANSPOSED_RIGHT = (((1,), (1,)), ((), ()))


def extra_rows(value):
    first = lax.reduce_precision(value, 8, 7)
    second = lax.reduce_precision(value - first, 8, 7)
    third = value - first - second
    row = lax.broadcasted_iota(jnp.int32, (EXTRA, value.shape[1]), 0)
    rows = jnp.where(row == 0, first, jnp.where(row == 1, second, jnp.where(row == 2, third, 0.0)))
    return rows.astype(BF16)


def side_by_side(refs, rows):
    return jnp.concatenate([ref[:rows, :] for ref in refs], axis=1)


def gram_kernel(pair, mask, where_ref, *refs):
    mine_ref, other_ref, whole = refs[-3:]
    fields = refs[:CHUNKS]
    rows, width = fields[0].shape
    half = whole.shape[0] // 2
    middle = CHUNKS * width // 2
    side = lax.rem(where_ref[0] // mask, 2)

    def fill(left, rights, count):
        for c, right in enumerate(rights):
            value = lax.dot_general(left, right[:rows, :], TRANSPOSED_LEFT, preferred_element_type=F32)
            whole[:count, c * width : (c + 1) * width] = value.astype(BF16)

    if pair:
        peers = refs[CHUNKS : 2 * CHUNKS]
        used = middle

        @pl.when(where_ref[1] == 0)
        def _():
            fill(side_by_side(peers[: CHUNKS // 2], rows), fields, middle)

        @pl.when(where_ref[1] == 1)
        def _():
            fill(side_by_side(fields[CHUNKS // 2 :], rows), peers, middle)
    else:
        used = middle + middle // 2
        upper = side_by_side(fields[CHUNKS // 2 :], rows)
        fill(side_by_side(fields[: CHUNKS // 2], rows), fields, middle)
        corner = lax.dot_general(upper, upper, TRANSPOSED_LEFT, preferred_element_type=F32).astype(BF16)
        whole[middle:used, :middle] = corner[: middle // 2]
        whole[middle:used, middle:] = corner[middle // 2 :]
    if used < whole.shape[0]:
        whole[used:, :] = jnp.zeros((whole.shape[0] - used, whole.shape[1]), BF16)
    mine_ref[:half, :] = whole[pl.ds(pl.multiple_of(side * half, half), half), :]
    other_ref[:half, :] = whole[pl.ds(pl.multiple_of((1 - side) * half, half), half), :]
    if mine_ref.shape[0] > half:
        ends = [fields[-1], *refs[2 * CHUNKS - 1 : -3]]
        total = sum(jnp.sum(end[rows:, :].astype(F32), axis=0, keepdims=True) for end in ends)
        carried = extra_rows(jnp.concatenate([total] * CHUNKS, axis=1))
        mine_ref[half:, :] = carried
        other_ref[half:, :] = carried


def join_kernel(upper_ref, lower_ref, out_ref):
    height = upper_ref.shape[0]
    out_ref[:height, :] = upper_ref[...]
    out_ref[height:, :] = lower_ref[...]


def sum_kernel(masks, hop, extra, entries, rows_total, where_ref, *refs):
    terms, outs = refs[: hop + 1], refs[hop + 1 :]
    height = terms[0].shape[0] - extra
    begins, offset = [0, 0], 0
    final = hop == len(masks)
    for i, mask in enumerate(masks[1 : hop + 1], 1):
        height //= 2
        keep = lax.rem(where_ref[0] // mask, 2)
        first_row = offset + (1 - keep) * height
        offset = offset + keep * height
        begins.append(offset)
    if final:
        first_row = offset
    step = terms[-1].shape[0] - extra if final else height
    value = 0.0
    for term, begin in zip(terms, begins):
        here = pl.ds(pl.multiple_of(first_row - begin, EXTRA), step)
        value = value + term[here, :].astype(F32)
    total = None
    if extra:
        total = sum(jnp.sum(term[-extra:, :].astype(F32), axis=0, keepdims=True) for term in terms)
    if not final:
        outs[0][:step, :] = value.astype(BF16)
        if extra:
            outs[0][step:, :] = extra_rows(total)
        return
    if extra:
        level = total / entries
        outs[1][...] = jnp.broadcast_to(level[:, :1], outs[1].shape)
    else:
        level_ref, *outs = outs
        level = level_ref[:1, :1]
    outs[0][...] = (value / (level * rows_total)).astype(BF16)


def mix_kernel(pair, masks, first, last, where_ref, *refs):
    level_ref, *refs = refs if last else (None, *refs)
    total_ref, *refs = (None, *refs) if first else refs
    fields, refs = refs[:CHUNKS], refs[CHUNKS:]
    out_ref, block = refs[-2:]
    own = refs[-2 - CHUNKS : -2]
    rows, width = fields[0].shape
    middle = CHUNKS * width // 2

    def finish(mixed, here):
        value = mixed if first else total_ref[:, here] + mixed
        if last:
            filtered = side_by_side(own, rows)[:, here].astype(F32)
            value = (1.5 * filtered - 0.5 * value) / jnp.sqrt(level_ref[:1, :1])
        out_ref[:, here] = value.astype(out_ref.dtype)

    def times(left, right):
        return jnp.dot(left, right, preferred_element_type=F32)

    def times_transposed(left, right):
        return lax.dot_general(left, right, TRANSPOSED_RIGHT, preferred_element_type=F32)

    if not pair:
        put_in_place(where_ref, masks, refs[0], refs[1], block, 0)
        lower, upper = side_by_side(fields[: CHUNKS // 2], rows), side_by_side(fields[CHUNKS // 2 :], rows)
        corner = block[middle : middle + middle // 2, :]
        corner = jnp.concatenate([corner[:, :middle], corner[:, middle:]], axis=0)
        finish(
            times(lower, block[:middle, :middle]) + times_transposed(upper, block[:middle, middle:]),
            slice(0, middle),
        )
        finish(times(lower, block[:middle, middle:]) + times(upper, corner), slice(middle, 2 * middle))
        return
    height = block.shape[0] // 2
    is_upper = where_ref[1]
    put_in_place(where_ref, masks, refs[0], refs[1], block, is_upper * height)
    put_in_place(where_ref, masks, refs[2], refs[3], block, (1 - is_upper) * height)

    @pl.when(is_upper == 0)
    def _():
        field = side_by_side(fields, rows)
        for c in range(CHUNKS):
            here = slice(c * width, (c + 1) * width)
            finish(times(field, jnp.concatenate([block[:middle, here], block[height : height + middle, here]])), here)

    @pl.when(is_upper == 1)
    def _():
        field = side_by_side(fields, rows)
        for c in range(CHUNKS):
            row = c * width if c * width < middle else height + c * width - middle
            finish(times_transposed(field, block[row : row + width, :]), slice(c * width, (c + 1) * width))


def local(orbitals, hamiltonian, neighbours):
    elements, slots, size, _ = hamiltonian.shape
    rows, columns = orbitals.shape
    tiles = lax.axis_size("elem")
    groups = lax.axis_size("orb")
    lines = tiles // 2
    my_tile = lax.axis_index("elem")
    my_group = lax.axis_index("orb")
    odd = my_tile % 2
    line = my_tile // 2

    swap = [(i, i ^ 1) for i in range(tiles)]
    outward = [(2 * i + side, 2 * ((i + 1 - 2 * side) % lines) + side) for i in range(lines) for side in (0, 1)]

    def to_group(value, d):
        return lax.ppermute(value, "orb", [(i, i ^ d) for i in range(groups)])

    place = neighbours % elements
    last_two = place[:, 5:]
    place = jnp.concatenate([place[:, :5], jnp.where(odd == 0, last_two[:, ::-1], last_two)], axis=1)
    by_slot = [hamiltonian[:, s] for s in range(5)]
    by_slot.append(jnp.where(odd == 0, hamiltonian[:, 6], hamiltonian[:, 5]))
    by_slot.append(jnp.where(odd == 0, hamiltonian[:, 5], hamiltonian[:, 6]))
    by_slot.append(jnp.zeros_like(by_slot[0]))
    blocks = jnp.concatenate(by_slot, axis=2)

    width = columns // CHUNKS
    start = [lax.slice_in_dim(orbitals, c * width, (c + 1) * width, axis=1) for c in range(CHUNKS)]
    near = {(0, 0): lax.ppermute(start[0], "elem", swap)}
    order = Order(jnp.zeros((8, 128), F32))
    positions = [
        jnp.stack([my_tile, my_group >> max(d.bit_length() - 1, 0) & 1]).astype(jnp.int32) for d in range(groups)
    ]
    blocks, place, *positions = order(blocks, place, *positions)
    start = [start[0]] + [order(field) for field in start[1:]]
    for c in range(1, CHUNKS):
        near[(0, c)] = lax.ppermute(start[c], "elem", swap)

    jobs = [(stage, c) for stage in range(3) for c in range(CHUNKS)]
    far = {}
    firsts, squares, pieces = {}, jnp.zeros((8, width), F32), [{} for _ in range(CHUNKS)]
    current = {(0, c): start[c] for c in range(CHUNKS)}

    def send_on(job):
        near[job] = order(near[job])
        far[job] = lax.ppermute(near[job], "elem", outward)

    def more_panel(c):
        for d in range(1, groups):
            if d & (d - 1):
                low = d & -d
                if d ^ low in pieces[c] and d not in pieces[c]:
                    pieces[c][d ^ low] = order(pieces[c][d ^ low])
                    pieces[c][d] = to_group(pieces[c][d ^ low], low)

    def settle(c, some=lambda d: True):
        for d in [d for d in pieces[c] if d and some(d)]:
            pieces[c][d] = order(pieces[c][d])

    def multiply(job):
        nonlocal squares
        stage, c = job
        far[job] = order(far[job])
        old = ((), (start[c],), (firsts.get(c), squares))[stage]
        last = stage == 2 and c == CHUNKS - 1
        out = product(stage, place, blocks, current[job], near[job], far[job], *old, last=last)
        if stage == 0:
            firsts[c], out = order(*out)
        elif stage == 1:
            out = order(out)
        else:
            if last:
                out = order(out)
            else:
                out, squares = order(*out)
            pieces[c][0] = out
            bit = groups // 2
            while bit:
                pieces[c][bit] = to_group(out, bit)
                bit //= 2
            if c > 1:
                more_panel(c - 2)
                settle(c - 2, lambda d: not d & (d - 1))
            if last:
                more_panel(c - 1)
            return
        current[(stage + 1, c)] = out
        near[(stage + 1, c)] = lax.ppermute(out, "elem", swap)

    for index, job in enumerate(jobs):
        send_on(job)
        if index:
            multiply(jobs[index - 1])
    multiply(jobs[-1])

    rows_total = rows * tiles
    level = None
    middle = columns // 2
    unit = 16 * tiles
    clock = Schedule()
    z_masks = [2 << i for i in range(lines.bit_length() - 1)]
    there = {d: 3.0 if d == 1 else 10.5 for d in range(1, groups)}
    mixed, mixes = None, 0

    def where(d):
        return positions[d]

    def all_chunks(d):
        return [pieces[c][d] for c in range(CHUNKS)]

    def over_tiles(value, mask):
        sent = lax.ppermute(value, "elem", [(i, i ^ mask) for i in range(tiles)])
        if mask <= 2:
            return sent, clock.transfer(value, "y" if mask == 1 else "z")
        clock.spend(-1.3)
        return sent, max(clock.transfer(value, "z", mask / 4), clock.transfer(value, "middle", mask / 2))

    def over_groups(value, d):
        return to_group(value, d), clock.transfer(value, "core" if d == 1 else "x")

    def panel_process():
        yield 10.5
        for c in range(CHUNKS - 1):
            more_panel(c)
            settle(c, lambda d: not d & (d - 1))
        more_panel(CHUNKS - 1)
        settle(CHUNKS - 1, lambda d: not d & (d - 1))
        clock.spend(1.3)
        for d in range(1, groups):
            if d & (d - 1):
                there[d] = clock.now + 3.5

    def gram_chunk(d, mask, extra):
        height = middle if d else middle + middle // 2
        height += -height % unit
        fields = all_chunks(0)
        if d:
            fields += list(order(*all_chunks(d)))
        if extra:
            fields += [pieces[-1][other] for other in range(1, groups) if other != d]
        half = jax.ShapeDtypeStruct((height // 2 + extra, columns), BF16)
        scratch = (pltpu.VMEM((height, columns), BF16),)
        name = "gram_pair" if d else "gram_own"
        clock.spend(3.2 if d else 3.0)
        return call(
            functools.partial(gram_kernel, d > 0, mask), name, (half, half), (where(d),), fields, scratch, moved=5 * MIB
        )

    sent = [None]

    def process(d, masks, extra=0, round_y=False, behind=None):
        nonlocal mixed, mixes, level
        need = list(there) if extra else [d] if d else []
        while any(other not in pieces[-1] or there[other] > clock.now for other in need):
            yield clock.now + 0.5
        mine, value = gram_chunk(d, masks[0], extra)
        if d:
            mine, value = order(mine, value)
        terms = [mine]
        height = mine.shape[0] - extra

        def added(hop):
            clock.spend(0.8)
            final = hop == len(masks)
            count = height if final else height + extra
            outs = jax.ShapeDtypeStruct((count, columns), BF16)
            args = list(terms)
            if final and extra:
                outs = (outs, jax.ShapeDtypeStruct((8, 128), F32))
            elif final:
                args.append(level)
            kernel = functools.partial(
                sum_kernel, masks, hop, extra, columns * groups * rows_total, rows_total
            )
            return call(kernel, "sum_last" if final else "sum_hop", outs, (where(d),), args)

        for hop, mask in enumerate(masks):
            if hop:
                height //= 2
                value = order(added(hop))
            received, arrival = over_tiles(value, mask)
            yield arrival if hop or mask > 1 else arrival - (3.0 if d else 6.0)
            terms.append(order(received))
        while level is None and not extra:
            yield clock.now + 0.5
        part = added(len(masks))
        if extra:
            part, level = order(*part)
        else:
            part = order(part)
        for mask in masks[:0:-1]:
            while mask != masks[-1] and d == 0 and behind not in sent:
                yield clock.now + 0.5
            received, arrival = over_tiles(order(part), mask)
            yield arrival
            joined = jax.ShapeDtypeStruct((2 * part.shape[0], columns), BF16)
            part = order(call(join_kernel, "join", joined, (), (part, order(received))))
            clock.spend(0.5)
        while behind not in sent:
            yield clock.now + 0.5
        part = order(part)
        far, arrival = over_tiles(part, masks[0])
        sent.append(d)
        if d:
            peer, peer_arrival = over_groups(part, d)
        if round_y:
            clock.now = max(clock.now, arrival)
            far = order(far)
            yield peer_arrival
            peer = order(peer)
            peer_far, peer_arrival = over_tiles(peer, masks[0])
        elif d:
            yield peer_arrival - 3.0
            peer = order(peer)
            yield arrival + (6.0 if d == 1 else 0.0)
            far = order(far)
        else:
            yield arrival
            while mixes < turn[d]:
                yield clock.now + 0.5
            far = order(far)
        parts = (part, far)
        if d:
            if not round_y:
                peer_far, peer_arrival = over_groups(far, d)
            yield peer_arrival
        while mixes < turn[d]:
            yield clock.now + 0.5
        if d:
            peer_far = order(peer_far)
            parts += (peer, peer_far)
        first, last = mixes == 0, mixes == groups - 1
        mixes += 1
        shape = jax.ShapeDtypeStruct((rows, columns), BF16 if last else F32)
        scratch = (pltpu.VMEM((len(parts) * part.shape[0], columns), BF16),)
        args = (() if first else (mixed,)) + (*all_chunks(d), *parts)
        if last:
            args = (level, *args, *all_chunks(0))
        kernel = functools.partial(mix_kernel, d > 0, masks, first, last)
        name = "mix_pair" if d else "mix_own"
        clock.spend(3.2)
        mixed = call(kernel, name, shape, (where(d),), args, scratch, {} if first or last else {1: 0}, 20, 5 * MIB)
        if not last:
            mixed = order(mixed)

    y_first, z_then_y, y_then_far = (1, *z_masks), (*z_masks[:1], 1, *z_masks[1:]), (1, *z_masks[::-1])
    there[1] = 25.0
    queue = sorted(range(1, groups), key=lambda d: (d == 1, d))
    turn = {d: place for place, d in enumerate([queue[-1], *queue[:-2], 0, *queue[-2:-1]])}
    carrier = queue[min(1, len(queue) - 1)]
    processes = [panel_process()]
    for d in queue:
        first = d == queue[0] and d != carrier
        behind = carrier if d == 1 and d != carrier else None
        processes.append(process(d, z_then_y if first else y_first, EXTRA if d == carrier else 0, first, behind))
    processes.append(process(0, y_then_far, behind=1))
    clock.run(processes)
    return mixed


def solution(mesh):
    return jax.shard_map(
        local,
        mesh=mesh,
        in_specs=(P("elem", "orb"), P("elem", None, None, None), P("elem", None)),
        out_specs=P("elem", "orb"),
        check_vma=False,
    )
```

```python
import functools

import jax
import jax.numpy as jnp
from jax import lax
from jax.experimental import pallas as pl
from jax.experimental.pallas import tpu as pltpu
from jax.sharding import PartitionSpec as P

CHUNKS = 4
F32 = jnp.float32
BF16 = jnp.bfloat16
MIB = 1024 * 1024
EXTRA = 16


class Order:
    def __init__(self, token):
        self.token = token

    def __call__(self, *values):
        *values, self.token = lax.optimization_barrier((*values, self.token))
        return values[0] if len(values) == 1 else tuple(values)


class Schedule:
    RATE = 94e3
    CORE_RATE = 400e3
    DELAY = 2.5

    def __init__(self):
        self.now = 0.0
        self.free = {}

    def spend(self, time):
        self.now += time

    def transfer(self, value, link, weight=1.0):
        self.spend(1.3)
        size = value.size * value.dtype.itemsize
        time = weight * (size / self.CORE_RATE if link == "core" else 2 * size / self.RATE)
        begin = max(self.now, self.free.get(link, 0.0))
        self.free[link] = begin + time
        return begin + time + self.DELAY

    def run(self, processes):
        ready = [0.0] * len(processes)
        alive = list(range(len(processes)))
        while alive:
            can = [i for i in alive if ready[i] <= self.now]
            if not can:
                self.now = min(ready[i] for i in alive)
                continue
            try:
                ready[can[0]] = next(processes[can[0]])
            except StopIteration:
                alive.remove(can[0])


def product_kernel(stage, place_ref, blocks_ref, field_ref, near_ref, far_ref, *refs):
    elements, size, _ = blocks_ref.shape
    width = field_ref.shape[1]
    squares = jnp.zeros((8, width), F32)
    filler = jnp.zeros((size, width), BF16)
    for element in range(elements):
        picked = []
        for slot in range(7):
            source = field_ref if slot < 5 else near_ref if slot == 5 else far_ref
            first_row = pl.multiple_of(place_ref[element, slot] * size, size)
            picked.append(source[pl.ds(first_row, size), :])
        stacked = jnp.concatenate(picked + [filler], axis=0)
        total = jnp.dot(blocks_ref[element], stacked, preferred_element_type=F32)
        here = pl.ds(element * size, size)
        if stage == 0:
            wide_ref, half_ref = refs
            wide_ref[here, :] = total
            half_ref[here, :] = total.astype(BF16)
        elif stage == 1:
            before_ref, half_ref = refs
            half_ref[here, :] = (2.0 * total - before_ref[here, :].astype(F32)).astype(BF16)
        else:
            before_ref, earlier_ref, half_ref, *squares_ref = refs
            value = (2.0 * total - before_ref[here, :]).astype(BF16)
            half_ref[here, :] = value
            wide = value.astype(F32)
            squares += jnp.sum((wide * wide).reshape(-1, 8, width), axis=0)
    if stage == 2:
        squares = earlier_ref[...] + squares
        if squares_ref:
            squares_ref[0][...] = squares
        else:
            half_ref[elements * size :, :] = extra_rows(jnp.full((1, width), jnp.sum(squares)))


def call(kernel, name, outs, scalars, args, scratch=(), aliases=None, vmem=10, moved=1024):
    return pl.pallas_call(
        kernel,
        out_shape=outs,
        in_specs=[pl.BlockSpec(memory_space=pltpu.SMEM)] * len(scalars)
        + [pl.BlockSpec(memory_space=pltpu.VMEM)] * len(args),
        scratch_shapes=list(scratch),
        input_output_aliases=aliases or {},
        compiler_params=pltpu.CompilerParams(vmem_limit_bytes=vmem * MIB),
        cost_estimate=pl.CostEstimate(flops=1024, bytes_accessed=moved, transcendentals=0),
        name=name,
    )(*scalars, *args)


def product(stage, place, blocks, field, by_near, by_far, *before, last=False):
    rows, width = field.shape
    ended = jax.ShapeDtypeStruct((rows + EXTRA, width), BF16)
    half = jax.ShapeDtypeStruct((rows, width), BF16)
    wide = jax.ShapeDtypeStruct((rows, width), F32)
    squares = jax.ShapeDtypeStruct((8, width), F32)
    outs = ((wide, half), half, ended if last else (half, squares))[stage]
    args = (blocks, field, by_near, by_far, *before)
    kernel = functools.partial(product_kernel, stage)
    return call(kernel, f"product_{stage}", outs, (place,), args)


def put_in_place(where_ref, masks, mine_ref, far_ref, out_ref, base):
    bits = len(masks)
    height = mine_ref.shape[0] >> (bits - 1)
    for side, ref in ((0, mine_ref), (1, far_ref)):
        for position in range(1 << (bits - 1)):
            distance = side << (bits - 1) | position
            number = 0
            for i, mask in enumerate(masks):
                apart = distance >> (bits - 1 - i) & 1
                number = 2 * number + lax.rem(where_ref[0] // mask + apart, 2)
            here = pl.ds(pl.multiple_of(base + number * height, height), height)
            out_ref[here, :] = ref[position * height : (position + 1) * height, :]


TRANSPOSED_LEFT = (((0,), (0,)), ((), ()))
TRANSPOSED_RIGHT = (((1,), (1,)), ((), ()))


def extra_rows(value):
    first = lax.reduce_precision(value, 8, 7)
    second = lax.reduce_precision(value - first, 8, 7)
    third = value - first - second
    row = lax.broadcasted_iota(jnp.int32, (EXTRA, value.shape[1]), 0)
    rows = jnp.where(row == 0, first, jnp.where(row == 1, second, jnp.where(row == 2, third, 0.0)))
    return rows.astype(BF16)


def side_by_side(refs, rows):
    return jnp.concatenate([ref[:rows, :] for ref in refs], axis=1)


def gram_kernel(pair, mask, where_ref, *refs):
    mine_ref, other_ref, whole = refs[-3:]
    fields = refs[:CHUNKS]
    rows, width = fields[0].shape
    half = whole.shape[0] // 2
    middle = CHUNKS * width // 2
    side = lax.rem(where_ref[0] // mask, 2)

    def fill(left, rights, count):
        for c, right in enumerate(rights):
            value = lax.dot_general(left, right[:rows, :], TRANSPOSED_LEFT, preferred_element_type=F32)
            whole[:count, c * width : (c + 1) * width] = value.astype(BF16)

    if pair:
        peers = refs[CHUNKS : 2 * CHUNKS]
        used = middle

        @pl.when(where_ref[1] == 0)
        def _():
            fill(side_by_side(peers[: CHUNKS // 2], rows), fields, middle)

        @pl.when(where_ref[1] == 1)
        def _():
            fill(side_by_side(fields[CHUNKS // 2 :], rows), peers, middle)
    else:
        used = middle + middle // 2
        upper = side_by_side(fields[CHUNKS // 2 :], rows)
        fill(side_by_side(fields[: CHUNKS // 2], rows), fields, middle)
        corner = lax.dot_general(upper, upper, TRANSPOSED_LEFT, preferred_element_type=F32).astype(BF16)
        whole[middle:used, :middle] = corner[: middle // 2]
        whole[middle:used, middle:] = corner[middle // 2 :]
    if used < whole.shape[0]:
        whole[used:, :] = jnp.zeros((whole.shape[0] - used, whole.shape[1]), BF16)
    mine_ref[:half, :] = whole[pl.ds(pl.multiple_of(side * half, half), half), :]
    other_ref[:half, :] = whole[pl.ds(pl.multiple_of((1 - side) * half, half), half), :]
    if mine_ref.shape[0] > half:
        ends = [fields[-1], *refs[2 * CHUNKS - 1 : -3]]
        total = sum(jnp.sum(end[rows:, :].astype(F32), axis=0, keepdims=True) for end in ends)
        carried = extra_rows(jnp.concatenate([total] * CHUNKS, axis=1))
        mine_ref[half:, :] = carried
        other_ref[half:, :] = carried


def join_kernel(upper_ref, lower_ref, out_ref):
    height = upper_ref.shape[0]
    out_ref[:height, :] = upper_ref[...]
    out_ref[height:, :] = lower_ref[...]


def sum_kernel(masks, hop, extra, entries, rows_total, where_ref, *refs):
    terms, outs = refs[: hop + 1], refs[hop + 1 :]
    height = terms[0].shape[0] - extra
    begins, offset = [0, 0], 0
    final = hop == len(masks)
    for i, mask in enumerate(masks[1 : hop + 1], 1):
        height //= 2
        keep = lax.rem(where_ref[0] // mask, 2)
        first_row = offset + (1 - keep) * height
        offset = offset + keep * height
        begins.append(offset)
    if final:
        first_row = offset
    step = terms[-1].shape[0] - extra if final else height
    value = 0.0
    for term, begin in zip(terms, begins):
        here = pl.ds(pl.multiple_of(first_row - begin, EXTRA), step)
        value = value + term[here, :].astype(F32)
    total = None
    if extra:
        total = sum(jnp.sum(term[-extra:, :].astype(F32), axis=0, keepdims=True) for term in terms)
    if not final:
        outs[0][:step, :] = value.astype(BF16)
        if extra:
            outs[0][step:, :] = extra_rows(total)
        return
    if extra:
        level = total / entries
        outs[1][...] = jnp.broadcast_to(level[:, :1], outs[1].shape)
    else:
        level_ref, *outs = outs
        level = level_ref[:1, :1]
    outs[0][...] = (value / (level * rows_total)).astype(BF16)


def mix_kernel(pair, masks, first, last, where_ref, *refs):
    level_ref, *refs = refs if last else (None, *refs)
    total_ref, *refs = (None, *refs) if first else refs
    fields, refs = refs[:CHUNKS], refs[CHUNKS:]
    out_ref, block = refs[-2:]
    own = refs[-2 - CHUNKS : -2]
    rows, width = fields[0].shape
    middle = CHUNKS * width // 2

    def finish(mixed, here):
        value = mixed if first else total_ref[:, here] + mixed
        if last:
            filtered = side_by_side(own, rows)[:, here].astype(F32)
            value = (1.5 * filtered - 0.5 * value) / jnp.sqrt(level_ref[:1, :1])
        out_ref[:, here] = value.astype(out_ref.dtype)

    def times(left, right):
        return jnp.dot(left, right, preferred_element_type=F32)

    def times_transposed(left, right):
        return lax.dot_general(left, right, TRANSPOSED_RIGHT, preferred_element_type=F32)

    if not pair:
        put_in_place(where_ref, masks, refs[0], refs[1], block, 0)
        lower, upper = side_by_side(fields[: CHUNKS // 2], rows), side_by_side(fields[CHUNKS // 2 :], rows)
        corner = block[middle : middle + middle // 2, :]
        corner = jnp.concatenate([corner[:, :middle], corner[:, middle:]], axis=0)
        finish(
            times(lower, block[:middle, :middle]) + times_transposed(upper, block[:middle, middle:]),
            slice(0, middle),
        )
        finish(times(lower, block[:middle, middle:]) + times(upper, corner), slice(middle, 2 * middle))
        return
    height = block.shape[0] // 2
    is_upper = where_ref[1]
    put_in_place(where_ref, masks, refs[0], refs[1], block, is_upper * height)
    put_in_place(where_ref, masks, refs[2], refs[3], block, (1 - is_upper) * height)

    @pl.when(is_upper == 0)
    def _():
        field = side_by_side(fields, rows)
        for c in range(CHUNKS):
            here = slice(c * width, (c + 1) * width)
            finish(times(field, jnp.concatenate([block[:middle, here], block[height : height + middle, here]])), here)

    @pl.when(is_upper == 1)
    def _():
        field = side_by_side(fields, rows)
        for c in range(CHUNKS):
            row = c * width if c * width < middle else height + c * width - middle
            finish(times_transposed(field, block[row : row + width, :]), slice(c * width, (c + 1) * width))


def local(orbitals, hamiltonian, neighbours):
    elements, slots, size, _ = hamiltonian.shape
    rows, columns = orbitals.shape
    tiles = lax.axis_size("elem")
    groups = lax.axis_size("orb")
    lines = tiles // 2
    my_tile = lax.axis_index("elem")
    my_group = lax.axis_index("orb")
    odd = my_tile % 2
    line = my_tile // 2

    swap = [(i, i ^ 1) for i in range(tiles)]
    outward = [(2 * i + side, 2 * ((i + 1 - 2 * side) % lines) + side) for i in range(lines) for side in (0, 1)]

    def to_group(value, d):
        return lax.ppermute(value, "orb", [(i, i ^ d) for i in range(groups)])

    place = neighbours % elements
    last_two = place[:, 5:]
    place = jnp.concatenate([place[:, :5], jnp.where(odd == 0, last_two[:, ::-1], last_two)], axis=1)
    by_slot = [hamiltonian[:, s] for s in range(5)]
    by_slot.append(jnp.where(odd == 0, hamiltonian[:, 6], hamiltonian[:, 5]))
    by_slot.append(jnp.where(odd == 0, hamiltonian[:, 5], hamiltonian[:, 6]))
    by_slot.append(jnp.zeros_like(by_slot[0]))
    blocks = jnp.concatenate(by_slot, axis=2)

    width = columns // CHUNKS
    start = [lax.slice_in_dim(orbitals, c * width, (c + 1) * width, axis=1) for c in range(CHUNKS)]
    near = {(0, 0): lax.ppermute(start[0], "elem", swap)}
    order = Order(jnp.zeros((8, 128), F32))
    positions = [
        jnp.stack([my_tile, my_group >> max(d.bit_length() - 1, 0) & 1]).astype(jnp.int32) for d in range(groups)
    ]
    blocks, place, *positions = order(blocks, place, *positions)
    start = [start[0]] + [order(field) for field in start[1:]]
    for c in range(1, CHUNKS):
        near[(0, c)] = lax.ppermute(start[c], "elem", swap)

    jobs = [(stage, c) for stage in range(3) for c in range(CHUNKS)]
    far = {}
    firsts, squares, pieces = {}, jnp.zeros((8, width), F32), [{} for _ in range(CHUNKS)]
    current = {(0, c): start[c] for c in range(CHUNKS)}

    def send_on(job):
        near[job] = order(near[job])
        far[job] = lax.ppermute(near[job], "elem", outward)

    def more_panel(c):
        for d in range(1, groups):
            if d & (d - 1):
                low = d & -d
                if d ^ low in pieces[c] and d not in pieces[c]:
                    pieces[c][d ^ low] = order(pieces[c][d ^ low])
                    pieces[c][d] = to_group(pieces[c][d ^ low], low)

    def settle(c, some=lambda d: True):
        for d in [d for d in pieces[c] if d and some(d)]:
            pieces[c][d] = order(pieces[c][d])

    def multiply(job):
        nonlocal squares
        stage, c = job
        far[job] = order(far[job])
        old = ((), (start[c],), (firsts.get(c), squares))[stage]
        last = stage == 2 and c == CHUNKS - 1
        out = product(stage, place, blocks, current[job], near[job], far[job], *old, last=last)
        if stage == 0:
            firsts[c], out = order(*out)
        elif stage == 1:
            out = order(out)
        else:
            if last:
                out = order(out)
            else:
                out, squares = order(*out)
            pieces[c][0] = out
            bit = groups // 2
            while bit:
                pieces[c][bit] = to_group(out, bit)
                bit //= 2
            if c > 1:
                more_panel(c - 2)
                settle(c - 2, lambda d: not d & (d - 1))
            if last:
                more_panel(c - 1)
            return
        current[(stage + 1, c)] = out
        near[(stage + 1, c)] = lax.ppermute(out, "elem", swap)

    for index, job in enumerate(jobs):
        send_on(job)
        if index:
            multiply(jobs[index - 1])
    multiply(jobs[-1])

    rows_total = rows * tiles
    level = None
    middle = columns // 2
    unit = 16 * tiles
    clock = Schedule()
    z_masks = [2 << i for i in range(lines.bit_length() - 1)]
    there = {d: 3.0 if d == 1 else 10.5 for d in range(1, groups)}
    mixed, mixes = None, 0

    def where(d):
        return positions[d]

    def all_chunks(d):
        return [pieces[c][d] for c in range(CHUNKS)]

    def over_tiles(value, mask):
        sent = lax.ppermute(value, "elem", [(i, i ^ mask) for i in range(tiles)])
        if mask <= 2:
            return sent, clock.transfer(value, "y" if mask == 1 else "z")
        clock.spend(-1.3)
        return sent, max(clock.transfer(value, "z", mask / 4), clock.transfer(value, "middle", mask / 2))

    def over_groups(value, d):
        return to_group(value, d), clock.transfer(value, "core" if d == 1 else "x")

    def panel_process():
        yield 10.5
        for c in range(CHUNKS - 1):
            more_panel(c)
            settle(c, lambda d: not d & (d - 1))
        more_panel(CHUNKS - 1)
        settle(CHUNKS - 1, lambda d: not d & (d - 1))
        clock.spend(1.3)
        for d in range(1, groups):
            if d & (d - 1):
                there[d] = clock.now + 3.5

    def gram_chunk(d, mask, extra):
        height = middle if d else middle + middle // 2
        height += -height % unit
        fields = all_chunks(0)
        if d:
            fields += list(order(*all_chunks(d)))
        if extra:
            fields += [pieces[-1][other] for other in range(1, groups) if other != d]
        half = jax.ShapeDtypeStruct((height // 2 + extra, columns), BF16)
        scratch = (pltpu.VMEM((height, columns), BF16),)
        name = "gram_pair" if d else "gram_own"
        clock.spend(3.2 if d else 3.0)
        return call(
            functools.partial(gram_kernel, d > 0, mask), name, (half, half), (where(d),), fields, scratch, moved=5 * MIB
        )

    sent = [None]

    def process(d, masks, extra=0, round_y=False, behind=None):
        nonlocal mixed, mixes, level
        need = list(there) if extra else [d] if d else []
        while any(other not in pieces[-1] or there[other] > clock.now for other in need):
            yield clock.now + 0.5
        mine, value = order(*gram_chunk(d, masks[0], extra))
        terms = [mine]
        height = mine.shape[0] - extra

        def added(hop):
            clock.spend(0.8)
            final = hop == len(masks)
            count = height if final else height + extra
            outs = jax.ShapeDtypeStruct((count, columns), BF16)
            args = list(terms)
            if final and extra:
                outs = (outs, jax.ShapeDtypeStruct((8, 128), F32))
            elif final:
                args.append(level)
            kernel = functools.partial(
                sum_kernel, masks, hop, extra, columns * groups * rows_total, rows_total
            )
            return call(kernel, "sum_last" if final else "sum_hop", outs, (where(d),), args)

        for hop, mask in enumerate(masks):
            if hop:
                height //= 2
                value = order(added(hop))
            received, arrival = over_tiles(value, mask)
            yield arrival if hop or mask > 1 else arrival - (3.0 if d else 6.0)
            terms.append(order(received))
        while level is None and not extra:
            yield clock.now + 0.5
        part = added(len(masks))
        if extra:
            part, level = order(*part)
        else:
            part = order(part)
        for mask in masks[:0:-1]:
            received, arrival = over_tiles(part, mask)
            yield arrival
            joined = jax.ShapeDtypeStruct((2 * part.shape[0], columns), BF16)
            part = order(call(join_kernel, "join", joined, (), (part, order(received))))
            clock.spend(0.5)
        while behind not in sent:
            yield clock.now + 0.5
        part = order(part)
        far, arrival = over_tiles(part, masks[0])
        sent.append(d)
        if d:
            peer, peer_arrival = over_groups(part, d)
        if round_y:
            clock.now = max(clock.now, arrival)
            far = order(far)
            yield peer_arrival
            peer = order(peer)
            peer_far, peer_arrival = over_tiles(peer, masks[0])
        elif d:
            yield peer_arrival - 3.0
            peer = order(peer)
            yield arrival + (6.0 if d == 1 else 0.0)
            far = order(far)
        else:
            yield arrival
            while mixes < turn[d]:
                yield clock.now + 0.5
            far = order(far)
        parts = (part, far)
        if d:
            if not round_y:
                peer_far, peer_arrival = over_groups(far, d)
            yield peer_arrival
        while mixes < turn[d]:
            yield clock.now + 0.5
        if d:
            peer_far = order(peer_far)
            parts += (peer, peer_far)
        first, last = mixes == 0, mixes == groups - 1
        mixes += 1
        shape = jax.ShapeDtypeStruct((rows, columns), BF16 if last else F32)
        scratch = (pltpu.VMEM((len(parts) * part.shape[0], columns), BF16),)
        args = (() if first else (mixed,)) + (*all_chunks(d), *parts)
        if last:
            args = (level, *args, *all_chunks(0))
        kernel = functools.partial(mix_kernel, d > 0, masks, first, last)
        name = "mix_pair" if d else "mix_own"
        clock.spend(3.2)
        mixed = call(kernel, name, shape, (where(d),), args, scratch, {} if first or last else {1: 0}, 20, 5 * MIB)
        if not last:
            mixed = order(mixed)

    y_first, z_then_y = (1, *z_masks), (*z_masks[:1], 1, *z_masks[1:])
    there[1] = 25.0
    queue = sorted(range(1, groups), key=lambda d: (d == 1, d))
    turn = {d: place for place, d in enumerate([queue[-1], *queue[:-2], 0, *queue[-2:-1]])}
    carrier = queue[min(1, len(queue) - 1)]
    processes = [panel_process()]
    for d in queue:
        first = d == queue[0] and d != carrier
        behind = carrier if d == 1 and d != carrier else None
        processes.append(process(d, z_then_y if first else y_first, EXTRA if d == carrier else 0, first, behind))
    processes.append(process(0, y_first, behind=1))
    clock.run(processes)
    return mixed


def solution(mesh):
    return jax.shard_map(
        local,
        mesh=mesh,
        in_specs=(P("elem", "orb"), P("elem", None, None, None), P("elem", None)),
        out_specs=P("elem", "orb"),
        check_vma=False,
    )
```

```python
import functools

import jax
import jax.numpy as jnp
from jax import lax
from jax.experimental import pallas as pl
from jax.experimental.pallas import tpu as pltpu
from jax.sharding import PartitionSpec as P

CHUNKS = 4
F32 = jnp.float32
BF16 = jnp.bfloat16
MIB = 1024 * 1024
EXTRA = 16


class Order:
    def __init__(self, token):
        self.token = token

    def __call__(self, *values):
        *values, self.token = lax.optimization_barrier((*values, self.token))
        return values[0] if len(values) == 1 else tuple(values)


class Schedule:
    RATE = 94e3
    CORE_RATE = 400e3
    DELAY = 2.5

    def __init__(self):
        self.now = 0.0
        self.free = {}

    def spend(self, time):
        self.now += time

    def transfer(self, value, link, weight=1.0):
        self.spend(1.3)
        size = value.size * value.dtype.itemsize
        time = weight * (size / self.CORE_RATE if link == "core" else 2 * size / self.RATE)
        begin = max(self.now, self.free.get(link, 0.0))
        self.free[link] = begin + time
        return begin + time + self.DELAY

    def run(self, processes):
        ready = [0.0] * len(processes)
        alive = list(range(len(processes)))
        while alive:
            can = [i for i in alive if ready[i] <= self.now]
            if not can:
                self.now = min(ready[i] for i in alive)
                continue
            try:
                ready[can[0]] = next(processes[can[0]])
            except StopIteration:
                alive.remove(can[0])


def product_kernel(stage, place_ref, blocks_ref, field_ref, near_ref, far_ref, *refs):
    elements, size, _ = blocks_ref.shape
    width = field_ref.shape[1]
    squares = jnp.zeros((8, width), F32)
    filler = jnp.zeros((size, width), BF16)
    for element in range(elements):
        picked = []
        for slot in range(7):
            source = field_ref if slot < 5 else near_ref if slot == 5 else far_ref
            first_row = pl.multiple_of(place_ref[element, slot] * size, size)
            picked.append(source[pl.ds(first_row, size), :])
        stacked = jnp.concatenate(picked + [filler], axis=0)
        total = jnp.dot(blocks_ref[element], stacked, preferred_element_type=F32)
        here = pl.ds(element * size, size)
        if stage == 0:
            wide_ref, half_ref = refs
            wide_ref[here, :] = total
            half_ref[here, :] = total.astype(BF16)
        elif stage == 1:
            before_ref, half_ref = refs
            half_ref[here, :] = (2.0 * total - before_ref[here, :].astype(F32)).astype(BF16)
        else:
            before_ref, earlier_ref, half_ref, *squares_ref = refs
            value = (2.0 * total - before_ref[here, :]).astype(BF16)
            half_ref[here, :] = value
            wide = value.astype(F32)
            squares += jnp.sum((wide * wide).reshape(-1, 8, width), axis=0)
    if stage == 2:
        squares = earlier_ref[...] + squares
        if squares_ref:
            squares_ref[0][...] = squares
        else:
            half_ref[elements * size :, :] = extra_rows(jnp.full((1, width), jnp.sum(squares)))


def call(kernel, name, outs, scalars, args, scratch=(), aliases=None, vmem=10, moved=1024):
    return pl.pallas_call(
        kernel,
        out_shape=outs,
        in_specs=[pl.BlockSpec(memory_space=pltpu.SMEM)] * len(scalars)
        + [pl.BlockSpec(memory_space=pltpu.VMEM)] * len(args),
        scratch_shapes=list(scratch),
        input_output_aliases=aliases or {},
        compiler_params=pltpu.CompilerParams(vmem_limit_bytes=vmem * MIB),
        cost_estimate=pl.CostEstimate(flops=1024, bytes_accessed=moved, transcendentals=0),
        name=name,
    )(*scalars, *args)


def product(stage, place, blocks, field, by_near, by_far, *before, last=False):
    rows, width = field.shape
    ended = jax.ShapeDtypeStruct((rows + EXTRA, width), BF16)
    half = jax.ShapeDtypeStruct((rows, width), BF16)
    wide = jax.ShapeDtypeStruct((rows, width), F32)
    squares = jax.ShapeDtypeStruct((8, width), F32)
    outs = ((wide, half), half, ended if last else (half, squares))[stage]
    args = (blocks, field, by_near, by_far, *before)
    kernel = functools.partial(product_kernel, stage)
    return call(kernel, f"product_{stage}", outs, (place,), args)


def put_in_place(where_ref, masks, mine_ref, far_ref, out_ref, base):
    bits = len(masks)
    height = mine_ref.shape[0] >> (bits - 1)
    for side, ref in ((0, mine_ref), (1, far_ref)):
        for position in range(1 << (bits - 1)):
            distance = side << (bits - 1) | position
            number = 0
            for i, mask in enumerate(masks):
                apart = distance >> (bits - 1 - i) & 1
                number = 2 * number + lax.rem(where_ref[0] // mask + apart, 2)
            here = pl.ds(pl.multiple_of(base + number * height, height), height)
            out_ref[here, :] = ref[position * height : (position + 1) * height, :]


TRANSPOSED_LEFT = (((0,), (0,)), ((), ()))
TRANSPOSED_RIGHT = (((1,), (1,)), ((), ()))


def extra_rows(value):
    first = lax.reduce_precision(value, 8, 7)
    second = lax.reduce_precision(value - first, 8, 7)
    third = value - first - second
    row = lax.broadcasted_iota(jnp.int32, (EXTRA, value.shape[1]), 0)
    rows = jnp.where(row == 0, first, jnp.where(row == 1, second, jnp.where(row == 2, third, 0.0)))
    return rows.astype(BF16)


def side_by_side(refs, rows):
    return jnp.concatenate([ref[:rows, :] for ref in refs], axis=1)


def gram_kernel(pair, mask, where_ref, *refs):
    mine_ref, other_ref, whole = refs[-3:]
    fields = refs[:CHUNKS]
    rows, width = fields[0].shape
    half = whole.shape[0] // 2
    middle = CHUNKS * width // 2
    side = lax.rem(where_ref[0] // mask, 2)

    def fill(left, rights, count):
        for c, right in enumerate(rights):
            value = lax.dot_general(left, right[:rows, :], TRANSPOSED_LEFT, preferred_element_type=F32)
            whole[:count, c * width : (c + 1) * width] = value.astype(BF16)

    if pair:
        peers = refs[CHUNKS : 2 * CHUNKS]
        used = middle

        @pl.when(where_ref[1] == 0)
        def _():
            fill(side_by_side(peers[: CHUNKS // 2], rows), fields, middle)

        @pl.when(where_ref[1] == 1)
        def _():
            fill(side_by_side(fields[CHUNKS // 2 :], rows), peers, middle)
    else:
        used = middle + middle // 2
        upper = side_by_side(fields[CHUNKS // 2 :], rows)
        fill(side_by_side(fields[: CHUNKS // 2], rows), fields, middle)
        corner = lax.dot_general(upper, upper, TRANSPOSED_LEFT, preferred_element_type=F32).astype(BF16)
        whole[middle:used, :middle] = corner[: middle // 2]
        whole[middle:used, middle:] = corner[middle // 2 :]
    if used < whole.shape[0]:
        whole[used:, :] = jnp.zeros((whole.shape[0] - used, whole.shape[1]), BF16)
    mine_ref[:half, :] = whole[pl.ds(pl.multiple_of(side * half, half), half), :]
    other_ref[:half, :] = whole[pl.ds(pl.multiple_of((1 - side) * half, half), half), :]
    if mine_ref.shape[0] > half:
        ends = [fields[-1], *refs[2 * CHUNKS - 1 : -3]]
        total = sum(jnp.sum(end[rows:, :].astype(F32), axis=0, keepdims=True) for end in ends)
        carried = extra_rows(jnp.concatenate([total] * CHUNKS, axis=1))
        mine_ref[half:, :] = carried
        other_ref[half:, :] = carried


def join_kernel(upper_ref, lower_ref, out_ref):
    height = upper_ref.shape[0]
    out_ref[:height, :] = upper_ref[...]
    out_ref[height:, :] = lower_ref[...]


def sum_kernel(masks, hop, extra, entries, rows_total, where_ref, *refs):
    terms, outs = refs[: hop + 1], refs[hop + 1 :]
    height = terms[0].shape[0] - extra
    begins, offset = [0, 0], 0
    final = hop == len(masks)
    for i, mask in enumerate(masks[1 : hop + 1], 1):
        height //= 2
        keep = lax.rem(where_ref[0] // mask, 2)
        first_row = offset + (1 - keep) * height
        offset = offset + keep * height
        begins.append(offset)
    if final:
        first_row = offset
    step = terms[-1].shape[0] - extra if final else height
    value = 0.0
    for term, begin in zip(terms, begins):
        here = pl.ds(pl.multiple_of(first_row - begin, EXTRA), step)
        value = value + term[here, :].astype(F32)
    total = None
    if extra:
        total = sum(jnp.sum(term[-extra:, :].astype(F32), axis=0, keepdims=True) for term in terms)
    if not final:
        outs[0][:step, :] = value.astype(BF16)
        if extra:
            outs[0][step:, :] = extra_rows(total)
        return
    if extra:
        level = total / entries
        outs[1][...] = jnp.broadcast_to(level[:, :1], outs[1].shape)
    else:
        level_ref, *outs = outs
        level = level_ref[:1, :1]
    outs[0][...] = (value / (level * rows_total)).astype(BF16)


def mix_kernel(pair, masks, first, last, where_ref, *refs):
    level_ref, *refs = refs if last else (None, *refs)
    total_ref, *refs = (None, *refs) if first else refs
    fields, refs = refs[:CHUNKS], refs[CHUNKS:]
    out_ref, block = refs[-2:]
    own = refs[-2 - CHUNKS : -2]
    rows, width = fields[0].shape
    middle = CHUNKS * width // 2

    def finish(mixed, here):
        value = mixed if first else total_ref[:, here] + mixed
        if last:
            filtered = side_by_side(own, rows)[:, here].astype(F32)
            value = (1.5 * filtered - 0.5 * value) / jnp.sqrt(level_ref[:1, :1])
        out_ref[:, here] = value.astype(out_ref.dtype)

    def times(left, right):
        return jnp.dot(left, right, preferred_element_type=F32)

    def times_transposed(left, right):
        return lax.dot_general(left, right, TRANSPOSED_RIGHT, preferred_element_type=F32)

    if not pair:
        put_in_place(where_ref, masks, refs[0], refs[1], block, 0)
        lower, upper = side_by_side(fields[: CHUNKS // 2], rows), side_by_side(fields[CHUNKS // 2 :], rows)
        corner = block[middle : middle + middle // 2, :]
        corner = jnp.concatenate([corner[:, :middle], corner[:, middle:]], axis=0)
        finish(
            times(lower, block[:middle, :middle]) + times_transposed(upper, block[:middle, middle:]),
            slice(0, middle),
        )
        finish(times(lower, block[:middle, middle:]) + times(upper, corner), slice(middle, 2 * middle))
        return
    height = block.shape[0] // 2
    is_upper = where_ref[1]
    put_in_place(where_ref, masks, refs[0], refs[1], block, is_upper * height)
    put_in_place(where_ref, masks, refs[2], refs[3], block, (1 - is_upper) * height)

    @pl.when(is_upper == 0)
    def _():
        field = side_by_side(fields, rows)
        for c in range(CHUNKS):
            here = slice(c * width, (c + 1) * width)
            finish(times(field, jnp.concatenate([block[:middle, here], block[height : height + middle, here]])), here)

    @pl.when(is_upper == 1)
    def _():
        field = side_by_side(fields, rows)
        for c in range(CHUNKS):
            row = c * width if c * width < middle else height + c * width - middle
            finish(times_transposed(field, block[row : row + width, :]), slice(c * width, (c + 1) * width))


def local(orbitals, hamiltonian, neighbours):
    elements, slots, size, _ = hamiltonian.shape
    rows, columns = orbitals.shape
    tiles = lax.axis_size("elem")
    groups = lax.axis_size("orb")
    lines = tiles // 2
    my_tile = lax.axis_index("elem")
    my_group = lax.axis_index("orb")
    odd = my_tile % 2
    line = my_tile // 2

    swap = [(i, i ^ 1) for i in range(tiles)]
    outward = [(2 * i + side, 2 * ((i + 1 - 2 * side) % lines) + side) for i in range(lines) for side in (0, 1)]

    def to_group(value, d):
        return lax.ppermute(value, "orb", [(i, i ^ d) for i in range(groups)])

    place = neighbours % elements
    last_two = place[:, 5:]
    place = jnp.concatenate([place[:, :5], jnp.where(odd == 0, last_two[:, ::-1], last_two)], axis=1)
    by_slot = [hamiltonian[:, s] for s in range(5)]
    by_slot.append(jnp.where(odd == 0, hamiltonian[:, 6], hamiltonian[:, 5]))
    by_slot.append(jnp.where(odd == 0, hamiltonian[:, 5], hamiltonian[:, 6]))
    by_slot.append(jnp.zeros_like(by_slot[0]))
    blocks = jnp.concatenate(by_slot, axis=2)

    width = columns // CHUNKS
    start = [lax.slice_in_dim(orbitals, c * width, (c + 1) * width, axis=1) for c in range(CHUNKS)]
    near = {(0, 0): lax.ppermute(start[0], "elem", swap)}
    order = Order(jnp.zeros((8, 128), F32))
    positions = [
        jnp.stack([my_tile, my_group >> max(d.bit_length() - 1, 0) & 1]).astype(jnp.int32) for d in range(groups)
    ]
    blocks, place, *positions = order(blocks, place, *positions)
    start = [start[0]] + [order(field) for field in start[1:]]
    for c in range(1, CHUNKS):
        near[(0, c)] = lax.ppermute(start[c], "elem", swap)

    jobs = [(stage, c) for stage in range(3) for c in range(CHUNKS)]
    far = {}
    firsts, squares, pieces = {}, jnp.zeros((8, width), F32), [{} for _ in range(CHUNKS)]
    current = {(0, c): start[c] for c in range(CHUNKS)}

    def send_on(job):
        near[job] = order(near[job])
        far[job] = lax.ppermute(near[job], "elem", outward)

    def more_panel(c):
        for d in range(1, groups):
            if d & (d - 1):
                low = d & -d
                if d ^ low in pieces[c] and d not in pieces[c]:
                    pieces[c][d ^ low] = order(pieces[c][d ^ low])
                    pieces[c][d] = to_group(pieces[c][d ^ low], low)

    def settle(c, some=lambda d: True):
        for d in [d for d in pieces[c] if d and some(d)]:
            pieces[c][d] = order(pieces[c][d])

    def multiply(job):
        nonlocal squares
        stage, c = job
        far[job] = order(far[job])
        old = ((), (start[c],), (firsts.get(c), squares))[stage]
        last = stage == 2 and c == CHUNKS - 1
        out = product(stage, place, blocks, current[job], near[job], far[job], *old, last=last)
        if stage == 0:
            firsts[c], out = order(*out)
        elif stage == 1:
            out = order(out)
        else:
            if last:
                out = order(out)
            else:
                out, squares = order(*out)
            pieces[c][0] = out
            bit = groups // 2
            while bit:
                pieces[c][bit] = to_group(out, bit)
                bit //= 2
            if c > 1:
                more_panel(c - 2)
                settle(c - 2, lambda d: not d & (d - 1))
            if last:
                more_panel(c - 1)
            return
        current[(stage + 1, c)] = out
        near[(stage + 1, c)] = lax.ppermute(out, "elem", swap)

    for index, job in enumerate(jobs):
        send_on(job)
        if index:
            multiply(jobs[index - 1])
    multiply(jobs[-1])

    rows_total = rows * tiles
    level = None
    middle = columns // 2
    unit = 16 * tiles
    clock = Schedule()
    z_masks = [2 << i for i in range(lines.bit_length() - 1)]
    there = {d: 3.0 if d == 1 else 10.5 for d in range(1, groups)}
    mixed, mixes = None, 0

    def where(d):
        return positions[d]

    def all_chunks(d):
        return [pieces[c][d] for c in range(CHUNKS)]

    def over_tiles(value, mask):
        sent = lax.ppermute(value, "elem", [(i, i ^ mask) for i in range(tiles)])
        if mask <= 2:
            return sent, clock.transfer(value, "y" if mask == 1 else "z")
        clock.spend(-1.3)
        return sent, max(clock.transfer(value, "z", mask / 4), clock.transfer(value, "middle", mask / 2))

    def over_groups(value, d):
        return to_group(value, d), clock.transfer(value, "core" if d == 1 else "x")

    def panel_process():
        yield 10.5
        for c in range(CHUNKS - 1):
            more_panel(c)
            settle(c, lambda d: not d & (d - 1))
        more_panel(CHUNKS - 1)
        settle(CHUNKS - 1, lambda d: not d & (d - 1))
        clock.spend(1.3)
        for d in range(1, groups):
            if d & (d - 1):
                there[d] = clock.now + 3.5

    def gram_chunk(d, mask, extra):
        height = middle if d else middle + middle // 2
        height += -height % unit
        fields = all_chunks(0)
        if d:
            fields += list(order(*all_chunks(d)))
        if extra:
            fields += [pieces[-1][other] for other in range(1, groups) if other != d]
        half = jax.ShapeDtypeStruct((height // 2 + extra, columns), BF16)
        scratch = (pltpu.VMEM((height, columns), BF16),)
        name = "gram_pair" if d else "gram_own"
        clock.spend(3.2 if d else 3.0)
        return call(
            functools.partial(gram_kernel, d > 0, mask), name, (half, half), (where(d),), fields, scratch
        )

    sent = [None]

    def process(d, masks, extra=0, round_y=False, behind=None):
        nonlocal mixed, mixes, level
        need = list(there) if extra else [d] if d else []
        while any(other not in pieces[-1] or there[other] > clock.now for other in need):
            yield clock.now + 0.5
        mine, value = order(*gram_chunk(d, masks[0], extra))
        terms = [mine]
        height = mine.shape[0] - extra

        def added(hop):
            clock.spend(0.8)
            final = hop == len(masks)
            count = height if final else height + extra
            outs = jax.ShapeDtypeStruct((count, columns), BF16)
            args = list(terms)
            if final and extra:
                outs = (outs, jax.ShapeDtypeStruct((8, 128), F32))
            elif final:
                args.append(level)
            kernel = functools.partial(
                sum_kernel, masks, hop, extra, columns * groups * rows_total, rows_total
            )
            return call(kernel, "sum_last" if final else "sum_hop", outs, (where(d),), args)

        for hop, mask in enumerate(masks):
            if hop:
                height //= 2
                value = order(added(hop))
            received, arrival = over_tiles(value, mask)
            yield arrival if hop or mask > 1 else arrival - (3.0 if d else 6.0)
            terms.append(order(received))
        while level is None and not extra:
            yield clock.now + 0.5
        part = added(len(masks))
        if extra:
            part, level = order(*part)
        else:
            part = order(part)
        for mask in masks[:0:-1]:
            received, arrival = over_tiles(part, mask)
            yield arrival
            joined = jax.ShapeDtypeStruct((2 * part.shape[0], columns), BF16)
            part = order(call(join_kernel, "join", joined, (), (part, order(received))))
            clock.spend(0.5)
        while behind not in sent:
            yield clock.now + 0.5
        part = order(part)
        far, arrival = over_tiles(part, masks[0])
        sent.append(d)
        if d:
            peer, peer_arrival = over_groups(part, d)
        if round_y:
            clock.now = max(clock.now, arrival)
            far = order(far)
            yield peer_arrival
            peer = order(peer)
            peer_far, peer_arrival = over_tiles(peer, masks[0])
        elif d:
            yield peer_arrival - 3.0
            peer = order(peer)
            yield arrival + (6.0 if d == 1 else 0.0)
            far = order(far)
        else:
            yield arrival
            while mixes < turn[d]:
                yield clock.now + 0.5
            far = order(far)
        parts = (part, far)
        if d:
            if not round_y:
                peer_far, peer_arrival = over_groups(far, d)
            yield peer_arrival
        while mixes < turn[d]:
            yield clock.now + 0.5
        if d:
            peer_far = order(peer_far)
            parts += (peer, peer_far)
        first, last = mixes == 0, mixes == groups - 1
        mixes += 1
        shape = jax.ShapeDtypeStruct((rows, columns), BF16 if last else F32)
        scratch = (pltpu.VMEM((len(parts) * part.shape[0], columns), BF16),)
        args = (() if first else (mixed,)) + (*all_chunks(d), *parts)
        if last:
            args = (level, *args, *all_chunks(0))
        kernel = functools.partial(mix_kernel, d > 0, masks, first, last)
        name = "mix_pair" if d else "mix_own"
        clock.spend(3.2)
        mixed = call(kernel, name, shape, (where(d),), args, scratch, {} if first or last else {1: 0}, 20, 5 * MIB)
        if not last:
            mixed = order(mixed)

    y_first, z_then_y, y_then_far = (1, *z_masks), (*z_masks[:1], 1, *z_masks[1:]), (1, *z_masks[::-1])
    there[1] = 25.0
    queue = sorted(range(1, groups), key=lambda d: (d == 1, d))
    turn = {d: place for place, d in enumerate([queue[-1], *queue[:-2], 0, *queue[-2:-1]])}
    carrier = queue[min(1, len(queue) - 1)]
    processes = [panel_process()]
    for d in queue:
        first = d == queue[0] and d != carrier
        behind = carrier if d == 1 and d != carrier else None
        processes.append(process(d, z_then_y if first else y_first, EXTRA if d == carrier else 0, first, behind))
    processes.append(process(0, y_then_far, behind=1))
    clock.run(processes)
    return mixed


def solution(mesh):
    return jax.shard_map(
        local,
        mesh=mesh,
        in_specs=(P("elem", "orb"), P("elem", None, None, None), P("elem", None)),
        out_specs=P("elem", "orb"),
        check_vma=False,
    )
```
